256 devices in a mesh: ctx: 32 (over z, y), ep: 8 (over x, core).
Axes of the slice: x: 4, y: 4, z: 8, core: 2. Of those that a mesh axis runs over, the one named last changes fastest.
Arguments:
- stream: bfloat16 [4096, 3072], P(('ctx', 'ep')), may hold values from -6 to 6
- query: bfloat16 [4096, 4096], P('ctx', 'ep'), may hold values from -2 to 2
- key: bfloat16 [4096, 4096], P('ctx', 'ep'), may hold values from -2 to 2
- value: bfloat16 [4096, 4096], P('ctx', 'ep'), may hold values from -6 to 6
- decay_rate: float32 [32], P('ep'), may hold values from 7.324219e-05 to 0.08
- out_weight: bfloat16 [4096, 3072], P('ep', 'ctx'), may hold values from -0.09375 to 0.09375
- norm_gain: float32 [3072], replicated, may hold values from 0.25 to 1.75
- router_weight: bfloat16 [3072, 16], replicated, may hold values from -0.109375 to 0.109375
- routes: int32 [4096, 2], P(('ctx', 'ep')), may hold values from 0 to 15, all different within a row; in each aligned block of 16 rows (0 to 15, 16 to 31, ...) at most 3 rows name the same one
- expert_gate: bfloat16 [3072, 73728], P(None, ('ep', 'ctx')), may hold values from -0.109375 to 0.109375
- expert_up: bfloat16 [3072, 73728], P(None, ('ep', 'ctx')), may hold values from -0.109375 to 0.109375
- expert_down: bfloat16 [73728, 3072], P(('ep', 'ctx')), may hold values from -0.09375 to 0.09375
Outputs:
- block_out: bfloat16 [4096, 3072], P(('ctx', 'ep'))
The draws below stay inside these ranges and needn't reach their ends.
Inputs may be any that keep to these rules, and one draw needn't show every extreme that they name: `routes`: in each aligned block of 16 tokens (the tokens of one device) no expert is named more than 3 times, a bound that some block reaches.
All inputs are finite; a program needn't handle non-finite values.
Results may differ from the reference program's by a relative error of at most 0.017.
Values may be sent and summed in bfloat16 or wider, within the bound.
A program may use at most 128 MiB of HBM per device.

```python
import math
import jax
import jax.numpy as jnp
import numpy as np
from jax import lax

DM = 3072
DH = 128
FFW = 4608
L_CTX = 128
HEADS = 32
EXPERTS = 16
SEQ = 4096
TOK_DEV = 16
CAP = 3
N_CTX = 32


def draw_decay_rate(key, part):
    key = jax.random.fold_in(key, 11)
    uniform_part = jax.random.uniform(key, (HEADS,), jnp.float32)
    lowest = 0.3 / SEQ
    highest = 0.08
    spread = jnp.log(highest) - jnp.log(lowest)
    return jnp.exp(jnp.log(lowest) + uniform_part * spread).astype(jnp.float32)


def shard_levels(key, shape, pieces, least, high):
    def one(position, blocks):
        heights = jax.random.uniform(jax.random.fold_in(jax.random.fold_in(key, 6), position), (blocks,), jnp.float32, least / len(pieces), high / len(pieces))
        return jnp.repeat(jnp.exp(heights), shape[position] // blocks).reshape((-1,) + (1,) * (len(shape) - position - 1))

    level = one(*pieces[0])
    for cut in pieces[1:]:
        level = level * one(*cut)
    return level


def shared_out(rng, own, number, rows, count, top, limit, lean):
    sequence = jax.random.permutation(rng, count)
    packed, usual = portions_of(count, rows * top, limit, lean, True), portions_of(count, rows * top, limit, lean, False)
    places = jnp.arange(count)

    def named(lengths, rotation):
        used = int((lengths > 0).sum())
        fixed = max(1, used // 4)
        shifted = fixed + (places - fixed + rotation * (used - fixed)) % max(1, count - fixed)
        return jnp.zeros((count,), jnp.int32).at[sequence[jnp.where(places < fixed, places, shifted)]].set(jnp.asarray(lengths, jnp.int32))

    lengths = jnp.where(number % 4 == 0, named(packed, number // 4), named(usual, number - number // 4 - 1))
    mixed = jax.random.permutation(jax.random.fold_in(own, 3), count)
    giver, receiver = mixed[0:count // 2 * 2:2], mixed[1:count // 2 * 2:2]
    room = jnp.minimum(lengths[giver] - 1, limit - lengths[receiver]) // 2
    room = jnp.where((giver == sequence[0]) | (receiver == sequence[0]) | (lengths[receiver] == 0), 0, jnp.maximum(room, 0))
    shifted = jax.random.randint(jax.random.fold_in(own, 4), (count // 2,), 0, 1 << 20) % (room + 1)
    lengths = lengths.at[giver].add(-shifted).at[receiver].add(shifted)
    labels = jnp.searchsorted(jnp.cumsum(lengths), jnp.arange(rows * top), side="right").astype(jnp.int32)
    table = labels.reshape(top, rows).T
    table = table[jax.random.permutation(jax.random.fold_in(own, 1), rows)]
    rotation = jax.random.randint(jax.random.fold_in(own, 2), (rows, 1), 0, top)
    return jnp.take_along_axis(table, (jnp.arange(top)[None, :] + rotation) % top, axis=1)


def portions_of(number_of, total, limit, skew, full):
    loads = [(1 << 20) // math.isqrt(standing ** skew) + 1 for standing in range(1, number_of + 1)]
    largest = limit if full else min(limit, max(-(-total // number_of), total * loads[0] // sum(loads)))
    least = 1 if total - largest >= number_of - 1 else 0
    counts, spare = [largest] + [least] * (number_of - 1), total - largest - least * (number_of - 1)
    while spare > 0:
        candidates = [i for i in range(1, number_of) if counts[i] < largest] or [i for i in range(1, number_of) if counts[i] < limit]
        whole, remaining = sum([loads[i] for i in candidates]), spare
        for i in candidates:
            more = min(limit - counts[i], max(1, remaining * loads[i] // whole), spare)
            counts[i] = counts[i] + more
            spare = spare - more
    return np.array(counts)


def centred(rng, dims, deviation, limit, cuts=(), held_as=jnp.bfloat16):
    drawn = jax.random.normal(rng, dims, jnp.float32) * deviation
    if len(cuts) > 0:
        drawn = shard_levels(rng, dims, cuts, -0.22, 0.18) * drawn
    return jnp.clip(drawn, min=-limit, max=limit).astype(held_as)


def setup_inputs(seed: int = 0) -> dict:
    arg_keys = jax.random.split(jax.random.key(seed), 13)
    stream = centred(arg_keys[0], (SEQ, DM), 1.0, 6.0, ((0, 256),))
    query = centred(arg_keys[1], (SEQ, HEADS * DH), 0.3, 2.0, ((0, 32), (1, 8)))
    key = centred(arg_keys[2], (SEQ, HEADS * DH), 0.3, 2.0, ((0, 32), (1, 8)))
    value = centred(arg_keys[3], (SEQ, HEADS * DH), 1.0, 6.0, ((0, 32), (1, 8)))
    decay_rate = draw_decay_rate(jax.random.fold_in(arg_keys[12], 71), 0)
    out_weight = centred(arg_keys[5], (HEADS * DH, DM), (HEADS * DH) ** -0.5, 0.09375, ((0, 8), (1, 32)))
    norm_gain = jnp.clip(1.0 + 0.15 * jax.random.normal(arg_keys[6], (DM,), jnp.float32), 0.25, 1.75)
    router_weight = centred(arg_keys[7], (DM, EXPERTS), DM ** -0.5, 0.109375)
    routes_keys = jax.random.split(jax.random.fold_in(arg_keys[8], 1), SEQ // TOK_DEV)
    routes_turns = jax.random.permutation(jax.random.fold_in(arg_keys[8], 3), SEQ // TOK_DEV)
    routes = jax.vmap(lambda own, number: shared_out(jax.random.fold_in(arg_keys[8], 2), own, number, TOK_DEV, EXPERTS, 2, CAP, 2))(routes_keys, routes_turns).reshape((SEQ, 2))
    expert_gate = centred(arg_keys[9], (DM, EXPERTS * FFW), DM ** -0.5, 0.109375, ((1, 256),))
    expert_up = centred(arg_keys[10], (DM, EXPERTS * FFW), DM ** -0.5, 0.109375, ((1, 256),))
    expert_down = centred(arg_keys[11], (EXPERTS * FFW, DM), FFW ** -0.5, 0.09375, ((0, 256),))
    return dict(stream=stream, query=query, key=key, value=value, decay_rate=decay_rate, out_weight=out_weight, norm_gain=norm_gain, router_weight=router_weight, routes=routes, expert_gate=expert_gate, expert_up=expert_up, expert_down=expert_down)


PRECISE = lax.Precision.HIGHEST
EPSILON = 1e-06

def shard_attention(carry_state, block_data, rate_vec):
    query, key, value = block_data
    length = query.shape[0]
    head_count = rate_vec.shape[0]
    query_wide = query.astype(jnp.float32).reshape(length, head_count, -1)
    key_wide = key.astype(jnp.float32).reshape(length, head_count, -1)
    value_wide = value.astype(jnp.float32).reshape(length, head_count, -1)
    positions = jnp.arange(length, dtype=jnp.float32)
    distance = positions[:, None] - positions[None, :]
    causal = distance >= 0
    decay_mask = jnp.where(causal[None], jnp.exp(-rate_vec[:, None, None] * jnp.where(causal, distance, 0.0)[None]), 0.0)
    scores = jnp.einsum('ihd,jhd->hij', query_wide, key_wide, precision=PRECISE)
    weights = lax.optimization_barrier((scores * decay_mask).astype(jnp.bfloat16)).astype(jnp.float32)
    intra_part = jnp.einsum('hij,jhd->ihd', weights, value_wide, precision=PRECISE)
    query_fade = jnp.exp(-rate_vec[None, :] * (positions[:, None] + 1.0))
    inter_part = jnp.einsum('ihd,hde->ihe', query_wide * query_fade[:, :, None], carry_state, precision=PRECISE)
    mixed = intra_part + inter_part
    normed = mixed * lax.rsqrt(lax.optimization_barrier(jnp.mean(mixed * mixed, axis=-1, keepdims=True)) + EPSILON)
    key_fade = jnp.exp(-rate_vec[None, :] * (length - 1.0 - positions[:, None]))
    local_state = jnp.einsum('jhd,jhe->hde', key_wide * key_fade[:, :, None], value_wide, precision=PRECISE)
    carried = jnp.exp(-rate_vec * length)[:, None, None] * carry_state + local_state
    return (carried, normed.reshape(length, -1).astype(jnp.bfloat16))

def reference(stream, query, key, value, decay_rate, out_weight, norm_gain, router_weight, routes, expert_gate, expert_up, expert_down):
    shards = (query.reshape(N_CTX, L_CTX, -1), key.reshape(N_CTX, L_CTX, -1), value.reshape(N_CTX, L_CTX, -1))
    initial = jnp.zeros((HEADS, DH, DH), jnp.float32)

    def scan_step(carry_state, block_data):
        return shard_attention(carry_state, block_data, decay_rate)
    final_state, heads_out = lax.scan(scan_step, initial, shards)
    heads_out = heads_out.reshape(SEQ, HEADS * DH)
    hidden = stream.astype(jnp.float32) + jnp.dot(heads_out, out_weight, preferred_element_type=jnp.float32)
    token_rows = (hidden * lax.rsqrt(lax.optimization_barrier(jnp.mean(hidden * hidden, axis=-1, keepdims=True)) + EPSILON) * norm_gain).astype(jnp.bfloat16)
    logits = jnp.dot(token_rows, router_weight, preferred_element_type=jnp.float32)
    chosen = jnp.take_along_axis(logits, routes, axis=1)
    lifted = jax.nn.sigmoid(chosen)
    gate_share = lifted / lax.optimization_barrier(jnp.sum(lifted, axis=1, keepdims=True))
    blocks = SEQ // TOK_DEV
    route_flat = routes.reshape(blocks, 2 * TOK_DEV)
    onehot = (route_flat[:, :, None] == jnp.arange(EXPERTS, dtype=jnp.int32)[None, None, :]).astype(jnp.int32)
    before = jnp.cumsum(onehot, axis=1) - onehot
    route_rank = lax.optimization_barrier(jnp.sum(before * onehot, axis=2)).astype(jnp.int32)
    column = (jnp.arange(blocks, dtype=jnp.int32)[:, None] * CAP + route_rank).astype(jnp.int32)
    token_ids = jnp.repeat(jnp.arange(SEQ, dtype=jnp.int32).reshape(blocks, TOK_DEV), 2, axis=1)
    slot_table = jnp.full((EXPERTS, blocks * CAP), SEQ, jnp.int32).at[route_flat, column].set(token_ids)
    padded = jnp.concatenate([token_rows, jnp.zeros((1, DM), token_rows.dtype)], axis=0)

    def expert(expert_id):
        picked = padded[slot_table[expert_id]]
        start_col = (expert_id * FFW).astype(jnp.int32)
        gate_part = jnp.dot(picked, lax.dynamic_slice_in_dim(expert_gate, start_col, FFW, 1), preferred_element_type=jnp.float32)
        up_part = jnp.dot(picked, lax.dynamic_slice_in_dim(expert_up, start_col, FFW, 1), preferred_element_type=jnp.float32)
        inner_act = (jax.nn.silu(gate_part) * up_part).astype(jnp.bfloat16)
        down_rows = lax.dynamic_slice_in_dim(expert_down, start_col, FFW, 0)
        return jnp.dot(inner_act, down_rows, preferred_element_type=jnp.float32).astype(jnp.bfloat16)
    outputs = lax.map(expert, jnp.arange(EXPERTS, dtype=jnp.int32))
    fetched = outputs[route_flat, column].reshape(SEQ, 2, DM).astype(jnp.float32)
    expert_mix = lax.optimization_barrier(jnp.sum(gate_share[:, :, None] * fetched, axis=1))
    return (hidden + expert_mix).astype(jnp.bfloat16)
```

```python
import jax
import jax.numpy as jnp
from jax import lax
from jax.experimental import pallas as pl
from jax.experimental.pallas import tpu as pltpu
from jax.sharding import PartitionSpec as P

EPSILON = 1e-06
MESH = pl.DeviceIdType.MESH
F32 = jnp.float32
BF16 = jnp.bfloat16
NY = 4
NZ = 8
NX = 4
DM = 3072
HALF = 1536
SLOTS = 24
CHUNK = 48
SHARD = 96


def place():
    ctx = lax.axis_index("ctx")
    ep = lax.axis_index("ep")
    return ctx // NY, ctx % NY, ep // 2, ep % 2


def at(z, y, x, c):
    return (z * NY + y, x * 2 + c)


def remote(src, dst, send, recv, device):
    return pltpu.make_async_remote_copy(
        src_ref=src,
        dst_ref=dst,
        send_sem=send,
        recv_sem=recv,
        device_id=device,
        device_id_type=MESH,
    )


def await_copy(dst, send, recv, device):
    remote(dst, dst, send, recv, device).wait_recv()


def greet(barrier, devices):
    for device in devices:
        pl.semaphore_signal(barrier, inc=1, device_id=device, device_id_type=MESH)


def nt_dot(a, b):
    return lax.dot_general(a, b, (((1,), (1,)), ((), ())), preferred_element_type=F32)


def tn_dot(a, b):
    return lax.dot_general(a, b, (((0,), (0,)), ((), ())), preferred_element_type=F32)


def dot(a, b):
    return jnp.dot(a, b, preferred_element_type=F32)


def attention_kernel(
    stream_ref,
    query_ref,
    key_ref,
    value_ref,
    rate_ref,
    weight_ref,
    gain_ref,
    routes_ref,
    hidden_ref,
    rows_ref,
    table_ref,
    intra,
    local_out,
    local_in,
    total_out,
    total_in,
    entry,
    state_out,
    state_in,
    proj,
    heads,
    pair_out,
    pair_in,
    part,
    part_out,
    part_in,
    tokens,
    tables,
    s1,
    r1,
    s2,
    r2,
    s3,
    r3,
    wzs,
    wzr,
    wys,
    wyr,
    pair_sem,
    xs,
    xr,
    ts,
    tr,
    cs,
    cr,
):
    z, y, x, c = place()
    up, down = lax.rem(y + 1, NY), lax.rem(y + NY - 1, NY)
    right, left = lax.rem(z + 1, NZ), lax.rem(z + NZ - 1, NZ)
    y_up, y_down = at(z, up, x, c), at(z, down, x, c)
    z_right, z_left = at(right, y, x, c), at(left, y, x, c)
    partner = at(z, y, x, 1 - c)
    barrier = pltpu.get_barrier_semaphore()
    greet(barrier, [at(z, lax.rem(y + d, NY), x, c) for d in range(1, NY)])
    greet(barrier, [at(lax.rem(z + d, NZ), y, x, c) for d in range(1, NZ)])
    greet(barrier, [at(z, y, lax.rem(x + d, NX), c) for d in range(1, NX)])
    greet(barrier, [partner])

    rates = rate_ref[...]
    length = query_ref.shape[0]
    row = lax.broadcasted_iota(jnp.int32, (length, length), 0)
    col = lax.broadcasted_iota(jnp.int32, (length, length), 1)
    gap = (row - col).astype(F32)
    position = lax.broadcasted_iota(jnp.int32, (length, 1), 0).astype(F32)

    def head(ref, h):
        return ref[:, 128 * h : 128 * (h + 1)]

    for h in range(4):
        rate = rates[:, h : h + 1]
        fade = jnp.exp(-rate * (length - 1.0 - position))
        faded = (head(key_ref, h).astype(F32) * fade).astype(BF16)
        local_out[h] = tn_dot(faded, head(value_ref, h)).astype(BF16)
    proj[z * NY + y] = weight_ref[...]
    pl.semaphore_wait(barrier, NY - 1 + NZ - 1 + NX - 1 + 1)

    sends = []

    def launch(copy):
        copy.start()
        sends.append(copy)

    for d in range(1, NY):
        other = lax.rem(y + d, NY)
        launch(remote(local_out.at[other], local_in.at[y], s1.at[d], r1.at[d], at(z, other, x, c)))
    local_in[y] = local_out[y]

    def slot(zz, yy):
        return proj.at[lax.rem(zz + 2 * NZ, NZ) * NY + lax.rem(yy + 2 * NY, NY)]

    def half_slot(zz, yy, half):
        return slot(zz, yy).at[pl.ds(half * 48, 48)]

    def z_step(k):
        if k < 4:
            launch(remote(slot(z - k + 1, y), slot(z - k + 1, y), wzs.at[0, k], wzr.at[0, k], z_right))
            launch(remote(slot(z + k - 1, y), slot(z + k - 1, y), wzs.at[1, k], wzr.at[1, k], z_left))
        else:
            a, b = half_slot(z - 3, y, 0), half_slot(z + 3, y, 1)
            launch(remote(a, a, wzs.at[0, k], wzr.at[0, k], z_right))
            launch(remote(b, b, wzs.at[1, k], wzr.at[1, k], z_left))

    def z_wait(k):
        if k < 4:
            await_copy(slot(z - k, y), wzs.at[0, k], wzr.at[0, k], z_right)
            await_copy(slot(z + k, y), wzs.at[1, k], wzr.at[1, k], z_left)
        else:
            await_copy(half_slot(z + 4, y, 0), wzs.at[0, k], wzr.at[0, k], z_right)
            await_copy(half_slot(z + 4, y, 1), wzs.at[1, k], wzr.at[1, k], z_left)

    def y_send(g):
        s = slot(z + g, y)
        launch(remote(s, s, wys.at[g, 0, 0], wyr.at[g, 0, 0], y_up))
        launch(remote(s, s, wys.at[g, 1, 0], wyr.at[g, 1, 0], y_down))

    def y_relay(g):
        await_copy(slot(z + g, y - 1), wys.at[g, 0, 0], wyr.at[g, 0, 0], y_up)
        a = half_slot(z + g, y - 1, 0)
        launch(remote(a, a, wys.at[g, 0, 1], wyr.at[g, 0, 1], y_up))
        await_copy(slot(z + g, y + 1), wys.at[g, 1, 0], wyr.at[g, 1, 0], y_down)
        b = half_slot(z + g, y + 1, 1)
        launch(remote(b, b, wys.at[g, 1, 1], wyr.at[g, 1, 1], y_down))

    def y_finish(g):
        await_copy(half_slot(z + g, y + 2, 0), wys.at[g, 0, 1], wyr.at[g, 0, 1], y_up)
        await_copy(half_slot(z + g, y + 2, 1), wys.at[g, 1, 1], wyr.at[g, 1, 1], y_down)

    z_step(1)
    y_send(0)

    for h in range(4):
        rate = rates[:, h : h + 1]
        decay = jnp.where(gap >= 0, jnp.exp(-rate * jnp.maximum(gap, 0.0)), 0.0)
        scores = nt_dot(head(query_ref, h), head(key_ref, h))
        intra[h] = dot((scores * decay).astype(BF16), head(value_ref, h))

    for d in range(1, NY):
        other = lax.rem(y + d, NY)
        await_copy(local_in.at[lax.rem(y + NY - d, NY)], s1.at[d], r1.at[d], at(z, other, x, c))
    lane = lax.broadcasted_iota(jnp.int32, rates.shape, 1)
    own_rate = jnp.sum(jnp.where(lane == y, rates, 0.0), axis=1, keepdims=True)

    def power(n):
        return jnp.exp(-own_rate * (128.0 * n))

    locals_in = [local_in[i].astype(F32) for i in range(NY)]
    total = locals_in[3]
    for i in range(3):
        total = total + power(3 - i) * locals_in[i]
    total_out[...] = total.astype(BF16)
    for d in range(1, NZ):

        @pl.when(z + d < NZ)
        def _(d=d):
            remote(
                total_out, total_in.at[z], s2.at[d], r2.at[d], at(lax.rem(z + d, NZ), y, x, c)
            ).start()

    z_wait(1)
    z_step(2)
    y_send(1)
    y_send(7)
    y_relay(0)

    entry[...] = jnp.zeros_like(entry)
    for d in range(1, NZ):

        @pl.when(z >= d)
        def _(d=d):
            source = lax.rem(z + NZ - d, NZ)
            await_copy(total_in.at[source], s2.at[d], r2.at[d], at(source, y, x, c))
            entry[...] += power(4 * (d - 1)) * total_in[source].astype(F32)

    incoming = entry[...]
    for i in range(NY):
        state_out[i] = incoming.astype(BF16)
        incoming = power(1) * incoming + locals_in[i]
    for d in range(1, NY):
        other = lax.rem(y + d, NY)
        launch(remote(state_out.at[other], state_in.at[y], s3.at[d], r3.at[d], at(z, other, x, c)))
    state_in[y] = state_out[y]

    z_wait(2)
    z_step(3)
    y_send(2)
    y_send(6)
    y_relay(1)
    y_relay(7)

    for d in range(1, NY):
        other = lax.rem(y + d, NY)
        await_copy(state_in.at[lax.rem(y + NY - d, NY)], s3.at[d], r3.at[d], at(z, other, x, c))
    for h in range(4):
        rate = rates[:, h : h + 1]
        fade = jnp.exp(-rate * (position + 1.0))
        mixed = intra[h] + fade * dot(head(query_ref, h), state_in[h])
        mean = jnp.mean(mixed * mixed, axis=-1, keepdims=True)
        out = (mixed * lax.rsqrt(mean + EPSILON)).astype(BF16)
        for e in range(8):
            heads[e // 2, e % 2, :, 128 * h : 128 * (h + 1)] = out[16 * e : 16 * (e + 1)]

    z_wait(3)
    z_step(4)
    y_send(3)
    y_send(5)
    y_relay(2)
    y_relay(6)
    z_wait(4)
    y_send(4)
    y_relay(3)
    y_relay(5)
    y_relay(4)
    for g in range(NZ):
        y_finish(g)

    def project(core, store):
        lhs = heads[:, core].reshape(64, 512)
        for n in range(4):
            rhs = proj[8 * n : 8 * (n + 1)].reshape(8 * SHARD, 512)
            store(n, nt_dot(lhs, rhs))

    def store_pair(n, value):
        pair_out[:, :, 768 * n : 768 * (n + 1)] = value.astype(BF16).reshape(4, 16, 768)

    project(1 - c, store_pair)
    pair_copy = remote(pair_out, pair_in, pair_sem.at[0], pair_sem.at[1], partner)
    launch(pair_copy)

    def store_part(n, value):
        part[:, :, 768 * n : 768 * (n + 1)] = value.reshape(4, 16, 768)

    project(c, store_part)
    pair_copy.wait_recv()
    part[...] += pair_in[...].astype(F32)
    part_out[...] = part[...].astype(BF16)
    for d in (2, 1, 3):
        other = lax.rem(x + d, NX)
        launch(remote(part_out.at[other], part_in.at[x], xs.at[d], xr.at[d], at(z, y, other, c)))
    hidden = stream_ref[...].astype(F32) + part[x]
    for d in (1, 3, 2):
        source = lax.rem(x + NX - d, NX)
        await_copy(part_in.at[source], xs.at[d], xr.at[d], at(z, y, source, c))
        hidden = hidden + part_in[source].astype(F32)
    hidden_ref[...] = hidden
    mean = jnp.mean(hidden * hidden, axis=-1, keepdims=True)
    tokens[x, c] = (hidden * lax.rsqrt(mean + EPSILON) * gain_ref[...]).astype(BF16)
    tables[x, c] = routes_ref[...]
    for d in (2, 1, 3):
        other = lax.rem(x + d, NX)
        device = at(z, y, other, c)
        launch(remote(tokens.at[x, c], tokens.at[x, c], ts.at[0, d], tr.at[0, d], device))
        launch(remote(tables.at[x, c], tables.at[x, c], ts.at[1, d], tr.at[1, d], device))
    for d in (0, 1, 3, 2):
        source = lax.rem(x + NX - d, NX)
        if d:
            device = at(z, y, source, c)
            await_copy(tokens.at[source, c], ts.at[0, d], tr.at[0, d], device)
            await_copy(tables.at[source, c], ts.at[1, d], tr.at[1, d], device)
        launch(remote(tokens.at[source, c], tokens.at[source, c], cs.at[0, d], cr.at[0, d], partner))
        launch(remote(tables.at[source, c], tables.at[source, c], cs.at[1, d], cr.at[1, d], partner))
    for d in (0, 1, 3, 2):
        source = lax.rem(x + NX - d, NX)
        await_copy(tokens.at[source, 1 - c], cs.at[0, d], cr.at[0, d], partner)
        await_copy(tables.at[source, 1 - c], cs.at[1, d], cr.at[1, d], partner)
    rows_ref[...] = tokens[...].reshape(128, DM)
    table_ref[...] = tables[...].reshape(128, 128)
    for d in range(1, NZ):

        @pl.when(z + d < NZ)
        def _(d=d):
            remote(
                total_out, total_in.at[z], s2.at[d], r2.at[d], at(lax.rem(z + d, NZ), y, x, c)
            ).wait_send()

    for copy in sends:
        copy.wait_send()


def expert_kernel(
    hidden_ref,
    rows_ref,
    table_ref,
    router_ref,
    gate_hbm,
    up_hbm,
    down_hbm,
    out_ref,
    gate,
    up,
    down,
    picked,
    cross_out,
    flat,
    part,
    first_up,
    first_down,
    second_up,
    second_down,
    total,
    line_out,
    line_in,
    back_out,
    back_in,
    mixed,
    pair_out,
    pair_in,
    home_out,
    home_in,
    wsem,
    dxs,
    dxr,
    dzs,
    dzr,
    dys,
    dyr,
    eys,
    eyr,
    ezs,
    ezr,
    bs,
    br,
    ps,
    pr,
    xs,
    xr,
):
    z, y, x, c = place()
    half, zl = z // 4, z % 4
    up_y, down_y = lax.rem(y + 1, NY), lax.rem(y + NY - 1, NY)
    far_y = lax.rem(y + 2, NY)
    y_up, y_down = at(z, up_y, x, c), at(z, down_y, x, c)
    z_right = at(lax.rem(z + 1, NZ), y, x, c)
    z_left = at(lax.rem(z + NZ - 1, NZ), y, x, c)
    mirror = at(NZ - 1 - z, y, x, c)
    partner = at(z, y, x, 1 - c)
    barrier = pltpu.get_barrier_semaphore()
    greet(barrier, [y_up, y_down, partner])
    greet(barrier, [at(lax.rem(z + d, NZ), y, x, c) for d in range(1, NZ)])
    greet(barrier, [at(z, y, lax.rem(x + d, NX), c) for d in range(1, NX)])
    loads = [
        pltpu.make_async_copy(gate_hbm, gate, wsem.at[0]),
        pltpu.make_async_copy(up_hbm, up, wsem.at[1]),
        pltpu.make_async_copy(down_hbm, down, wsem.at[2]),
    ]
    for load in loads:
        load.start()
    sends = []

    def launch(copy):
        copy.start()
        sends.append(copy)

    first = table_ref[:, 0:1]
    second = table_ref[:, 1:2]
    group = x * 2 + c
    lane = lax.broadcasted_iota(jnp.int32, (128, 128), 1)
    earlier = (lane < lax.broadcasted_iota(jnp.int32, (128, 128), 0)).astype(BF16)

    def select(which):
        expert = group * 2 + which
        hit = jnp.logical_or(first == expert, second == expert)
        wide = jnp.broadcast_to(jnp.where(hit, 1.0, 0.0), (128, 128))
        rank = dot(earlier, wide.astype(BF16)).astype(jnp.int32)
        low = jnp.where(rank == lane, wide, 0.0)[:, :CHUNK]
        high = jnp.where(rank == lane - SLOTS, wide, 0.0)[:, :CHUNK]
        keep = lax.broadcasted_iota(jnp.int32, (128, CHUNK), 1) < SLOTS
        return jnp.where(keep, low, 0.0).astype(BF16), jnp.where(keep, 0.0, high).astype(BF16)

    def pick(which):
        low, high = select(which)
        return (tn_dot(low, rows_ref[:, :HALF]) + tn_dot(high, rows_ref[:, HALF:])).astype(BF16)

    cross_out[...] = pick(1 - half)
    picked[z * NY + y] = pick(half)
    pl.semaphore_wait(barrier, 3 + NZ - 1 + NX - 1)
    here = picked.at[z * NY + y]
    launch(remote(cross_out, here, dxs, dxr, mirror))

    order = [zl, zl + 1 - 2 * (zl % 2), 2 - zl // 2, 3 - 3 * (zl // 2)]

    def z_index(p, e):
        own = half * 4 + p
        return own if e == 0 else NZ - 1 - own

    def slot(zz, yy):
        return picked.at[zz * NY + yy]

    def lanes(ref, which):
        return ref.at[:, pl.ds(which * 768, 768)]

    def forward(p, e):
        s = slot(z_index(p, e), y)
        return (
            remote(s, s, dzs.at[0, p, e], dzr.at[p, e], z_right),
            remote(s, s, dzs.at[1, p, e], dzr.at[p, e], z_left),
        )

    def spread(i, e):
        p = order[i]
        zz = z_index(p, e)
        s = slot(zz, y)
        if i > 0:
            await_copy(s, dzs.at[0, p, e], dzr.at[p, e], z_right)
        elif e == 1:
            await_copy(s, dxs, dxr, mirror)

        @pl.when(jnp.logical_and(p <= zl, zl < 3))
        def _():
            forward(p, e)[0].start()

        @pl.when(jnp.logical_and(p >= zl, zl > 0))
        def _():
            forward(p, e)[1].start()

        launch(remote(s, s, dys.at[zz, 0, 0], dyr.at[zz, 0, 0], y_up))
        launch(remote(s, s, dys.at[zz, 1, 0], dyr.at[zz, 1, 0], y_down))

    def relay(i, e):
        zz = z_index(order[i], e)
        await_copy(slot(zz, down_y), dys.at[zz, 0, 0], dyr.at[zz, 0, 0], y_up)
        a = lanes(slot(zz, down_y), 0)
        launch(remote(a, a, dys.at[zz, 0, 1], dyr.at[zz, 0, 1], y_up))
        await_copy(slot(zz, up_y), dys.at[zz, 1, 0], dyr.at[zz, 1, 0], y_down)
        b = lanes(slot(zz, up_y), 1)
        launch(remote(b, b, dys.at[zz, 1, 1], dyr.at[zz, 1, 1], y_down))

    def finish(i, e):
        zz = z_index(order[i], e)
        await_copy(lanes(slot(zz, far_y), 0), dys.at[zz, 0, 1], dyr.at[zz, 0, 1], y_up)
        await_copy(lanes(slot(zz, far_y), 1), dys.at[zz, 1, 1], dyr.at[zz, 1, 1], y_down)

    sequence = [(0, 0), (1, 0), (0, 1), (2, 0), (1, 1), (3, 0), (2, 1), (3, 1)]
    for n, (i, e) in enumerate(sequence):
        spread(i, e)
        if n >= 1:
            relay(*sequence[n - 1])
    relay(*sequence[-1])
    for i, e in sequence:
        finish(i, e)

    def flatten(n, carry):
        a = picked[2 * n].astype(F32)
        b = picked[2 * n + 1].astype(F32)
        rows = pl.ds(pl.multiple_of(n * CHUNK, CHUNK), CHUNK)
        flat[rows, :HALF] = jnp.concatenate([a[:SLOTS], b[:SLOTS]], axis=0).astype(BF16)
        flat[rows, HALF:] = jnp.concatenate([a[SLOTS:], b[SLOTS:]], axis=0).astype(BF16)
        return carry

    lax.fori_loop(0, 16, flatten, 0)
    for load in loads:
        load.wait()

    def compute(m, carry):
        rows = flat[pl.ds(pl.multiple_of(m * 192, 192), 192), :]
        gated = dot(rows, gate[...])
        inner = (gated * jax.nn.sigmoid(gated) * dot(rows, up[...])).astype(BF16)
        for side in range(2):
            result = dot(inner, down[:, HALF * side : HALF * (side + 1)])
            if side == 0:
                kept = result
            else:
                for i in range(8):
                    block = slice(SLOTS * i, SLOTS * (i + 1))
                    part[m * 8 + i] = jnp.concatenate([kept[block], result[block]], axis=0).astype(BF16)
        return carry

    lax.fori_loop(0, 4, compute, 0)

    def mine(zz, yy):
        return part.at[zz * NY + yy]

    groups = [(i, e) for i in (3, 2, 1, 0) for e in (0, 1)]
    for i, e in groups:
        zz = z_index(order[i], e)
        launch(remote(lanes(mine(zz, far_y), 0), first_up.at[zz], eys.at[zz, 0, 0], eyr.at[zz, 0, 0], y_up))
        launch(remote(lanes(mine(zz, far_y), 1), first_down.at[zz], eys.at[zz, 1, 0], eyr.at[zz, 1, 0], y_down))

    def pass_on(i, e):
        zz = z_index(order[i], e)
        await_copy(first_up.at[zz], eys.at[zz, 0, 0], eyr.at[zz, 0, 0], y_up)
        a = zz * NY + up_y
        part[a, :, :768] = (part[a, :, :768].astype(F32) + first_up[zz].astype(F32)).astype(BF16)
        launch(remote(part.at[a], second_up.at[zz], eys.at[zz, 0, 1], eyr.at[zz, 0, 1], y_up))
        await_copy(first_down.at[zz], eys.at[zz, 1, 0], eyr.at[zz, 1, 0], y_down)
        b = zz * NY + down_y
        part[b, :, 768:] = (part[b, :, 768:].astype(F32) + first_down[zz].astype(F32)).astype(BF16)
        launch(remote(part.at[b], second_down.at[zz], eys.at[zz, 1, 1], eyr.at[zz, 1, 1], y_down))

    def collect(i, e):
        zz = z_index(order[i], e)
        await_copy(second_up.at[zz], eys.at[zz, 0, 1], eyr.at[zz, 0, 1], y_up)
        await_copy(second_down.at[zz], eys.at[zz, 1, 1], eyr.at[zz, 1, 1], y_down)
        total[zz] = (
            part[zz * NY + y].astype(F32)
            + second_up[zz].astype(F32)
            + second_down[zz].astype(F32)
        )

    def line_copy(p, e, side):
        return remote(
            line_out.at[p, e],
            line_in.at[side, p, e],
            ezs.at[p, e],
            ezr.at[side, p, e],
            z_right if side == 0 else z_left,
        )

    def along(i, e):
        p = order[i]
        zz = z_index(p, e)

        @pl.when(jnp.logical_and(p > zl, zl > 0))
        def _():
            await_copy(line_in.at[0, p, e], ezs.at[p, e], ezr.at[0, p, e], z_left)
            total[zz] += line_in[0, p, e].astype(F32)

        @pl.when(jnp.logical_and(p < zl, zl < 3))
        def _():
            await_copy(line_in.at[1, p, e], ezs.at[p, e], ezr.at[1, p, e], z_right)
            total[zz] += line_in[1, p, e].astype(F32)

        line_out[p, e] = total[zz].astype(BF16)

        @pl.when(p > zl)
        def _():
            line_copy(p, e, 0).start()

        @pl.when(p < zl)
        def _():
            line_copy(p, e, 1).start()

    def arrive(e):
        zz = z_index(zl, e)

        @pl.when(zl > 0)
        def _():
            await_copy(line_in.at[0, zl, e], ezs.at[zl, e], ezr.at[0, zl, e], z_left)
            total[zz] += line_in[0, zl, e].astype(F32)

        @pl.when(zl < 3)
        def _():
            await_copy(line_in.at[1, zl, e], ezs.at[zl, e], ezr.at[1, zl, e], z_right)
            total[zz] += line_in[1, zl, e].astype(F32)

    for n in range(10):
        if n < 8:
            pass_on(*groups[n])
        if n >= 2:
            collect(*groups[n - 2])
            if groups[n - 2][0] > 0:
                along(*groups[n - 2])
    arrive(1)
    back_out[1] = total[z_index(zl, 1)].astype(BF16)
    launch(remote(back_out.at[1], back_in, bs, br, mirror))
    arrive(0)
    back_out[0] = total[z_index(zl, 0)].astype(BF16)

    logits = dot(rows_ref[...], router_ref[...])
    expert = lax.broadcasted_iota(jnp.int32, logits.shape, 1)
    lift_first = jax.nn.sigmoid(jnp.sum(jnp.where(expert == first, logits, 0.0), axis=1, keepdims=True))
    lift_second = jax.nn.sigmoid(jnp.sum(jnp.where(expert == second, logits, 0.0), axis=1, keepdims=True))
    both = lift_first + lift_second
    share_first, share_second = lift_first / both, lift_second / both

    def contribution(which, returned):
        chosen = group * 2 + which
        share = jnp.where(first == chosen, share_first, 0.0) + jnp.where(
            second == chosen, share_second, 0.0
        )
        low, high = select(which)
        return share * dot(low, returned), share * dot(high, returned)

    low, high = contribution(half, back_out[0])
    await_copy(back_in, bs, br, mirror)
    far_low, far_high = contribution(1 - half, back_in[...])
    mixed[:, :, :, :HALF] = (low + far_low).reshape(4, 2, 16, HALF)
    mixed[:, :, :, HALF:] = (high + far_high).reshape(4, 2, 16, HALF)
    pair_out[...] = mixed[:, 1 - c].astype(BF16)
    pair_copy = remote(pair_out, pair_in, ps, pr, partner)
    launch(pair_copy)
    pair_copy.wait_recv()
    summed = mixed[:, c] + pair_in[...].astype(F32)
    mixed[:, c] = summed
    home_out[...] = summed.astype(BF16)
    for d in (2, 1, 3):
        other = lax.rem(x + d, NX)
        launch(remote(home_out.at[other], home_in.at[x], xs.at[d], xr.at[d], at(z, y, other, c)))
    result = hidden_ref[...] + mixed[x, c]
    for d in (1, 3, 2):
        source = lax.rem(x + NX - d, NX)
        await_copy(home_in.at[source], xs.at[d], xr.at[d], at(z, y, source, c))
        result = result + home_in[source].astype(F32)
    out_ref[...] = result.astype(BF16)

    for i in range(4):
        for e in range(2):
            p = order[i]

            @pl.when(jnp.logical_and(p <= zl, zl < 3))
            def _(p=p, e=e):
                forward(p, e)[0].wait_send()

            @pl.when(jnp.logical_and(p >= zl, zl > 0))
            def _(p=p, e=e):
                forward(p, e)[1].wait_send()

            if i > 0:

                @pl.when(p > zl)
                def _(p=p, e=e):
                    line_copy(p, e, 0).wait_send()

                @pl.when(p < zl)
                def _(p=p, e=e):
                    line_copy(p, e, 1).wait_send()

    for copy in sends:
        copy.wait_send()


VMEM = pl.BlockSpec(memory_space=pltpu.VMEM)
ANY = pl.BlockSpec(memory_space=pl.ANY)
DMA = pltpu.SemaphoreType.DMA
LIMIT = 56 * 2**20


def attention_call(*operands):
    bf = lambda *shape: pltpu.VMEM(shape, BF16)
    fl = lambda *shape: pltpu.VMEM(shape, F32)
    return pl.pallas_call(
        attention_kernel,
        out_shape=(
            jax.ShapeDtypeStruct((16, DM), F32),
            jax.ShapeDtypeStruct((128, DM), BF16),
            jax.ShapeDtypeStruct((128, 128), jnp.int32),
        ),
        in_specs=[VMEM] * 8,
        out_specs=(VMEM, VMEM, VMEM),
        scratch_shapes=[
            fl(4, 128, 128),
            bf(4, 128, 128),
            bf(4, 128, 128),
            bf(128, 128),
            bf(8, 128, 128),
            fl(128, 128),
            bf(4, 128, 128),
            bf(4, 128, 128),
            bf(32, SHARD, 512),
            bf(4, 2, 16, 512),
            bf(4, 16, DM),
            bf(4, 16, DM),
            fl(4, 16, DM),
            bf(4, 16, DM),
            bf(4, 16, DM),
            bf(4, 2, 16, DM),
            pltpu.VMEM((4, 2, 16, 128), jnp.int32),
            DMA((4,)),
            DMA((4,)),
            DMA((8,)),
            DMA((8,)),
            DMA((4,)),
            DMA((4,)),
            DMA((2, 5)),
            DMA((2, 5)),
            DMA((8, 2, 2)),
            DMA((8, 2, 2)),
            DMA((2,)),
            DMA((4,)),
            DMA((4,)),
            DMA((2, 4)),
            DMA((2, 4)),
            DMA((2, 4)),
            DMA((2, 4)),
        ],
        compiler_params=pltpu.CompilerParams(
            collective_id=0, has_side_effects=True, vmem_limit_bytes=LIMIT
        ),
        name="attend",
    )(*operands)


def expert_call(*operands):
    bf = lambda *shape: pltpu.VMEM(shape, BF16)
    fl = lambda *shape: pltpu.VMEM(shape, F32)
    return pl.pallas_call(
        expert_kernel,
        out_shape=jax.ShapeDtypeStruct((16, DM), BF16),
        in_specs=[VMEM] * 4 + [ANY] * 3,
        out_specs=VMEM,
        scratch_shapes=[
            bf(DM, 288),
            bf(DM, 288),
            bf(288, DM),
            bf(32, CHUNK, HALF),
            bf(CHUNK, HALF),
            bf(768, DM),
            bf(32, CHUNK, HALF),
            bf(8, CHUNK, 768),
            bf(8, CHUNK, 768),
            bf(8, CHUNK, HALF),
            bf(8, CHUNK, HALF),
            fl(8, CHUNK, HALF),
            bf(4, 2, CHUNK, HALF),
            bf(2, 4, 2, CHUNK, HALF),
            bf(2, CHUNK, HALF),
            bf(CHUNK, HALF),
            fl(4, 2, 16, DM),
            bf(4, 16, DM),
            bf(4, 16, DM),
            bf(4, 16, DM),
            bf(4, 16, DM),
            DMA((3,)),
            DMA,
            DMA,
            DMA((2, 4, 2)),
            DMA((4, 2)),
            DMA((8, 2, 2)),
            DMA((8, 2, 2)),
            DMA((8, 2, 2)),
            DMA((8, 2, 2)),
            DMA((4, 2)),
            DMA((2, 4, 2)),
            DMA,
            DMA,
            DMA,
            DMA,
            DMA((4,)),
            DMA((4,)),
        ],
        compiler_params=pltpu.CompilerParams(
            collective_id=1, has_side_effects=True, vmem_limit_bytes=LIMIT
        ),
        name="experts",
    )(*operands)


def body(
    stream,
    query,
    key,
    value,
    decay_rate,
    out_weight,
    norm_gain,
    router_weight,
    routes,
    expert_gate,
    expert_up,
    expert_down,
):
    wide_routes = jnp.pad(routes, ((0, 0), (0, 126)))
    hidden, rows, table = attention_call(
        stream,
        query,
        key,
        value,
        decay_rate.reshape(1, 4),
        out_weight.T,
        norm_gain.reshape(1, DM),
        wide_routes,
    )
    return expert_call(hidden, rows, table, router_weight, expert_gate, expert_up, expert_down)


def solution(mesh):
    placed = (
        P(("ctx", "ep"), None),
        P("ctx", "ep"),
        P("ctx", "ep"),
        P("ctx", "ep"),
        P("ep"),
        P("ep", "ctx"),
        P(),
        P(),
        P(("ctx", "ep"), None),
        P(None, ("ep", "ctx")),
        P(None, ("ep", "ctx")),
        P(("ep", "ctx"), None),
    )
    return jax.shard_map(
        body, mesh=mesh, in_specs=placed, out_specs=P(("ctx", "ep"), None), check_vma=False
    )
```

```python
import jax
import jax.numpy as jnp
from jax import lax
from jax.experimental import pallas as pl
from jax.experimental.pallas import tpu as pltpu
from jax.sharding import PartitionSpec as P

EPSILON = 1e-06
MESH = pl.DeviceIdType.MESH
F32 = jnp.float32
BF16 = jnp.bfloat16
NY = 4
NZ = 8
NX = 4
DM = 3072
HALF = 1536
SLOTS = 24
CHUNK = 48
SHARD = 96
HIDDEN = 288
PIECE = 144


def bf(*shape):
    return pltpu.VMEM(shape, BF16)


def fl(*shape):
    return pltpu.VMEM(shape, F32)


def dma(*shape):
    return pltpu.SemaphoreType.DMA(shape)


INPUTS = (
    "stream", "query", "key", "value", "rates", "weight", "gain", "routes", "router",
    "gate_hbm", "up_hbm", "down_hbm", "out",
)
SCRATCH = dict(
    intra=fl(4, 128, 128),
    local_out=bf(4, 128, 128),
    local_in=bf(4, 128, 128),
    total_out=bf(128, 128),
    total_in=bf(8, 128, 128),
    entry=fl(128, 128),
    state_out=bf(4, 128, 128),
    state_in=bf(4, 128, 128),
    proj=bf(8, SHARD, 512),
    heads=bf(4, 4, 2, 16, 512),
    pair_out=bf(4, 4, 16, 768),
    pair_in=bf(4, 4, 16, 768),
    part=fl(4, 4, 16, 768),
    part_out=bf(4, 4, 16, 768),
    part_in=bf(4, 4, 16, 768),
    slab=fl(4, 16, 768),
    slab_out=bf(4, 16, 768),
    slab_in=bf(4, 16, 768),
    hidden=fl(16, DM),
    tokens=bf(4, 2, 16, DM),
    tables=pltpu.VMEM((4, 2, 16, 128), jnp.int32),
    gate=bf(2 * HIDDEN, DM),
    up=bf(2 * HIDDEN, DM),
    down=bf(2 * HIDDEN, DM),
    sel=bf(2, 2, 2, 128, CHUNK),
    share=fl(2, 2, 128, 128),
    cross=bf(2, CHUNK, HALF),
    line=bf(2, 4, CHUNK, HALF),
    got=bf(3, 4, CHUNK, HALF),
    flat=bf(192, DM),
    partial=bf(4, 4, CHUNK, HALF),
    back=bf(3, 4, CHUNK, HALF),
    total=fl(2, 4, CHUNK, HALF),
    line_out=bf(2, 4, CHUNK, HALF),
    line_in=bf(2, 2, 4, CHUNK, HALF),
    final=bf(2, CHUNK, HALF),
    ret=bf(2, CHUNK, HALF),
    mixed=fl(4, 2, 16, DM),
    home_out=bf(4, 2, 16, DM),
    home_in=bf(4, 16, DM),
    home=fl(16, DM),
    load_sem=dma(3),
    local_s=dma(4), local_r=dma(4),
    total_s=dma(8), total_r=dma(8),
    state_s=dma(4), state_r=dma(4),
    proj_s=dma(2, 5), proj_r=dma(2, 5),
    heads_s=dma(4), heads_r=dma(4),
    pair_s=dma(1), pair_r=dma(1),
    part_s=dma(4), part_r=dma(4),
    slab_s=dma(4), slab_r=dma(4),
    tok_s=dma(2, 4), tok_r=dma(2, 4, 2),
    own_s=dma(3), own_r=dma(3),
    swap_s=dma(3, 2), swap_r=dma(3, 2),
    pass_s=dma(3, 2), pass_r=dma(3, 2),
    cross_s=dma(2), cross_r=dma(2),
    line_s=dma(2, 2, 4), line_r=dma(2, 4),
    got_s=dma(3, 4), got_r=dma(3, 4),
    back_s=dma(3, 4), back_r=dma(3, 4),
    sum_s=dma(2, 4), sum_r=dma(2, 2, 4),
    ret_s=dma(2), ret_r=dma(2),
    home_s=dma(4, 2), home_r=dma(4),
)


class Refs:
    def __init__(self, refs):
        for name, ref in zip(INPUTS + tuple(SCRATCH), refs, strict=True):
            setattr(self, name, ref)


def at(z, y, x, c):
    return (z * NY + y, x * 2 + c)


def remote(src, dst, send, recv, device):
    return pltpu.make_async_remote_copy(
        src_ref=src,
        dst_ref=dst,
        send_sem=send,
        recv_sem=recv,
        device_id=device,
        device_id_type=MESH,
    )


def await_copy(dst, send, recv, device):
    remote(dst, dst, send, recv, device).wait_recv()


def greet(barrier, devices):
    for device in devices:
        pl.semaphore_signal(barrier, inc=1, device_id=device, device_id_type=MESH)


def nt_dot(a, b):
    return lax.dot_general(a, b, (((1,), (1,)), ((), ())), preferred_element_type=F32)


def tn_dot(a, b):
    return lax.dot_general(a, b, (((0,), (0,)), ((), ())), preferred_element_type=F32)


def dot(a, b):
    return jnp.dot(a, b, preferred_element_type=F32)


def kernel(*refs):
    r = Refs(refs)
    ctx = lax.axis_index("ctx")
    ep = lax.axis_index("ep")
    z, y, x, c = ctx // NY, ctx % NY, ep // 2, ep % 2
    half, zl = z // 4, z % 4
    role = y % 2
    source = z % 2 == c
    keeper = c == role
    core = z % 2

    def ring_y(d):
        return lax.rem(y + d + NY, NY)

    def ring_z(d):
        return lax.rem(z + d + NZ, NZ)

    def ring_x(d):
        return lax.rem(x + d + NX, NX)

    def on_y(d):
        return at(z, ring_y(d), x, c)

    def on_z(d):
        return at(ring_z(d), y, x, c)

    def on_x(d):
        return at(z, y, ring_x(d), c)

    partner = at(z, y, x, 1 - c)
    mirror = at(NZ - 1 - z, y, x, c)
    swap_to = (at(z, ring_y(1), x, 1 - c), at(z, ring_y(-1), x, 1 - c))
    barrier = pltpu.get_barrier_semaphore()
    greet(barrier, [on_y(d) for d in range(1, NY)])
    greet(barrier, [on_z(d) for d in range(1, NZ)])
    greet(barrier, [on_x(d) for d in range(1, NX)])
    greet(barrier, [at(z, y, ring_x(d), 1 - c) for d in range(NX)])
    greet(barrier, swap_to)
    sends = []
    guarded = []

    def launch(copy):
        copy.start()
        sends.append(copy)

    def launch_if(condition, make):
        @pl.when(condition)
        def _():
            make().start()

        guarded.append((condition, make))

    experts = ((r.gate_hbm, r.gate), (r.up_hbm, r.up), (r.down_hbm, r.down))
    own_rows = pl.ds(0, HIDDEN)
    piece_rows = (pl.ds(HIDDEN, PIECE), pl.ds(HIDDEN + PIECE, PIECE))

    def load(m):
        hbm, ref = experts[m]
        return pltpu.make_async_copy(hbm, ref.at[own_rows], r.load_sem.at[m])

    @pl.when(keeper)
    def _():
        for m in range(3):
            load(m).start()

    rates = r.rates[...]
    length = r.query.shape[0]
    gap = (
        lax.broadcasted_iota(jnp.int32, (length, length), 0)
        - lax.broadcasted_iota(jnp.int32, (length, length), 1)
    ).astype(F32)
    position = lax.broadcasted_iota(jnp.int32, (length, 1), 0).astype(F32)

    def head(ref, h):
        return ref[:, 128 * h : 128 * (h + 1)]

    for h in range(4):
        fade = jnp.exp(-rates[:, h : h + 1] * (length - 1.0 - position))
        faded = (head(r.key, h).astype(F32) * fade).astype(BF16)
        r.local_out[h] = tn_dot(faded, head(r.value, h)).astype(BF16)
    r.proj[z] = r.weight[...]
    pl.semaphore_wait(barrier, NY - 1 + NZ - 1 + NX - 1 + NX + 2)

    for d in (2, 1, 3):
        launch(
            remote(
                r.local_out.at[ring_y(d)], r.local_in.at[y], r.local_s.at[d], r.local_r.at[d], on_y(d)
            )
        )
    r.local_in[y] = r.local_out[y]

    def z_parts(k):
        if k < 4:
            return r.proj.at[ring_z(1 - k)], r.proj.at[ring_z(k - 1)]
        return r.proj.at[ring_z(-3)].at[pl.ds(0, 48)], r.proj.at[ring_z(3)].at[pl.ds(48, 48)]

    def z_step(k):
        a, b = z_parts(k)
        launch(remote(a, a, r.proj_s.at[0, k], r.proj_r.at[0, k], on_z(1)))
        launch(remote(b, b, r.proj_s.at[1, k], r.proj_r.at[1, k], on_z(-1)))

    def z_wait(k):
        if k < 4:
            a, b = r.proj.at[ring_z(-k)], r.proj.at[ring_z(k)]
        else:
            a, b = r.proj.at[ring_z(4)].at[pl.ds(0, 48)], r.proj.at[ring_z(4)].at[pl.ds(48, 48)]
        await_copy(a, r.proj_s.at[0, k], r.proj_r.at[0, k], on_z(1))
        await_copy(b, r.proj_s.at[1, k], r.proj_r.at[1, k], on_z(-1))

    z_step(1)
    for m in range(3):
        launch_if(
            keeper,
            lambda m=m: remote(
                experts[m][0], experts[m][1].at[own_rows], r.own_s.at[m], r.own_r.at[m], partner
            ),
        )

    for h in range(4):
        decay = jnp.where(gap >= 0, jnp.exp(-rates[:, h : h + 1] * jnp.maximum(gap, 0.0)), 0.0)
        scores = nt_dot(head(r.query, h), head(r.key, h))
        r.intra[h] = dot((scores * decay).astype(BF16), head(r.value, h))

    for d in (1, 3, 2):
        await_copy(r.local_in.at[ring_y(-d)], r.local_s.at[d], r.local_r.at[d], on_y(d))
    lane = lax.broadcasted_iota(jnp.int32, rates.shape, 1)
    own_rate = jnp.sum(jnp.where(lane == y, rates, 0.0), axis=1, keepdims=True)

    def power(n):
        return jnp.exp(-own_rate * (128.0 * n))

    locals_in = [r.local_in[i].astype(F32) for i in range(NY)]
    total = locals_in[3]
    for i in range(3):
        total = total + power(3 - i) * locals_in[i]
    r.total_out[...] = total.astype(BF16)
    for d in range(NZ - 1, 0, -1):
        launch_if(
            z + d < NZ,
            lambda d=d: remote(
                r.total_out, r.total_in.at[z], r.total_s.at[d], r.total_r.at[d], on_z(d)
            ),
        )
    z_wait(1)
    z_step(2)
    r.entry[...] = jnp.zeros_like(r.entry)
    for d in range(1, NZ):

        @pl.when(z >= d)
        def _(d=d):
            await_copy(r.total_in.at[ring_z(-d)], r.total_s.at[d], r.total_r.at[d], on_z(d))
            r.entry[...] += power(4 * (d - 1)) * r.total_in[ring_z(-d)].astype(F32)

    incoming = r.entry[...]
    for i in range(NY):
        r.state_out[i] = incoming.astype(BF16)
        incoming = power(1) * incoming + locals_in[i]
    for d in (2, 1, 3):
        launch(
            remote(
                r.state_out.at[ring_y(d)], r.state_in.at[y], r.state_s.at[d], r.state_r.at[d], on_y(d)
            )
        )
    r.state_in[y] = r.state_out[y]
    z_wait(2)
    z_step(3)
    for d in (1, 3, 2):
        await_copy(r.state_in.at[ring_y(-d)], r.state_s.at[d], r.state_r.at[d], on_y(d))
    for h in range(4):
        fade = jnp.exp(-rates[:, h : h + 1] * (position + 1.0))
        mixed = r.intra[h] + fade * dot(head(r.query, h), r.state_in[h])
        mean = jnp.mean(mixed * mixed, axis=-1, keepdims=True)
        out = (mixed * lax.rsqrt(mean + EPSILON)).astype(BF16)
        for e in range(8):
            r.heads[y, e // 2, e % 2, :, 128 * h : 128 * (h + 1)] = out[16 * e : 16 * (e + 1)]
    for d in (2, 1, 3):
        launch(remote(r.heads.at[y], r.heads.at[y], r.heads_s.at[d], r.heads_r.at[d], on_y(d)))
    z_wait(3)
    z_step(4)

    for m in range(3):
        for side in range(2):
            launch_if(
                jnp.logical_not(keeper),
                lambda m=m, side=side: remote(
                    experts[m][0].at[pl.ds(side * PIECE, PIECE)],
                    experts[m][1].at[piece_rows[side]],
                    r.swap_s.at[m, side],
                    r.swap_r.at[m, side],
                    swap_to[side],
                ),
            )

    def pass_on(m):
        for side in range(2):
            ref = experts[m][1].at[piece_rows[side]]

            @pl.when(jnp.logical_not(keeper))
            def _(m=m, side=side, ref=ref):
                await_copy(ref, r.swap_s.at[m, side], r.swap_r.at[m, side], swap_to[1 - side])

            launch_if(
                jnp.logical_not(keeper),
                lambda m=m, side=side, ref=ref: remote(
                    ref, ref, r.pass_s.at[m, side], r.pass_r.at[m, side], partner
                ),
            )

    def weights_ready():
        @pl.when(keeper)
        def _():
            for m in range(3):
                load(m).wait()
                for side in range(2):
                    ref = experts[m][1].at[piece_rows[side]]
                    await_copy(ref, r.pass_s.at[m, side], r.pass_r.at[m, side], partner)

        @pl.when(jnp.logical_not(keeper))
        def _():
            for m in range(3):
                ref = experts[m][1].at[own_rows]
                await_copy(ref, r.own_s.at[m], r.own_r.at[m], partner)

    for d in (1, 3, 2):
        await_copy(r.heads.at[ring_y(-d)], r.heads_s.at[d], r.heads_r.at[d], on_y(d))
    z_wait(4)

    def project(which):
        lhs = r.heads[:, :, which].reshape(256, 512)
        return nt_dot(lhs, r.proj[...].reshape(768, 512)).reshape(4, 4, 16, 768)

    r.pair_out[...] = project(1 - c).astype(BF16)
    pair_copy = remote(r.pair_out, r.pair_in, r.pair_s.at[0], r.pair_r.at[0], partner)
    launch(pair_copy)
    r.part[...] = project(c)
    pair_copy.wait_recv()
    r.part[...] += r.pair_in[...].astype(F32)
    r.part_out[...] = r.part[...].astype(BF16)
    for d in (2, 1, 3):
        launch(
            remote(
                r.part_out.at[:, ring_x(d)], r.part_in.at[x], r.part_s.at[d], r.part_r.at[d], on_x(d)
            )
        )
    slab = r.part[:, x]
    for d in (1, 3, 2):
        await_copy(r.part_in.at[ring_x(-d)], r.part_s.at[d], r.part_r.at[d], on_x(d))
        slab = slab + r.part_in[ring_x(-d)].astype(F32)
    r.slab[...] = slab
    r.slab_out[...] = slab.astype(BF16)
    for d in (2, 1, 3):
        launch(
            remote(
                r.slab_out.at[ring_y(d)], r.slab_in.at[y], r.slab_s.at[d], r.slab_r.at[d], on_y(d)
            )
        )
    for d in (1, 3, 2):
        await_copy(r.slab_in.at[ring_y(-d)], r.slab_s.at[d], r.slab_r.at[d], on_y(d))
        r.slab[ring_y(-d)] = r.slab_in[ring_y(-d)].astype(F32)
    attended = jnp.concatenate(
        [r.slab[yy][:, SHARD * zz : SHARD * (zz + 1)] for zz in range(NZ) for yy in range(NY)], axis=1
    )
    hidden = r.stream[...].astype(F32) + attended
    r.hidden[...] = hidden
    mean = jnp.mean(hidden * hidden, axis=-1, keepdims=True)
    r.tokens[x, c] = (hidden * lax.rsqrt(mean + EPSILON) * r.gain[...]).astype(BF16)
    square = lax.broadcasted_iota(jnp.int32, (16, 16), 0) == lax.broadcasted_iota(
        jnp.int32, (16, 16), 1
    )

    def upright(row):
        wide = jnp.where(square, jnp.broadcast_to(row, (16, 16)).astype(F32), 0.0)
        return jnp.sum(wide, axis=1, keepdims=True)

    table_lane = lax.broadcasted_iota(jnp.int32, (16, 128), 1)
    r.tables[x, c] = jnp.where(
        table_lane == 0, upright(r.routes[0:1, :]), upright(r.routes[1:2, :])
    ).astype(jnp.int32)

    for d in (2, 1, 3, 0):
        for n, ref in enumerate((r.tokens, r.tables)):

            def make(d=d, n=n, ref=ref):
                block = ref.at[x, c]
                device = at(z, y, ring_x(d), core)
                return remote(block, block, r.tok_s.at[n, d], r.tok_r.at[n, d, c], device)

            if d:
                launch(make())
            else:
                launch_if(jnp.logical_not(source), make)

    pass_on(0)
    pass_on(1)

    low_lane = lax.broadcasted_iota(jnp.int32, (128, CHUNK), 1) < SLOTS

    def expert_of(rel, t):
        return x * 4 + t * 2 + (half if rel == 0 else 1 - half)

    @pl.when(source)
    def _():
        for d in (0, 1, 3, 2):
            for n, ref in enumerate((r.tokens, r.tables)):
                for other in range(2):
                    if d == 0 and other == 1:
                        continue
                    cc = 1 - c if d == 0 else other
                    block = ref.at[ring_x(-d), cc]
                    await_copy(block, r.tok_s.at[n, d], r.tok_r.at[n, d, cc], on_x(d))
        rows = r.tokens[...].reshape(128, DM)
        table = r.tables[...].reshape(128, 128)
        first, second = table[:, 0:1], table[:, 1:2]
        lanes = lax.broadcasted_iota(jnp.int32, (128, 128), 1)
        earlier = (lanes < lax.broadcasted_iota(jnp.int32, (128, 128), 0)).astype(BF16)
        for rel in (1, 0):
            for t in range(2):
                expert = expert_of(rel, t)
                hit = jnp.logical_or(first == expert, second == expert)
                wide = jnp.broadcast_to(jnp.where(hit, 1.0, 0.0), (128, 128))
                rank = dot(earlier, wide.astype(BF16)).astype(jnp.int32)
                low = jnp.where(rank == lanes, wide, 0.0)[:, :CHUNK]
                high = jnp.where(rank == lanes - SLOTS, wide, 0.0)[:, :CHUNK]
                low = jnp.where(low_lane, low, 0.0).astype(BF16)
                high = jnp.where(low_lane, 0.0, high).astype(BF16)
                r.sel[rel, t, 0] = low
                r.sel[rel, t, 1] = high
                chunk = (tn_dot(low, rows[:, :HALF]) + tn_dot(high, rows[:, HALF:])).astype(BF16)
                if rel == 0:
                    r.line[t, zl] = chunk
                else:
                    r.cross[t] = chunk
                    remote(
                        r.cross.at[t], r.line.at[t, 3 - zl], r.cross_s.at[t], r.cross_r.at[t], mirror
                    ).start()

    @pl.when(jnp.logical_not(source))
    def _():
        for t in range(2):
            await_copy(r.line.at[t, zl], r.cross_s.at[t], r.cross_r.at[t], mirror)

    order = [zl, zl + 1 - 2 * (zl % 2), 2 - zl // 2, 3 - 3 * (zl // 2)]

    def spread(i):
        p = order[i]
        for t in range(2):
            s = r.line.at[t, p]
            if i > 0:
                await_copy(s, r.line_s.at[0, t, p], r.line_r.at[t, p], on_z(1))
            launch_if(
                jnp.logical_and(p <= zl, zl < 3),
                lambda s=s, t=t, p=p: remote(
                    s, s, r.line_s.at[0, t, p], r.line_r.at[t, p], on_z(1)
                ),
            )
            launch_if(
                jnp.logical_and(p >= zl, zl > 0),
                lambda s=s, t=t, p=p: remote(
                    s, s, r.line_s.at[1, t, p], r.line_r.at[t, p], on_z(-1)
                ),
            )
        for j, d, t in ((0, 2, role), (1, 1, 1 - role), (2, -1, 1 - role)):
            launch(
                remote(
                    r.line.at[t, p], r.got.at[j, p], r.got_s.at[j, p], r.got_r.at[j, p], on_y(d)
                )
            )

    for i in range(4):
        spread(i)

    pass_on(2)

    @pl.when(source)
    def _():
        logits = nt_dot(r.tokens[...].reshape(128, DM), r.router[...])
        table = r.tables[...].reshape(128, 128)
        first, second = table[:, 0:1], table[:, 1:2]
        expert = lax.broadcasted_iota(jnp.int32, logits.shape, 1)

        def lifted(chosen):
            logit = jnp.sum(jnp.where(expert == chosen, logits, 0.0), axis=1, keepdims=True)
            return jax.nn.sigmoid(logit)

        lift_first, lift_second = lifted(first), lifted(second)
        both = lift_first + lift_second
        for rel in range(2):
            for t in range(2):
                chosen = expert_of(rel, t)
                share = jnp.where(first == chosen, lift_first / both, 0.0) + jnp.where(
                    second == chosen, lift_second / both, 0.0
                )
                r.share[rel, t] = jnp.broadcast_to(share, (128, 128))

    def arrived(i):
        p = order[i]
        for j, d in ((0, 2), (1, 1), (2, -1)):
            await_copy(r.got.at[j, p], r.got_s.at[j, p], r.got_r.at[j, p], on_y(d))

    def compute(which):
        chunks = []
        for i in which:
            p = order[i]
            chunks += [r.line[role, p]] + [r.got[j, p] for j in range(3)]
        for n in range(4):
            a, b = chunks[2 * n].astype(F32), chunks[2 * n + 1].astype(F32)
            rows = slice(CHUNK * n, CHUNK * (n + 1))
            r.flat[rows, :HALF] = jnp.concatenate([a[:SLOTS], b[:SLOTS]], axis=0).astype(BF16)
            r.flat[rows, HALF:] = jnp.concatenate([a[SLOTS:], b[SLOTS:]], axis=0).astype(BF16)
        rows = r.flat[...]
        gated = nt_dot(rows, r.gate[...])
        inner = (gated * jax.nn.sigmoid(gated) * nt_dot(rows, r.up[...])).astype(BF16)
        left = dot(inner, r.down[:, :HALF])
        right = dot(inner, r.down[:, HALF:])
        for n, i in enumerate(which):
            for j in range(4):
                rows = slice(SLOTS * (4 * n + j), SLOTS * (4 * n + j + 1))
                r.partial[j, order[i]] = jnp.concatenate([left[rows], right[rows]], axis=0).astype(BF16)

    def give_back(i):
        p = order[i]
        for j, d in ((0, 2), (1, -1), (2, 1)):
            launch(
                remote(
                    r.partial.at[j + 1, p], r.back.at[j, p], r.back_s.at[j, p], r.back_r.at[j, p], on_y(d)
                )
            )

    arrived(0)
    arrived(1)
    weights_ready()
    compute((0, 1))
    arrived(2)
    arrived(3)
    compute((3, 2))
    for i in (3, 2, 1, 0):
        give_back(i)

    def collect(i):
        p = order[i]
        for j, d in ((0, 2), (1, 1), (2, -1)):
            await_copy(r.back.at[j, p], r.back_s.at[j, p], r.back_r.at[j, p], on_y(d))
        r.total[role, p] = r.partial[0, p].astype(F32) + r.back[0, p].astype(F32)
        r.total[1 - role, p] = r.back[1, p].astype(F32) + r.back[2, p].astype(F32)

    def add_line(t, p, side):
        await_copy(r.line_in.at[side, t, p], r.sum_s.at[t, p], r.sum_r.at[side, t, p], on_z(1))
        r.total[t, p] += r.line_in[side, t, p].astype(F32)

    def along(i):
        p = order[i]
        for t in range(2):

            @pl.when(jnp.logical_and(p > zl, zl > 0))
            def _(t=t):
                add_line(t, p, 0)

            @pl.when(jnp.logical_and(p < zl, zl < 3))
            def _(t=t):
                add_line(t, p, 1)

            r.line_out[t, p] = r.total[t, p].astype(BF16)
            for side, condition in ((0, p > zl), (1, p < zl)):
                launch_if(
                    condition,
                    lambda t=t, p=p, side=side: remote(
                        r.line_out.at[t, p],
                        r.line_in.at[side, t, p],
                        r.sum_s.at[t, p],
                        r.sum_r.at[side, t, p],
                        on_z(-1 if side else 1),
                    ),
                )

    for i in (3, 2, 1):
        collect(i)
        along(i)
    collect(0)
    for t in range(2):

        @pl.when(zl > 0)
        def _(t=t):
            add_line(t, zl, 0)

        @pl.when(zl < 3)
        def _(t=t):
            add_line(t, zl, 1)

        r.final[t] = r.total[t, zl].astype(BF16)
        launch_if(
            jnp.logical_not(source),
            lambda t=t: remote(r.final.at[t], r.ret.at[t], r.ret_s.at[t], r.ret_r.at[t], mirror),
        )

    @pl.when(source)
    def _():
        for rel in range(2):
            for t in range(2):
                if rel == 1:
                    await_copy(r.ret.at[t], r.ret_s.at[t], r.ret_r.at[t], mirror)
                rows = (r.ret if rel else r.final)[t]
                share = r.share[rel, t][:, 0:1]
                for side in range(2):
                    cols = slice(HALF * side, HALF * (side + 1))
                    value = (share * dot(r.sel[rel, t, side], rows)).reshape(4, 2, 16, HALF)
                    if rel == 0 and t == 0:
                        r.mixed[:, :, :, cols] = value
                    else:
                        r.mixed[:, :, :, cols] += value
        r.home_out[...] = r.mixed[...].astype(BF16)
        r.home[...] = r.mixed[x, c]

    for d in (2, 1, 3, 0):
        for other in range(2):
            if d == 0 and other == 1:
                continue
            cc = 1 - c if d == 0 else other
            launch_if(
                source,
                lambda d=d, cc=cc: remote(
                    r.home_out.at[ring_x(d), cc],
                    r.home_in.at[x],
                    r.home_s.at[d, cc],
                    r.home_r.at[d],
                    at(z, y, ring_x(d), cc),
                ),
            )

    @pl.when(jnp.logical_not(source))
    def _():
        await_copy(r.home_in.at[x], r.home_s.at[0, c], r.home_r.at[0], partner)
        r.home[...] = r.home_in[x].astype(F32)

    result = r.hidden[...] + r.home[...]
    for d in (1, 3, 2):
        await_copy(r.home_in.at[ring_x(-d)], r.home_s.at[d, c], r.home_r.at[d], on_x(d))
        result = result + r.home_in[ring_x(-d)].astype(F32)
    r.out[...] = result.astype(BF16)

    @pl.when(source)
    def _():
        for t in range(2):
            remote(
                r.cross.at[t], r.line.at[t, 3 - zl], r.cross_s.at[t], r.cross_r.at[t], mirror
            ).wait_send()

    for condition, make in guarded:

        @pl.when(condition)
        def _(make=make):
            make().wait_send()

    for copy in sends:
        copy.wait_send()


VMEM = pl.BlockSpec(memory_space=pltpu.VMEM)
ANY = pl.BlockSpec(memory_space=pl.ANY)


def body(
    stream,
    query,
    key,
    value,
    decay_rate,
    out_weight,
    norm_gain,
    router_weight,
    routes,
    expert_gate,
    expert_up,
    expert_down,
):
    return pl.pallas_call(
        kernel,
        out_shape=jax.ShapeDtypeStruct(stream.shape, BF16),
        in_specs=[VMEM] * 9 + [ANY] * 3,
        out_specs=VMEM,
        scratch_shapes=list(SCRATCH.values()),
        compiler_params=pltpu.CompilerParams(
            collective_id=0, has_side_effects=True, vmem_limit_bytes=56 * 2**20
        ),
        name="whole",
    )(
        stream,
        query,
        key,
        value,
        decay_rate.reshape(1, 4),
        out_weight.T,
        norm_gain.reshape(1, DM),
        routes.T,
        router_weight.T,
        expert_gate.T,
        expert_up.T,
        expert_down,
    )


def solution(mesh):
    placed = (
        P(("ctx", "ep"), None),
        P("ctx", "ep"),
        P("ctx", "ep"),
        P("ctx", "ep"),
        P("ep"),
        P("ep", "ctx"),
        P(),
        P(),
        P(("ctx", "ep"), None),
        P(None, ("ep", "ctx")),
        P(None, ("ep", "ctx")),
        P(("ep", "ctx"), None),
    )
    return jax.shard_map(
        body, mesh=mesh, in_specs=placed, out_specs=P(("ctx", "ep"), None), check_vma=False
    )
```

```python
import jax
import jax.numpy as jnp
from jax import lax
from jax.experimental import pallas as pl
from jax.experimental.pallas import tpu as pltpu
from jax.sharding import PartitionSpec as P

EPSILON = 1e-06
MESH = pl.DeviceIdType.MESH
F32 = jnp.float32
BF16 = jnp.bfloat16
NY = 4
NZ = 8
NX = 4
DM = 3072
HALF = 1536
SLOTS = 24
CHUNK = 48
SHARD = 96
HIDDEN = 288
PIECE = 96
PART = 48


def bf(*shape):
    return pltpu.VMEM(shape, BF16)


def fl(*shape):
    return pltpu.VMEM(shape, F32)


def dma(*shape):
    return pltpu.SemaphoreType.DMA(shape)


INPUTS = (
    "stream", "query", "key", "value", "rates", "weight", "gain", "routes", "router",
    "gate_hbm", "up_hbm", "down_hbm", "out",
)
SCRATCH = dict(
    intra=fl(4, 128, 128),
    key_in=bf(4, 128, 128),
    value_in=bf(4, 128, 128),
    query_in=bf(4, 128, 128),
    local=fl(4, 128, 128),
    total_out=bf(128, 128),
    total_in=bf(8, 128, 128),
    entry=fl(128, 128),
    proj=bf(8, SHARD, 512),
    heads=bf(4, 4, 4, 2, 16, 128),
    pair_out=bf(2, 4, 4, 16, 384),
    pair_in=bf(2, 4, 4, 16, 384),
    part=fl(2, 4, 4, 16, 384),
    part_out=bf(2, 4, 4, 16, 384),
    part_in=bf(2, 4, 4, 16, 384),
    slab=fl(2, 4, 16, 384),
    slab_out=bf(2, 4, 16, 384),
    slab_in=bf(2, 4, 16, 384),
    hidden=fl(16, DM),
    tokens=bf(4, 2, 16, DM),
    tables=pltpu.VMEM((4, 2, 16, 128), jnp.int32),
    gate=bf(2 * HIDDEN, DM),
    up=bf(2 * HIDDEN, DM),
    down=bf(2 * HIDDEN, DM),
    sel=bf(2, 2, 2, 128, CHUNK),
    share=fl(2, 2, 128, 128),
    cross=bf(2, CHUNK, HALF),
    line=bf(2, 4, CHUNK, HALF),
    got=bf(3, 4, CHUNK, HALF),
    flat=bf(192, DM),
    partial=bf(4, 4, CHUNK, HALF),
    back=bf(3, 4, CHUNK, HALF),
    total=fl(2, 4, CHUNK, HALF),
    line_out=bf(2, 4, CHUNK, HALF),
    line_in=bf(2, 2, 4, CHUNK, HALF),
    ret=bf(2, CHUNK, HALF),
    mixed=fl(4, 2, 16, DM),
    home_out=bf(4, 2, 16, DM),
    home_in=bf(4, 16, DM),
    home=fl(16, DM),
    load_sem=dma(3),
    block_s=dma(3, 4), block_r=dma(3, 4),
    total_s=dma(8), total_r=dma(8),
    proj_s=dma(2, 5), proj_r=dma(2, 5),
    heads_s=dma(4), heads_r=dma(4),
    pair_s=dma(2), pair_r=dma(2),
    part_s=dma(2, 4), part_r=dma(2, 4),
    slab_s=dma(2, 4), slab_r=dma(2, 4),
    tok_s=dma(2, 4), tok_r=dma(2, 4, 2),
    own_s=dma(3), own_r=dma(3),
    swap_s=dma(3, 2, 3), swap_r=dma(3, 2, 3),
    pass_s=dma(3, 2, 3), pass_r=dma(3, 2, 3),
    cross_s=dma(2, 2),
    line_s=dma(2, 2, 4, 2), line_r=dma(2, 4, 2),
    got_s=dma(3, 4), got_r=dma(3, 4),
    back_s=dma(3, 4), back_r=dma(3, 4),
    sum_s=dma(2, 4, 2), sum_r=dma(2, 2, 4, 2),
    ret_r=dma(2, 2),
    home_s=dma(2, 4, 2), home_r=dma(2, 4),
)


class Refs:
    def __init__(self, refs):
        for name, ref in zip(INPUTS + tuple(SCRATCH), refs, strict=True):
            setattr(self, name, ref)


def at(z, y, x, c):
    return (z * NY + y, x * 2 + c)


def remote(src, dst, send, recv, device):
    return pltpu.make_async_remote_copy(
        src_ref=src,
        dst_ref=dst,
        send_sem=send,
        recv_sem=recv,
        device_id=device,
        device_id_type=MESH,
    )


def await_copy(dst, send, recv, device):
    remote(dst, dst, send, recv, device).wait_recv()


def greet(barrier, devices):
    for device in devices:
        pl.semaphore_signal(barrier, inc=1, device_id=device, device_id_type=MESH)


def nt_dot(a, b):
    return lax.dot_general(a, b, (((1,), (1,)), ((), ())), preferred_element_type=F32)


def tn_dot(a, b):
    return lax.dot_general(a, b, (((0,), (0,)), ((), ())), preferred_element_type=F32)


def dot(a, b):
    return jnp.dot(a, b, preferred_element_type=F32)


def kernel(*refs):
    r = Refs(refs)
    ctx = lax.axis_index("ctx")
    ep = lax.axis_index("ep")
    z, y, x, c = ctx // NY, ctx % NY, ep // 2, ep % 2
    half, zl = z // 4, z % 4
    role = (y + z) % 2
    source = z % 2 == c
    keeper = c == role
    core = z % 2

    def ring_y(d):
        return lax.rem(y + d + NY, NY)

    def ring_z(d):
        return lax.rem(z + d + NZ, NZ)

    def ring_x(d):
        return lax.rem(x + d + NX, NX)

    def on_y(d):
        return at(z, ring_y(d), x, c)

    def on_z(d):
        return at(ring_z(d), y, x, c)

    def on_x(d):
        return at(z, y, ring_x(d), c)

    partner = at(z, y, x, 1 - c)
    beside = z + 1 - 2 * (z % 2)
    swap_to = (
        at(z, ring_y(1), x, 1 - c),
        at(z, ring_y(-1), x, 1 - c),
        at(beside, y, x, 1 - c),
    )
    barrier = pltpu.get_barrier_semaphore()
    greet(barrier, [on_y(d) for d in range(1, NY)])
    greet(barrier, [on_z(d) for d in range(1, NZ)])
    greet(barrier, [on_x(d) for d in range(1, NX)])
    greet(barrier, [at(z, y, ring_x(d), 1 - c) for d in range(NX)])
    greet(barrier, swap_to)
    sends = []
    guarded = []

    def launch(copy):
        copy.start()
        sends.append(copy)

    def launch_if(condition, make):
        @pl.when(condition)
        def _():
            make().start()

        guarded.append((condition, make))

    experts = ((r.gate_hbm, r.gate), (r.up_hbm, r.up), (r.down_hbm, r.down))
    own_rows = pl.ds(0, HIDDEN)

    def part_rows(base, k, side):
        return pl.ds(base + side * PIECE + k * PART, PART)

    def load(m):
        hbm, ref = experts[m]
        return pltpu.make_async_copy(hbm, ref.at[own_rows], r.load_sem.at[m])

    @pl.when(keeper)
    def _():
        for m in range(3):
            load(m).start()

    away = jnp.logical_not(keeper)
    back_side = (1, 0, 2)

    def swap(sides, units):
        for unit in units:
            m, k = divmod(unit, 2)
            for side in sides:
                launch_if(
                    away,
                    lambda m=m, k=k, side=side: remote(
                        experts[m][0].at[part_rows(0, k, side)],
                        experts[m][1].at[part_rows(HIDDEN, k, side)],
                        r.swap_s.at[m, k, side],
                        r.swap_r.at[m, k, side],
                        swap_to[side],
                    ),
                )

    def pass_on(sides, units):
        for unit in units:
            m, k = divmod(unit, 2)
            for side in sides:
                ref = experts[m][1].at[part_rows(HIDDEN, k, side)]

                @pl.when(away)
                def _(m=m, k=k, side=side, ref=ref):
                    await_copy(
                        ref,
                        r.swap_s.at[m, k, side],
                        r.swap_r.at[m, k, side],
                        swap_to[back_side[side]],
                    )

                launch_if(
                    away,
                    lambda m=m, k=k, side=side, ref=ref: remote(
                        ref, ref, r.pass_s.at[m, k, side], r.pass_r.at[m, k, side], partner
                    ),
                )

    def weights_ready():
        @pl.when(keeper)
        def _():
            for m in range(3):
                load(m).wait()
                for k in range(2):
                    for side in range(3):
                        ref = experts[m][1].at[part_rows(HIDDEN, k, side)]
                        await_copy(ref, r.pass_s.at[m, k, side], r.pass_r.at[m, k, side], partner)

        @pl.when(away)
        def _():
            for m in range(3):
                ref = experts[m][1].at[own_rows]
                await_copy(ref, r.own_s.at[m], r.own_r.at[m], partner)

    rates = r.rates[...]
    length = r.query.shape[0]
    gap = (
        lax.broadcasted_iota(jnp.int32, (length, length), 0)
        - lax.broadcasted_iota(jnp.int32, (length, length), 1)
    ).astype(F32)
    position = lax.broadcasted_iota(jnp.int32, (length, 1), 0).astype(F32)
    lane = lax.broadcasted_iota(jnp.int32, rates.shape, 1)
    own_rate = jnp.sum(jnp.where(lane == y, rates, 0.0), axis=1, keepdims=True)

    def power(n):
        return jnp.exp(-own_rate * (128.0 * n))

    def head_columns(h):
        return pl.ds(pl.multiple_of(h * 128, 128), 128)

    blocks = ((r.key, r.key_in), (r.value, r.value_in), (r.query, r.query_in))
    for whole, own in blocks:
        own[y] = whole[:, head_columns(y)]
    r.proj[z] = r.weight[...]
    pl.semaphore_wait(barrier, NY - 1 + NZ - 1 + NX - 1 + NX + 3)

    for n, (whole, own) in enumerate(blocks):
        for d in (2, 1, 3):
            launch(
                remote(
                    whole.at[:, head_columns(ring_y(d))],
                    own.at[y],
                    r.block_s.at[n, d],
                    r.block_r.at[n, d],
                    on_y(d),
                )
            )

    def block_wait(n, d):
        await_copy(blocks[n][1].at[ring_y(-d)], r.block_s.at[n, d], r.block_r.at[n, d], on_y(d))

    def z_parts(k):
        if k < 4:
            return r.proj.at[ring_z(1 - k)], r.proj.at[ring_z(k - 1)]
        return r.proj.at[ring_z(-3)].at[pl.ds(0, 48)], r.proj.at[ring_z(3)].at[pl.ds(48, 48)]

    def z_step(k):
        a, b = z_parts(k)
        launch(remote(a, a, r.proj_s.at[0, k], r.proj_r.at[0, k], on_z(1)))
        launch(remote(b, b, r.proj_s.at[1, k], r.proj_r.at[1, k], on_z(-1)))

    def z_wait(k):
        if k < 4:
            a, b = r.proj.at[ring_z(-k)], r.proj.at[ring_z(k)]
        else:
            a, b = r.proj.at[ring_z(4)].at[pl.ds(0, 48)], r.proj.at[ring_z(4)].at[pl.ds(48, 48)]
        await_copy(a, r.proj_s.at[0, k], r.proj_r.at[0, k], on_z(1))
        await_copy(b, r.proj_s.at[1, k], r.proj_r.at[1, k], on_z(-1))

    z_step(1)
    swap((0, 1), (0,))
    for m in range(3):
        launch_if(
            keeper,
            lambda m=m: remote(
                experts[m][0], experts[m][1].at[own_rows], r.own_s.at[m], r.own_r.at[m], partner
            ),
        )

    fade = jnp.exp(-own_rate * (length - 1.0 - position))
    for d in (0, 1, 3, 2):
        if d:
            block_wait(0, d)
            block_wait(1, d)
        i = ring_y(-d)
        faded = (r.key_in[i].astype(F32) * fade).astype(BF16)
        r.local[i] = tn_dot(faded, r.value_in[i])
    swap((0, 1), (1,))
    total = r.local[3]
    for i in range(3):
        total = total + power(3 - i) * r.local[i]
    r.total_out[...] = total.astype(BF16)
    for d in range(NZ - 1, 0, -1):
        launch_if(
            z + d < NZ,
            lambda d=d: remote(
                r.total_out, r.total_in.at[z], r.total_s.at[d], r.total_r.at[d], on_z(d)
            ),
        )
    z_wait(1)
    z_step(2)
    decay = jnp.where(gap >= 0, jnp.exp(-own_rate * jnp.maximum(gap, 0.0)), 0.0)
    for d in (0, 1, 3, 2):
        if d:
            block_wait(2, d)
        i = ring_y(-d)
        scores = nt_dot(r.query_in[i], r.key_in[i])
        r.intra[i] = dot((scores * decay).astype(BF16), r.value_in[i])
    r.entry[...] = jnp.zeros_like(r.entry)
    for d in range(1, NZ):

        @pl.when(z >= d)
        def _(d=d):
            await_copy(r.total_in.at[ring_z(-d)], r.total_s.at[d], r.total_r.at[d], on_z(d))
            r.entry[...] += power(4 * (d - 1)) * r.total_in[ring_z(-d)].astype(F32)

    incoming = r.entry[...]
    fade = jnp.exp(-own_rate * (position + 1.0))
    for i in range(NY):
        mixed = r.intra[i] + fade * dot(r.query_in[i], incoming.astype(BF16))
        incoming = power(1) * incoming + r.local[i]
        mean = jnp.mean(mixed * mixed, axis=-1, keepdims=True)
        out = (mixed * lax.rsqrt(mean + EPSILON)).astype(BF16)
        r.heads[y, i] = out.reshape(4, 2, 16, 128)
    for d in (2, 1, 3):
        launch(remote(r.heads.at[y], r.heads.at[y], r.heads_s.at[d], r.heads_r.at[d], on_y(d)))
    z_wait(2)
    z_step(3)

    def heads_wait(d):
        await_copy(r.heads.at[ring_y(-d)], r.heads_s.at[d], r.heads_r.at[d], on_y(d))

    z_wait(3)
    z_step(4)
    swap((2,), range(6))
    heads_wait(1)
    heads_wait(3)
    heads_wait(2)
    swap((0, 1), (2, 3, 4))
    z_wait(4)

    def project(which, n):
        lhs = jnp.concatenate([r.heads[h, :, :, which].reshape(256, 128) for h in range(4)], axis=1)
        rhs = r.proj[4 * n : 4 * (n + 1)].reshape(384, 512)
        return nt_dot(lhs, rhs).reshape(4, 4, 16, 384)

    pair_copies = []
    for n in range(2):
        r.pair_out[n] = project(1 - c, n).astype(BF16)
        pair_copies.append(
            remote(r.pair_out.at[n], r.pair_in.at[n], r.pair_s.at[n], r.pair_r.at[n], partner)
        )
        launch(pair_copies[n])
    for n in range(2):
        r.part[n] = project(c, n)
    for n in range(2):
        pair_copies[n].wait_recv()
        both = r.part[n] + r.pair_in[n].astype(F32)
        r.part[n] = both
        r.part_out[n] = both.astype(BF16)
        for d in (2, 1, 3):
            launch(
                remote(
                    r.part_out.at[n, :, ring_x(d)],
                    r.part_in.at[n, x],
                    r.part_s.at[n, d],
                    r.part_r.at[n, d],
                    on_x(d),
                )
            )
    pass_on((0, 1), (0, 1))
    for n in range(2):
        slab = r.part[n, :, x]
        for d in (1, 3, 2):
            await_copy(r.part_in.at[n, ring_x(-d)], r.part_s.at[n, d], r.part_r.at[n, d], on_x(d))
            slab = slab + r.part_in[n, ring_x(-d)].astype(F32)
        r.slab[n] = slab
        r.slab_out[n] = slab.astype(BF16)
        for d in (2, 1, 3):
            launch(
                remote(
                    r.slab_out.at[n, ring_y(d)],
                    r.slab_in.at[n, y],
                    r.slab_s.at[n, d],
                    r.slab_r.at[n, d],
                    on_y(d),
                )
            )
    for n in range(2):
        for d in (1, 3, 2):
            await_copy(r.slab_in.at[n, ring_y(-d)], r.slab_s.at[n, d], r.slab_r.at[n, d], on_y(d))
            r.slab[n, ring_y(-d)] = r.slab_in[n, ring_y(-d)].astype(F32)
    swap((0, 1), (5,))
    attended = jnp.concatenate(
        [
            r.slab[zz // 4, yy][:, SHARD * (zz % 4) : SHARD * (zz % 4 + 1)]
            for zz in range(NZ)
            for yy in range(NY)
        ],
        axis=1,
    )
    hidden = r.stream[...].astype(F32) + attended
    r.hidden[...] = hidden
    mean = jnp.mean(hidden * hidden, axis=-1, keepdims=True)
    r.tokens[x, c] = (hidden * lax.rsqrt(mean + EPSILON) * r.gain[...]).astype(BF16)
    square = lax.broadcasted_iota(jnp.int32, (16, 16), 0) == lax.broadcasted_iota(
        jnp.int32, (16, 16), 1
    )

    def upright(row):
        wide = jnp.where(square, jnp.broadcast_to(row, (16, 16)).astype(F32), 0.0)
        return jnp.sum(wide, axis=1, keepdims=True)

    table_lane = lax.broadcasted_iota(jnp.int32, (16, 128), 1)
    r.tables[x, c] = jnp.where(
        table_lane == 0, upright(r.routes[0:1, :]), upright(r.routes[1:2, :])
    ).astype(jnp.int32)

    for d in (2, 1, 3, 0):
        for n, ref in enumerate((r.tokens, r.tables)):

            def make(d=d, n=n, ref=ref):
                block = ref.at[x, c]
                device = at(z, y, ring_x(d), core)
                return remote(block, block, r.tok_s.at[n, d], r.tok_r.at[n, d, c], device)

            if d:
                launch(make())
            else:
                launch_if(jnp.logical_not(source), make)

    pass_on((0, 1), (2, 3, 4))

    near = zl // 2
    edge = (zl * zl - 3 * zl + 2) // 2
    cross_to = at(lax.rem(4 * half + 7 - 3 * near, NZ), y, x, c)

    def lanes_of(ref, q):
        return ref.at[:, pl.ds(768 * q, 768)]

    def cross_copy(t, q):
        return remote(
            lanes_of(r.cross.at[t], q),
            lanes_of(r.line.at[t, 3 - near], q),
            r.cross_s.at[t, q],
            r.line_r.at[t, 3 - near, q],
            cross_to,
        )

    low_lane = lax.broadcasted_iota(jnp.int32, (128, CHUNK), 1) < SLOTS

    def expert_of(rel, t):
        return x * 4 + t * 2 + (half if rel == 0 else 1 - half)

    @pl.when(source)
    def _():
        for d in (0, 1, 3, 2):
            for n, ref in enumerate((r.tokens, r.tables)):
                for other in range(2):
                    if d == 0 and other == 1:
                        continue
                    cc = 1 - c if d == 0 else other
                    block = ref.at[ring_x(-d), cc]
                    await_copy(block, r.tok_s.at[n, d], r.tok_r.at[n, d, cc], on_x(d))
        rows = r.tokens[...].reshape(128, DM)
        table = r.tables[...].reshape(128, 128)
        first, second = table[:, 0:1], table[:, 1:2]
        lanes = lax.broadcasted_iota(jnp.int32, (128, 128), 1)
        earlier = (lanes < lax.broadcasted_iota(jnp.int32, (128, 128), 0)).astype(BF16)
        pairs = [(1, 0), (1, 1), (0, 0), (0, 1)]
        hits = []
        for rel, t in pairs:
            expert = expert_of(rel, t)
            hits.append(jnp.where(jnp.logical_or(first == expert, second == expert), 1.0, 0.0))
        wide = jnp.zeros((128, 128), F32)
        for n, hit in enumerate(hits):
            wide = jnp.where(lanes == n, hit, wide)
        ranks = dot(earlier, wide.astype(BF16)).astype(jnp.int32)
        slot = lax.broadcasted_iota(jnp.int32, (128, CHUNK), 1)
        lows, highs = [], []
        for n, (rel, t) in enumerate(pairs):
            rank = ranks[:, n : n + 1]
            low = jnp.where(slot == rank, hits[n], 0.0)
            low = jnp.where(low_lane, low, 0.0).astype(BF16)
            high = jnp.where(slot - SLOTS == rank, hits[n], 0.0).astype(BF16)
            r.sel[rel, t, 0] = low
            r.sel[rel, t, 1] = high
            lows.append(low)
            highs.append(high)
        for n in range(2):
            low = jnp.concatenate(lows[2 * n : 2 * n + 2], axis=1)
            high = jnp.concatenate(highs[2 * n : 2 * n + 2], axis=1)
            both = (tn_dot(low, rows[:, :HALF]) + tn_dot(high, rows[:, HALF:])).astype(BF16)
            for t in range(2):
                chunk = both[CHUNK * t : CHUNK * (t + 1)]
                if n == 0:
                    r.cross[t] = chunk
                    for q in range(2):
                        cross_copy(t, q).start()
                else:
                    r.line[t, near] = chunk

    order = [
        near,
        edge * (2 + near) + (1 - edge) * (1 - near),
        edge * (1 - near) + (1 - edge) * (2 + near),
        3 - near,
    ]

    def origin(s):
        outer = s // 2
        return (1 - outer) * (c + 2 * s) + outer * (5 * s - 11)

    def spread(i):
        s = order[i]
        o = origin(s)
        for t in range(2):
            block = r.line.at[t, s]
            for q in range(2):
                piece = lanes_of(block, q)
                if i > 0:
                    await_copy(piece, r.line_s.at[0, t, s, q], r.line_r.at[t, s, q], on_z(1))
                else:

                    @pl.when(jnp.logical_not(source))
                    def _(t=t, q=q, piece=piece):
                        await_copy(piece, r.line_s.at[0, t, s, q], r.line_r.at[t, s, q], on_z(1))

                for side, condition in (
                    (0, jnp.logical_and(o <= zl, zl < 3)),
                    (1, jnp.logical_and(o >= zl, zl > 0)),
                ):
                    launch_if(
                        condition,
                        lambda piece=piece, t=t, s=s, q=q, side=side: remote(
                            piece,
                            piece,
                            r.line_s.at[side, t, s, q],
                            r.line_r.at[t, s, q],
                            on_z(-1 if side else 1),
                        ),
                    )
            for j, d, wanted in ((0, 2, role == t), (1, 1, role != t), (2, -1, role != t)):
                launch_if(
                    wanted,
                    lambda block=block, s=s, j=j, d=d: remote(
                        block, r.got.at[j, s], r.got_s.at[j, s], r.got_r.at[j, s], on_y(d)
                    ),
                )

    spread(0)
    spread(1)
    pass_on((0, 1), (5,))
    pass_on((2,), range(6))
    spread(2)
    spread(3)

    @pl.when(source)
    def _():
        logits = nt_dot(r.tokens[...].reshape(128, DM), r.router[...])
        table = r.tables[...].reshape(128, 128)
        first, second = table[:, 0:1], table[:, 1:2]
        expert = lax.broadcasted_iota(jnp.int32, logits.shape, 1)

        def lifted(chosen):
            logit = jnp.sum(jnp.where(expert == chosen, logits, 0.0), axis=1, keepdims=True)
            return jax.nn.sigmoid(logit)

        lift_first, lift_second = lifted(first), lifted(second)
        both = lift_first + lift_second
        for rel in range(2):
            for t in range(2):
                chosen = expert_of(rel, t)
                share = jnp.where(first == chosen, lift_first / both, 0.0) + jnp.where(
                    second == chosen, lift_second / both, 0.0
                )
                r.share[rel, t] = jnp.broadcast_to(share, (128, 128))

    other, side_end, far_end = 1 - near, 2 + near, 3 - near

    def arrived(p):
        for j, d in ((0, 2), (1, 1), (2, -1)):
            await_copy(r.got.at[j, p], r.got_s.at[j, p], r.got_r.at[j, p], on_y(d))

    def compute(which):
        chunks = []
        for p in which:
            chunks += [r.line[role, p]] + [r.got[j, p] for j in range(3)]
        for n in range(4):
            a, b = chunks[2 * n].astype(F32), chunks[2 * n + 1].astype(F32)
            rows = slice(CHUNK * n, CHUNK * (n + 1))
            r.flat[rows, :HALF] = jnp.concatenate([a[:SLOTS], b[:SLOTS]], axis=0).astype(BF16)
            r.flat[rows, HALF:] = jnp.concatenate([a[SLOTS:], b[SLOTS:]], axis=0).astype(BF16)
        rows = r.flat[...]
        gated = nt_dot(rows, r.gate[...])
        inner = (gated * jax.nn.sigmoid(gated) * nt_dot(rows, r.up[...])).astype(BF16)
        left = dot(inner, r.down[:, :HALF])
        right = dot(inner, r.down[:, HALF:])
        for n, p in enumerate(which):
            for j in range(4):
                rows = slice(SLOTS * (4 * n + j), SLOTS * (4 * n + j + 1))
                r.partial[j, p] = jnp.concatenate([left[rows], right[rows]], axis=0).astype(BF16)

    def give_back(p):
        for j, d in ((0, 2), (1, -1), (2, 1)):
            launch(
                remote(
                    r.partial.at[j + 1, p], r.back.at[j, p], r.back_s.at[j, p], r.back_r.at[j, p], on_y(d)
                )
            )

    arrived(near)
    arrived(other)
    weights_ready()
    compute((near, other))
    give_back(other)
    arrived(side_end)
    arrived(far_end)
    compute((far_end, side_end))
    for p in (far_end, side_end, near):
        give_back(p)

    def collect(p):
        for j, d in ((0, 2), (1, 1), (2, -1)):
            await_copy(r.back.at[j, p], r.back_s.at[j, p], r.back_r.at[j, p], on_y(d))
        r.total[role, p] = r.partial[0, p].astype(F32) + r.back[0, p].astype(F32)
        r.total[1 - role, p] = r.back[1, p].astype(F32) + r.back[2, p].astype(F32)

    ends = (at(lax.rem(4 * half + 4 + c, NZ), y, x, c), at(lax.rem(4 * half + 6 + c, NZ), y, x, c))

    def along(s):
        o = origin(s)
        for t in range(2):
            for q in range(2):
                cols = slice(768 * q, 768 * (q + 1))
                out = lanes_of(r.line_out.at[t, s], q)

                def add_line(side, t=t, q=q, cols=cols):
                    block = lanes_of(r.line_in.at[side, t, s], q)
                    await_copy(block, r.sum_s.at[t, s, q], r.sum_r.at[side, t, s, q], on_z(1))
                    r.total[t, s, :, cols] += r.line_in[side, t, s, :, cols].astype(F32)

                @pl.when(jnp.logical_and(o >= zl, zl > 0))
                def _(add_line=add_line):
                    add_line(0)

                @pl.when(jnp.logical_and(o <= zl, zl < 3))
                def _(add_line=add_line):
                    add_line(1)

                r.line_out[t, s, :, cols] = r.total[t, s, :, cols].astype(BF16)
                for side, wanted, last in ((0, o > zl, zl == 3), (1, o < zl, zl == 0)):
                    launch_if(
                        jnp.logical_and(wanted, jnp.logical_not(last)),
                        lambda out=out, t=t, s=s, q=q, side=side: remote(
                            out,
                            lanes_of(r.line_in.at[side, t, s], q),
                            r.sum_s.at[t, s, q],
                            r.sum_r.at[side, t, s, q],
                            on_z(-1 if side else 1),
                        ),
                    )
                    launch_if(
                        jnp.logical_and(wanted, last),
                        lambda out=out, t=t, s=s, q=q, side=side: remote(
                            out,
                            lanes_of(r.ret.at[t], q),
                            r.sum_s.at[t, s, q],
                            r.ret_r.at[t, q],
                            ends[side],
                        ),
                    )

    for p in (other, far_end, side_end, near):
        collect(p)
        along(p)

    def home_copy(side, d, cc):
        cols = pl.ds(HALF * side, HALF)
        return remote(
            r.home_out.at[ring_x(d), cc, :, cols],
            r.home_in.at[x, :, cols],
            r.home_s.at[side, d, cc],
            r.home_r.at[side, d],
            at(z, y, ring_x(d), cc),
        )

    home_targets = [(d, other) for d in (2, 1, 3) for other in range(2)] + [(0, 1 - c)]

    @pl.when(source)
    def _():
        for side in range(2):
            cols = slice(HALF * side, HALF * (side + 1))
            value = None
            for rel in range(2):
                for t in range(2):
                    if rel == 1 and side == 0:
                        for q in range(2):
                            block = lanes_of(r.ret.at[t], q)
                            await_copy(block, r.sum_s.at[t, 0, q], r.ret_r.at[t, q], ends[0])
                    rows = r.ret[t] if rel else r.line_out[t, near]
                    term = r.share[rel, t][:, 0:1] * dot(r.sel[rel, t, side], rows)
                    value = term if value is None else value + term
            value = value.reshape(4, 2, 16, HALF)
            r.mixed[:, :, :, cols] = value
            r.home_out[:, :, :, cols] = value.astype(BF16)
            for d, cc in home_targets:
                home_copy(side, d, cc).start()
        r.home[...] = r.mixed[x, c]

    def home_wait(d):
        for side in range(2):
            cols = pl.ds(HALF * side, HALF)
            block = r.home_in.at[ring_x(-d), :, cols]
            await_copy(block, r.home_s.at[side, d, c], r.home_r.at[side, d], on_x(d))

    @pl.when(jnp.logical_not(source))
    def _():
        home_wait(0)
        r.home[...] = r.home_in[x].astype(F32)

    result = r.hidden[...] + r.home[...]
    for d in (1, 3, 2):
        home_wait(d)
        result = result + r.home_in[ring_x(-d)].astype(F32)
    r.out[...] = result.astype(BF16)

    @pl.when(source)
    def _():
        for t in range(2):
            for q in range(2):
                cross_copy(t, q).wait_send()
        for side in range(2):
            for d, cc in home_targets:
                home_copy(side, d, cc).wait_send()

    for condition, make in guarded:

        @pl.when(condition)
        def _(make=make):
            make().wait_send()

    for copy in sends:
        copy.wait_send()


VMEM = pl.BlockSpec(memory_space=pltpu.VMEM)
ANY = pl.BlockSpec(memory_space=pl.ANY)


def body(
    stream,
    query,
    key,
    value,
    decay_rate,
    out_weight,
    norm_gain,
    router_weight,
    routes,
    expert_gate,
    expert_up,
    expert_down,
):
    return pl.pallas_call(
        kernel,
        out_shape=jax.ShapeDtypeStruct(stream.shape, BF16),
        in_specs=[VMEM] * 9 + [ANY] * 3,
        out_specs=VMEM,
        scratch_shapes=list(SCRATCH.values()),
        compiler_params=pltpu.CompilerParams(
            collective_id=0, has_side_effects=True, vmem_limit_bytes=56 * 2**20
        ),
        name="whole",
    )(
        stream,
        query,
        key,
        value,
        decay_rate.reshape(1, 4),
        out_weight.T,
        norm_gain.reshape(1, DM),
        routes.T,
        router_weight.T,
        expert_gate.T,
        expert_up.T,
        expert_down,
    )


def solution(mesh):
    placed = (
        P(("ctx", "ep"), None),
        P("ctx", "ep"),
        P("ctx", "ep"),
        P("ctx", "ep"),
        P("ep"),
        P("ep", "ctx"),
        P(),
        P(),
        P(("ctx", "ep"), None),
        P(None, ("ep", "ctx")),
        P(None, ("ep", "ctx")),
        P(("ep", "ctx"), None),
    )
    return jax.shard_map(
        body, mesh=mesh, in_specs=placed, out_specs=P(("ctx", "ep"), None), check_vma=False
    )
```

```python
import jax
import jax.numpy as jnp
from jax import lax
from jax.experimental import pallas as pl
from jax.experimental.pallas import tpu as pltpu
from jax.sharding import PartitionSpec as P

EPSILON = 1e-06
MESH = pl.DeviceIdType.MESH
F32 = jnp.float32
BF16 = jnp.bfloat16
NY = 4
NZ = 8
NX = 4
DM = 3072
HALF = 1536
SLOTS = 24
CHUNK = 48
SHARD = 96
HIDDEN = 288
PIECES = 2
WIDTH = HALF // PIECES
PIECE = 96
PART = 48


def bf(*shape):
    return pltpu.VMEM(shape, BF16)


def fl(*shape):
    return pltpu.VMEM(shape, F32)


def dma(*shape):
    return pltpu.SemaphoreType.DMA(shape)


INPUTS = (
    "stream", "query", "key", "value", "rates", "weight", "gain", "routes", "router",
    "gate_hbm", "up_hbm", "down_hbm", "out",
)
SCRATCH = dict(
    intra=fl(4, 128, 128),
    key_in=bf(4, 128, 128),
    value_in=bf(4, 128, 128),
    query_in=bf(4, 128, 128),
    local=fl(4, 128, 128),
    total_out=bf(128, 128),
    total_in=bf(8, 128, 128),
    entry=fl(128, 128),
    proj=bf(8, SHARD, 512),
    heads=bf(4, 4, 4, 2, 16, 128),
    pair_out=bf(2, 4, 4, 16, 384),
    pair_in=bf(2, 4, 4, 16, 384),
    part=fl(2, 4, 4, 16, 384),
    part_out=bf(2, 4, 4, 16, 384),
    part_in=bf(2, 4, 4, 16, 384),
    slab=fl(2, 4, 16, 384),
    slab_out=bf(2, 4, 16, 384),
    slab_in=bf(2, 4, 16, 384),
    hidden=fl(16, DM),
    tokens=bf(8, 16, DM),
    tables=pltpu.VMEM((8, 16, 128), jnp.int32),
    gate=bf(2 * HIDDEN, DM),
    up=bf(2 * HIDDEN, DM),
    down=bf(2 * HIDDEN, DM),
    sel=bf(2, 2, 2, 128, CHUNK),
    share=fl(2, 2, 128, 128),
    cross=bf(2, CHUNK, HALF),
    line=bf(2, 4, CHUNK, HALF),
    got=bf(3, 4, CHUNK, HALF),
    flat=bf(192, DM),
    partial=bf(4, 4, CHUNK, HALF),
    back=bf(3, 4, CHUNK, HALF),
    total=fl(2, 4, CHUNK, HALF),
    line_out=bf(2, 4, CHUNK, HALF),
    line_in=bf(2, 2, 4, CHUNK, HALF),
    ret=bf(2, CHUNK, HALF),
    mixed=fl(4, 2, 16, DM),
    home_out=bf(4, 2, 16, DM),
    home_in=bf(4, 16, DM),
    home=fl(16, DM),
    early_s=dma(1), slab_s=dma(1), tok_s=dma(4), total_s=dma(1), own_s=dma(2),
    swap_s=dma(2), pass_s=dma(2), cross_s=dma(1), line_s=dma(1), row_s=dma(1), sum_s=dma(1),
    home_s=dma(1),
    block_r=dma(4), total_r=dma(1), proj_r=dma(4), heads_r=dma(1), pair_r=dma(2), part_r=dma(2),
    slab_r=dma(1), tok_r=dma(2), own_r=dma(2), swap_r=dma(4), pass_r=dma(2),
    line_r=dma(2, 4, PIECES), got_r=dma(4), back_r=dma(4), sum_r=dma(2, 5, PIECES), ret_r=dma(1),
    home_r=dma(2),
)


class Refs:
    def __init__(self, refs):
        for name, ref in zip(INPUTS + tuple(SCRATCH), refs, strict=True):
            setattr(self, name, ref)


def at(z, y, x, c):
    return (z * NY + y, x * 2 + c)


def remote(src, dst, send, recv, device):
    return pltpu.make_async_remote_copy(
        src_ref=src,
        dst_ref=dst,
        send_sem=send,
        recv_sem=recv,
        device_id=device,
        device_id_type=MESH,
    )


def await_bytes(ref, semaphore):
    pltpu.make_async_copy(ref, ref, semaphore).wait()


def greet(barrier, devices):
    for device in devices:
        pl.semaphore_signal(barrier, inc=1, device_id=device, device_id_type=MESH)


def nt_dot(a, b):
    return lax.dot_general(a, b, (((1,), (1,)), ((), ())), preferred_element_type=F32)


def tn_dot(a, b):
    return lax.dot_general(a, b, (((0,), (0,)), ((), ())), preferred_element_type=F32)


def dot(a, b):
    return jnp.dot(a, b, preferred_element_type=F32)


def kernel(*refs):
    r = Refs(refs)
    ctx = lax.axis_index("ctx")
    ep = lax.axis_index("ep")
    z, y, x, c = ctx // NY, ctx % NY, ep // 2, ep % 2
    half, zl = z // 4, z % 4
    role = (y + z) % 2
    source = z % 2 == c
    keeper = c == role
    core = z % 2

    def ring_y(d):
        return lax.rem(y + d + NY, NY)

    def ring_z(d):
        return lax.rem(z + d + NZ, NZ)

    def ring_x(d):
        return lax.rem(x + d + NX, NX)

    def on_y(d):
        return at(z, ring_y(d), x, c)

    def on_z(d):
        return at(ring_z(d), y, x, c)

    def on_x(d):
        return at(z, y, ring_x(d), c)

    partner = at(z, y, x, 1 - c)
    beside = z + 1 - 2 * (z % 2)
    swap_to = (
        at(z, ring_y(1), x, 1 - c),
        at(z, ring_y(-1), x, 1 - c),
        at(beside, y, x, 1 - c),
    )
    barrier = pltpu.get_barrier_semaphore()
    greet(barrier, [on_y(d) for d in range(1, NY)])
    greet(barrier, [on_z(d) for d in range(1, NZ)])
    greet(barrier, [on_x(d) for d in range(1, NX)])
    greet(barrier, [at(z, y, ring_x(d), 1 - c) for d in range(NX)])
    greet(barrier, swap_to)

    def launch(copy):
        copy.start()

    def launch_if(condition, make):
        @pl.when(condition)
        def _():
            make().start()

    def units(n):
        return r.gate.at[pl.ds(0, 16 * n)]

    experts = ((r.gate_hbm, r.gate), (r.up_hbm, r.up), (r.down_hbm, r.down))
    own_rows = pl.ds(0, HIDDEN)

    def part_rows(base, k, side):
        return pl.ds(base + side * PIECE + k * PART, PART)

    def load(m):
        hbm, ref = experts[m]
        return pltpu.make_async_copy(hbm, ref.at[own_rows], r.own_r.at[m // 2])

    @pl.when(keeper)
    def _():
        for m in range(3):
            load(m).start()

    away = jnp.logical_not(keeper)
    batches = (((0, 1), (0, 1)), ((0, 1), (2, 3, 4)), ((0, 1), (5,)), ((2,), range(6)))

    def parts(batch):
        sides, numbers = batches[batch]
        return [(number // 2, number % 2, side) for number in numbers for side in sides]

    def swap(batch, numbers=range(6)):
        for m, k, side in parts(batch):
            if m * 2 + k in numbers:
                launch_if(
                    away,
                    lambda m=m, k=k, side=side: remote(
                        experts[m][0].at[part_rows(0, k, side)],
                        experts[m][1].at[part_rows(HIDDEN, k, side)],
                        r.swap_s.at[side // 2],
                        r.swap_r.at[batch],
                        swap_to[side],
                    ),
                )

    def pass_on(batch):
        @pl.when(away)
        def _():
            await_bytes(units(3 * len(parts(batch))), r.swap_r.at[batch])
            for m, k, side in parts(batch):
                ref = experts[m][1].at[part_rows(HIDDEN, k, side)]
                remote(ref, ref, r.pass_s.at[side // 2], r.pass_r.at[side // 2], partner).start()

    def weights_ready():
        await_bytes(r.gate, r.own_r.at[0])
        await_bytes(r.gate.at[own_rows], r.own_r.at[1])

        @pl.when(keeper)
        def _():
            await_bytes(r.gate, r.pass_r.at[0])
            await_bytes(r.gate.at[own_rows], r.pass_r.at[1])

    rates = r.rates[...]
    length = r.query.shape[0]
    gap = (
        lax.broadcasted_iota(jnp.int32, (length, length), 0)
        - lax.broadcasted_iota(jnp.int32, (length, length), 1)
    ).astype(F32)
    position = lax.broadcasted_iota(jnp.int32, (length, 1), 0).astype(F32)
    lane = lax.broadcasted_iota(jnp.int32, rates.shape, 1)
    own_rate = jnp.sum(jnp.where(lane == y, rates, 0.0), axis=1, keepdims=True)

    def power(n):
        return jnp.exp(-own_rate * (128.0 * n))

    def head_columns(h):
        return pl.ds(pl.multiple_of(h * 128, 128), 128)

    blocks = ((r.key, r.key_in), (r.value, r.value_in), (r.query, r.query_in))
    for whole, own in blocks:
        own[y] = whole[:, head_columns(y)]
    r.proj[z] = r.weight[...]
    pl.semaphore_wait(barrier, NY - 1 + NZ - 1 + NX - 1 + NX + 3)

    for n, (whole, own) in enumerate(blocks):
        for d in (2, 1, 3):
            launch(
                remote(
                    whole.at[:, head_columns(ring_y(d))],
                    own.at[y],
                    r.early_s.at[0],
                    r.block_r.at[0 if n == 2 else d],
                    on_y(d),
                )
            )

    def z_parts(k):
        if k < 4:
            return r.proj.at[ring_z(1 - k)], r.proj.at[ring_z(k - 1)]
        return r.proj.at[ring_z(-3)].at[pl.ds(0, 48)], r.proj.at[ring_z(3)].at[pl.ds(48, 48)]

    def z_step(k):
        a, b = z_parts(k)
        launch(remote(a, a, r.early_s.at[0], r.proj_r.at[k - 1], on_z(1)))
        launch(remote(b, b, r.early_s.at[0], r.proj_r.at[k - 1], on_z(-1)))

    def z_wait(k):
        await_bytes(r.proj.at[pl.ds(0, 2 if k < 4 else 1)], r.proj_r.at[k - 1])

    z_step(1)
    swap(0, (0,))
    for m in range(3):
        launch_if(
            keeper,
            lambda m=m: remote(
                experts[m][0], experts[m][1].at[own_rows], r.own_s.at[m // 2], r.own_r.at[m // 2], partner
            ),
        )

    fade = jnp.exp(-own_rate * (length - 1.0 - position))
    for d in (0, 1, 3, 2):
        if d:
            await_bytes(r.key_in.at[pl.ds(0, 2)], r.block_r.at[d])
        i = ring_y(-d)
        faded = (r.key_in[i].astype(F32) * fade).astype(BF16)
        r.local[i] = tn_dot(faded, r.value_in[i])
    swap(0, (1,))
    total = r.local[3]
    for i in range(3):
        total = total + power(3 - i) * r.local[i]
    r.total_out[...] = total.astype(BF16)
    for d in range(NZ - 1, 0, -1):
        launch_if(
            z + d < NZ,
            lambda d=d: remote(
                r.total_out, r.total_in.at[z], r.total_s.at[0], r.total_r.at[0], on_z(d)
            ),
        )
    z_wait(1)
    z_step(2)
    decay = jnp.where(gap >= 0, jnp.exp(-own_rate * jnp.maximum(gap, 0.0)), 0.0)
    await_bytes(r.key_in.at[pl.ds(0, 3)], r.block_r.at[0])
    for i in range(NY):
        scores = nt_dot(r.query_in[i], r.key_in[i])
        r.intra[i] = dot((scores * decay).astype(BF16), r.value_in[i])
    r.entry[...] = jnp.zeros_like(r.entry)
    for d in range(1, NZ):

        @pl.when(z == d)
        def _(d=d):
            await_bytes(r.total_in.at[pl.ds(0, d)], r.total_r.at[0])

    for d in range(1, NZ):

        @pl.when(z >= d)
        def _(d=d):
            r.entry[...] += power(4 * (d - 1)) * r.total_in[ring_z(-d)].astype(F32)

    incoming = r.entry[...]
    fade = jnp.exp(-own_rate * (position + 1.0))
    for i in range(NY):
        mixed = r.intra[i] + fade * dot(r.query_in[i], incoming.astype(BF16))
        incoming = power(1) * incoming + r.local[i]
        mean = jnp.mean(mixed * mixed, axis=-1, keepdims=True)
        out = (mixed * lax.rsqrt(mean + EPSILON)).astype(BF16)
        r.heads[y, i] = out.reshape(4, 2, 16, 128)
    for d in (2, 1, 3):
        launch(remote(r.heads.at[y], r.heads.at[y], r.early_s.at[0], r.heads_r.at[0], on_y(d)))
    z_wait(2)
    z_step(3)

    z_wait(3)
    z_step(4)
    swap(3)
    await_bytes(r.heads.at[pl.ds(0, 3)], r.heads_r.at[0])
    swap(1)
    z_wait(4)

    def project(which, n):
        lhs = jnp.concatenate([r.heads[h, :, :, which].reshape(256, 128) for h in range(4)], axis=1)
        rhs = r.proj[4 * n : 4 * (n + 1)].reshape(384, 512)
        return nt_dot(lhs, rhs).reshape(4, 4, 16, 384)

    for n in range(2):
        r.pair_out[n] = project(1 - c, n).astype(BF16)
        launch(remote(r.pair_out.at[n], r.pair_in.at[n], r.early_s.at[0], r.pair_r.at[n], partner))
    for n in range(2):
        r.part[n] = project(c, n)
    for n in range(2):
        await_bytes(r.pair_in.at[n], r.pair_r.at[n])
        both = r.part[n] + r.pair_in[n].astype(F32)
        r.part[n] = both
        r.part_out[n] = both.astype(BF16)
        for d in (2, 1, 3):
            launch(
                remote(
                    r.part_out.at[n, :, ring_x(d)],
                    r.part_in.at[n, x],
                    r.early_s.at[0],
                    r.part_r.at[n],
                    on_x(d),
                )
            )
    pass_on(0)
    for n in range(2):
        slab = r.part[n, :, x]
        await_bytes(r.part_in.at[n, pl.ds(0, 3)], r.part_r.at[n])
        for d in (1, 3, 2):
            slab = slab + r.part_in[n, ring_x(-d)].astype(F32)
        r.slab[n] = slab
        r.slab_out[n] = slab.astype(BF16)
        for d in (2, 1, 3):
            launch(
                remote(
                    r.slab_out.at[n, ring_y(d)],
                    r.slab_in.at[n, y],
                    r.slab_s.at[0],
                    r.slab_r.at[0],
                    on_y(d),
                )
            )
    await_bytes(r.slab_in.at[:, pl.ds(0, 3)], r.slab_r.at[0])
    for n in range(2):
        for d in (1, 3, 2):
            r.slab[n, ring_y(-d)] = r.slab_in[n, ring_y(-d)].astype(F32)
    swap(2)
    attended = jnp.concatenate(
        [
            r.slab[zz // 4, yy][:, SHARD * (zz % 4) : SHARD * (zz % 4 + 1)]
            for zz in range(NZ)
            for yy in range(NY)
        ],
        axis=1,
    )
    hidden = r.stream[...].astype(F32) + attended
    r.hidden[...] = hidden
    mean = jnp.mean(hidden * hidden, axis=-1, keepdims=True)
    r.tokens[ep] = (hidden * lax.rsqrt(mean + EPSILON) * r.gain[...]).astype(BF16)
    square = lax.broadcasted_iota(jnp.int32, (16, 16), 0) == lax.broadcasted_iota(
        jnp.int32, (16, 16), 1
    )

    def upright(row):
        wide = jnp.where(square, jnp.broadcast_to(row, (16, 16)).astype(F32), 0.0)
        return jnp.sum(wide, axis=1, keepdims=True)

    table_lane = lax.broadcasted_iota(jnp.int32, (16, 128), 1)
    r.tables[ep] = jnp.where(
        table_lane == 0, upright(r.routes[0:1, :]), upright(r.routes[1:2, :])
    ).astype(jnp.int32)

    for d in (2, 1, 3, 0):
        for n, ref in enumerate((r.tokens, r.tables)):

            def make(d=d, n=n, ref=ref):
                block = ref.at[ep]
                device = at(z, y, ring_x(d), core)
                return remote(block, block, r.tok_s.at[n if d else n + 2], r.tok_r.at[n], device)

            if d:
                launch(make())
            else:
                launch_if(jnp.logical_not(source), make)

    pass_on(1)

    near = zl // 2
    edge = (zl * zl - 3 * zl + 2) // 2
    cross_to = at(lax.rem(4 * half + 7 - 3 * near, NZ), y, x, c)

    def lanes_of(ref, q):
        return ref.at[:, pl.ds(WIDTH * q, WIDTH)]

    def cross_copy(t, q):
        return remote(
            lanes_of(r.cross.at[t], q),
            lanes_of(r.line.at[t, 3 - near], q),
            r.cross_s.at[0],
            r.line_r.at[t, 3 - near, q],
            cross_to,
        )

    low_lane = lax.broadcasted_iota(jnp.int32, (128, CHUNK), 1) < SLOTS

    def expert_of(rel, t):
        return x * 4 + t * 2 + (half if rel == 0 else 1 - half)

    @pl.when(source)
    def _():
        for n, ref in enumerate((r.tokens, r.tables)):
            await_bytes(ref.at[pl.ds(0, 7)], r.tok_r.at[n])
        rows = r.tokens[...].reshape(128, DM)
        table = r.tables[...].reshape(128, 128)
        first, second = table[:, 0:1], table[:, 1:2]
        lanes = lax.broadcasted_iota(jnp.int32, (128, 128), 1)
        earlier = (lanes < lax.broadcasted_iota(jnp.int32, (128, 128), 0)).astype(BF16)
        pairs = [(1, 0), (1, 1), (0, 0), (0, 1)]
        hits = []
        for rel, t in pairs:
            expert = expert_of(rel, t)
            hits.append(jnp.where(jnp.logical_or(first == expert, second == expert), 1.0, 0.0))
        wide = jnp.zeros((128, 128), F32)
        for n, hit in enumerate(hits):
            wide = jnp.where(lanes == n, hit, wide)
        ranks = dot(earlier, wide.astype(BF16)).astype(jnp.int32)
        slot = lax.broadcasted_iota(jnp.int32, (128, CHUNK), 1)
        lows, highs = [], []
        for n, (rel, t) in enumerate(pairs):
            rank = ranks[:, n : n + 1]
            low = jnp.where(slot == rank, hits[n], 0.0)
            low = jnp.where(low_lane, low, 0.0).astype(BF16)
            high = jnp.where(slot - SLOTS == rank, hits[n], 0.0).astype(BF16)
            r.sel[rel, t, 0] = low
            r.sel[rel, t, 1] = high
            lows.append(low)
            highs.append(high)
        for n in range(2):
            low = jnp.concatenate(lows[2 * n : 2 * n + 2], axis=1)
            high = jnp.concatenate(highs[2 * n : 2 * n + 2], axis=1)
            both = (tn_dot(low, rows[:, :HALF]) + tn_dot(high, rows[:, HALF:])).astype(BF16)
            for t in range(2):
                chunk = both[CHUNK * t : CHUNK * (t + 1)]
                if n == 0:
                    r.cross[t] = chunk
                    for q in range(PIECES):
                        cross_copy(t, q).start()
                else:
                    r.line[t, near] = chunk

    order = [
        near,
        edge * (2 + near) + (1 - edge) * (1 - near),
        edge * (1 - near) + (1 - edge) * (2 + near),
        3 - near,
    ]

    def origin(s):
        outer = s // 2
        return (1 - outer) * (c + 2 * s) + outer * (5 * s - 11)

    def spread(i):
        s = order[i]
        o = origin(s)
        for t in range(2):
            block = r.line.at[t, s]
            for q in range(PIECES):
                piece = lanes_of(block, q)
                if i > 0:
                    await_bytes(piece, r.line_r.at[t, s, q])
                else:

                    @pl.when(jnp.logical_not(source))
                    def _(t=t, q=q, piece=piece):
                        await_bytes(piece, r.line_r.at[t, s, q])

                for side, condition in (
                    (0, jnp.logical_and(o <= zl, zl < 3)),
                    (1, jnp.logical_and(o >= zl, zl > 0)),
                ):
                    launch_if(
                        condition,
                        lambda piece=piece, t=t, s=s, q=q, side=side: remote(
                            piece,
                            piece,
                            r.line_s.at[0],
                            r.line_r.at[t, s, q],
                            on_z(-1 if side else 1),
                        ),
                    )
            for j, d, wanted in ((0, 2, role == t), (1, 1, role != t), (2, -1, role != t)):
                launch_if(
                    wanted,
                    lambda block=block, s=s, j=j, d=d: remote(
                        block, r.got.at[j, s], r.row_s.at[0], r.got_r.at[s], on_y(d)
                    ),
                )

    spread(0)
    spread(1)
    pass_on(2)
    pass_on(3)
    spread(2)
    spread(3)

    @pl.when(source)
    def _():
        logits = nt_dot(r.tokens[...].reshape(128, DM), r.router[...])
        table = r.tables[...].reshape(128, 128)
        first, second = table[:, 0:1], table[:, 1:2]
        expert = lax.broadcasted_iota(jnp.int32, logits.shape, 1)

        def lifted(chosen):
            logit = jnp.sum(jnp.where(expert == chosen, logits, 0.0), axis=1, keepdims=True)
            return jax.nn.sigmoid(logit)

        lift_first, lift_second = lifted(first), lifted(second)
        both = lift_first + lift_second
        for rel in range(2):
            for t in range(2):
                chosen = expert_of(rel, t)
                share = jnp.where(first == chosen, lift_first / both, 0.0) + jnp.where(
                    second == chosen, lift_second / both, 0.0
                )
                r.share[rel, t] = jnp.broadcast_to(share, (128, 128))

    other, side_end, far_end = 1 - near, 2 + near, 3 - near
    swapped = edge * (core - c) * (core - c)
    third = side_end + swapped * (near - side_end)
    fourth = near + swapped * (side_end - near)

    def arrived(p):
        await_bytes(r.got.at[:, p], r.got_r.at[p])

    def flatten(p, place):
        chunks = [r.line[role, p]] + [r.got[j, p] for j in range(3)]
        for n in range(2):
            a, b = chunks[2 * n].astype(F32), chunks[2 * n + 1].astype(F32)
            rows = slice(CHUNK * (2 * place + n), CHUNK * (2 * place + n + 1))
            r.flat[rows, :HALF] = jnp.concatenate([a[:SLOTS], b[:SLOTS]], axis=0).astype(BF16)
            r.flat[rows, HALF:] = jnp.concatenate([a[SLOTS:], b[SLOTS:]], axis=0).astype(BF16)

    def compute(which):
        rows = r.flat[...]
        gated = nt_dot(rows, r.gate[...])
        inner = (gated * jax.nn.sigmoid(gated) * nt_dot(rows, r.up[...])).astype(BF16)
        left = dot(inner, r.down[:, :HALF])
        right = dot(inner, r.down[:, HALF:])
        for n, p in enumerate(which):
            for j in range(4):
                rows = slice(SLOTS * (4 * n + j), SLOTS * (4 * n + j + 1))
                r.partial[j, p] = jnp.concatenate([left[rows], right[rows]], axis=0).astype(BF16)

    def give_back(p):
        for j, d in ((0, 2), (1, -1), (2, 1)):
            launch(
                remote(
                    r.partial.at[j + 1, p], r.back.at[j, p], r.row_s.at[0], r.back_r.at[p], on_y(d)
                )
            )

    arrived(near)
    flatten(near, 0)
    weights_ready()
    arrived(other)
    flatten(other, 1)
    compute((near, other))
    give_back(other)
    arrived(side_end)
    flatten(side_end, 1)
    arrived(far_end)
    flatten(far_end, 0)
    compute((far_end, side_end))
    for p in (far_end, third, fourth):
        give_back(p)

    def collect(p):
        await_bytes(r.back.at[:, p], r.back_r.at[p])
        r.total[role, p] = r.partial[0, p].astype(F32) + r.back[0, p].astype(F32)
        r.total[1 - role, p] = r.back[1, p].astype(F32) + r.back[2, p].astype(F32)

    ends = (at(lax.rem(4 * half + 4 + c, NZ), y, x, c), at(lax.rem(4 * half + 6 + c, NZ), y, x, c))

    def stream(s, place, side):
        here = 1 - lax.min(1, (origin(s) - place) * (origin(s) - place))
        return s + here * side * (4 - s)

    def along(s):
        o = origin(s)
        for t in range(2):
            for q in range(PIECES):
                cols = slice(WIDTH * q, WIDTH * (q + 1))
                out = lanes_of(r.line_out.at[t, s], q)

                def add_line(side, t=t, q=q, cols=cols):
                    block = lanes_of(r.line_in.at[side, t, s], q)
                    await_bytes(block, r.sum_r.at[t, stream(s, zl, side), q])
                    r.total[t, s, :, cols] += r.line_in[side, t, s, :, cols].astype(F32)

                @pl.when(jnp.logical_and(o >= zl, zl > 0))
                def _(add_line=add_line):
                    add_line(0)

                @pl.when(jnp.logical_and(o <= zl, zl < 3))
                def _(add_line=add_line):
                    add_line(1)

                r.line_out[t, s, :, cols] = r.total[t, s, :, cols].astype(BF16)
                for side, wanted, last in ((0, o > zl, zl == 3), (1, o < zl, zl == 0)):
                    launch_if(
                        jnp.logical_and(wanted, jnp.logical_not(last)),
                        lambda out=out, t=t, s=s, q=q, side=side: remote(
                            out,
                            lanes_of(r.line_in.at[side, t, s], q),
                            r.sum_s.at[0],
                            r.sum_r.at[t, stream(s, zl + 1 - 2 * side, side), q],
                            on_z(-1 if side else 1),
                        ),
                    )
                    launch_if(
                        jnp.logical_and(wanted, last),
                        lambda out=out, t=t, s=s, q=q, side=side: remote(
                            out,
                            lanes_of(r.ret.at[t], q),
                            r.sum_s.at[0],
                            r.ret_r.at[0],
                            ends[side],
                        ),
                    )

    for p in (other, far_end, third, fourth):
        collect(p)
        along(p)

    def home_copy(side, d, cc):
        cols = pl.ds(HALF * side, HALF)
        return remote(
            r.home_out.at[ring_x(d), cc, :, cols],
            r.home_in.at[x, :, cols],
            r.home_s.at[0],
            r.home_r.at[1 if d else 0],
            at(z, y, ring_x(d), cc),
        )

    home_targets = [(d, other) for d in (2, 1, 3) for other in range(2)] + [(0, 1 - c)]

    @pl.when(source)
    def _():
        for side in range(2):
            cols = slice(HALF * side, HALF * (side + 1))
            value = None
            for rel in range(2):
                for t in range(2):
                    if rel == 1 and side == 0 and t == 0:
                        await_bytes(r.ret, r.ret_r.at[0])
                    rows = r.ret[t] if rel else r.line_out[t, near]
                    term = r.share[rel, t][:, 0:1] * dot(r.sel[rel, t, side], rows)
                    value = term if value is None else value + term
            value = value.reshape(4, 2, 16, HALF)
            r.mixed[:, :, :, cols] = value
            r.home_out[:, :, :, cols] = value.astype(BF16)
            for d, cc in home_targets:
                home_copy(side, d, cc).start()
        r.home[...] = r.mixed[x, c]

    @pl.when(jnp.logical_not(source))
    def _():
        await_bytes(r.home_in.at[0], r.home_r.at[0])
        r.home[...] = r.home_in[x].astype(F32)

    result = r.hidden[...] + r.home[...]
    await_bytes(r.home_in.at[pl.ds(0, 3)], r.home_r.at[1])
    for d in (1, 3, 2):
        result = result + r.home_in[ring_x(-d)].astype(F32)
    r.out[...] = result.astype(BF16)

    await_bytes(units(21), r.early_s.at[0])
    await_bytes(r.slab_out.at[:, pl.ds(0, 3)], r.slab_s.at[0])
    await_bytes(units(36), r.row_s.at[0])
    for n, ref in enumerate((r.tokens, r.tables)):
        await_bytes(ref.at[pl.ds(0, 3)], r.tok_s.at[n])
    for d in range(1, NZ):

        @pl.when(z + d == NZ - 1)
        def _(d=d):
            await_bytes(r.total_in.at[pl.ds(0, d)], r.total_s.at[0])

    @pl.when(keeper)
    def _():
        await_bytes(r.gate, r.own_s.at[0])
        await_bytes(r.gate.at[own_rows], r.own_s.at[1])

    @pl.when(away)
    def _():
        for semaphore in (r.swap_s, r.pass_s):
            await_bytes(r.gate, semaphore.at[0])
            await_bytes(r.gate.at[own_rows], semaphore.at[1])

    @pl.when(source)
    def _():
        await_bytes(units(3), r.cross_s.at[0])
        await_bytes(units(9), r.sum_s.at[0])
        await_bytes(units(7), r.home_s.at[0])

    @pl.when(jnp.logical_not(source))
    def _():
        for n, ref in enumerate((r.tokens, r.tables)):
            await_bytes(ref.at[0], r.tok_s.at[n + 2])
        await_bytes(units(12), r.sum_s.at[0])

    forwards = sum(
        jnp.where(jnp.logical_and(origin(s) <= zl, zl < 3), 1, 0)
        + jnp.where(jnp.logical_and(origin(s) >= zl, zl > 0), 1, 0)
        for s in range(4)
    )
    for n in range(1, 9):

        @pl.when(forwards == n)
        def _(n=n):
            await_bytes(units(3 * n), r.line_s.at[0])


VMEM = pl.BlockSpec(memory_space=pltpu.VMEM)
ANY = pl.BlockSpec(memory_space=pl.ANY)


def body(
    stream,
    query,
    key,
    value,
    decay_rate,
    out_weight,
    norm_gain,
    router_weight,
    routes,
    expert_gate,
    expert_up,
    expert_down,
):
    return pl.pallas_call(
        kernel,
        out_shape=jax.ShapeDtypeStruct(stream.shape, BF16),
        in_specs=[VMEM] * 9 + [ANY] * 3,
        out_specs=VMEM,
        scratch_shapes=list(SCRATCH.values()),
        compiler_params=pltpu.CompilerParams(
            collective_id=0, has_side_effects=True, vmem_limit_bytes=56 * 2**20
        ),
        name="whole",
    )(
        stream,
        query,
        key,
        value,
        decay_rate.reshape(1, 4),
        out_weight.T,
        norm_gain.reshape(1, DM),
        routes.T,
        router_weight.T,
        expert_gate.T,
        expert_up.T,
        expert_down,
    )


def solution(mesh):
    placed = (
        P(("ctx", "ep"), None),
        P("ctx", "ep"),
        P("ctx", "ep"),
        P("ctx", "ep"),
        P("ep"),
        P("ep", "ctx"),
        P(),
        P(),
        P(("ctx", "ep"), None),
        P(None, ("ep", "ctx")),
        P(None, ("ep", "ctx")),
        P(("ep", "ctx"), None),
    )
    return jax.shard_map(
        body, mesh=mesh, in_specs=placed, out_specs=P(("ctx", "ep"), None), check_vma=False
    )
```

```python
import jax
import jax.numpy as jnp
from jax import lax
from jax.experimental import pallas as pl
from jax.experimental.pallas import tpu as pltpu
from jax.sharding import PartitionSpec as P

EPSILON = 1e-06
MESH = pl.DeviceIdType.MESH
F32 = jnp.float32
BF16 = jnp.bfloat16
NY = 4
NZ = 8
NX = 4
DM = 3072
HALF = 1536
SLOTS = 24
CHUNK = 48
SHARD = 96
HIDDEN = 288
PIECES = 4
WIDTH = HALF // PIECES
PIECE = 96
PART = 48
SHARD_ORDER = (0, 1, 7, 2, 6, 3, 5, 4)


def bf(*shape):
    return pltpu.VMEM(shape, BF16)


def fl(*shape):
    return pltpu.VMEM(shape, F32)


def dma(*shape):
    return pltpu.SemaphoreType.DMA(shape)


INPUTS = (
    "stream_hbm", "query", "key", "value", "rates_hbm", "weight", "gain_hbm", "routes_hbm",
    "router_hbm", "gate_hbm", "up_hbm", "down_hbm", "out",
)
SCRATCH = dict(
    stream=bf(16, DM),
    rates=fl(1, 4),
    gain=fl(1, DM),
    routes=pltpu.VMEM((2, 16), jnp.int32),
    router=bf(16, DM),
    intra=fl(4, 128, 128),
    key_in=bf(4, 128, 128),
    value_in=bf(4, 128, 128),
    query_in=bf(4, 128, 128),
    local=fl(4, 128, 128),
    total_out=bf(128, 128),
    total_in=bf(8, 128, 128),
    entry=fl(128, 128),
    proj=bf(8, SHARD, 512),
    heads=bf(4, 4, 4, 2, 16, 128),
    pair_out=bf(2, 4, 4, 16, 384),
    pair_in=bf(2, 4, 4, 16, 384),
    part=fl(2, 4, 4, 16, 384),
    part_out=bf(2, 4, 4, 16, 384),
    part_in=bf(2, 4, 4, 16, 384),
    slab=fl(2, 4, 16, 384),
    slab_out=bf(2, 4, 16, 384),
    slab_in=bf(2, 4, 16, 384),
    hidden=fl(16, DM),
    tokens=bf(8, 16, DM),
    tables=pltpu.VMEM((8, 16, 128), jnp.int32),
    gate=bf(2 * HIDDEN, DM),
    up=bf(2 * HIDDEN, DM),
    down=bf(2 * HIDDEN, DM),
    sel=bf(2, 2, 2, 128, CHUNK),
    share=fl(2, 2, 128, 128),
    cross=bf(2, CHUNK, HALF),
    line=bf(2, 4, CHUNK, HALF),
    got=bf(3, 4, CHUNK, HALF),
    flat=bf(192, DM),
    partial=bf(4, 4, CHUNK, HALF),
    back=bf(3, 4, CHUNK, HALF),
    total=fl(2, 4, CHUNK, HALF),
    line_out=bf(2, 4, CHUNK, HALF),
    line_in=bf(2, 2, 4, CHUNK, HALF),
    ret=bf(2, CHUNK, HALF),
    mixed=fl(4, 2, 16, DM),
    home_out=bf(4, 2, 16, DM),
    home_in=bf(4, 16, DM),
    home=fl(16, DM),
    load_r=dma(6), early_s=dma(1), slab_s=dma(1), tok_s=dma(4), total_s=dma(1), own_s=dma(2),
    swap_s=dma(2), pass_s=dma(2), cross_s=dma(1), line_s=dma(1), row_s=dma(1), sum_s=dma(1),
    home_s=dma(1),
    block_r=dma(4), total_r=dma(1), proj_r=dma(4), heads_r=dma(1), pair_r=dma(2), part_r=dma(2),
    slab_r=dma(1), tok_r=dma(2), own_r=dma(2), swap_r=dma(4), pass_r=dma(2),
    line_r=dma(2, 4, PIECES), got_r=dma(4), back_r=dma(4), sum_r=dma(2, 5, PIECES), ret_r=dma(1),
    home_r=dma(2),
)


class Refs:
    def __init__(self, refs):
        for name, ref in zip(INPUTS + tuple(SCRATCH), refs, strict=True):
            setattr(self, name, ref)


def at(z, y, x, c):
    return (z * NY + y, x * 2 + c)


def remote(src, dst, send, recv, device):
    return pltpu.make_async_remote_copy(
        src_ref=src,
        dst_ref=dst,
        send_sem=send,
        recv_sem=recv,
        device_id=device,
        device_id_type=MESH,
    )


def await_bytes(ref, semaphore):
    pltpu.make_async_copy(ref, ref, semaphore).wait()


def greet(barrier, devices):
    for device in devices:
        pl.semaphore_signal(barrier, inc=1, device_id=device, device_id_type=MESH)


def nt_dot(a, b):
    return lax.dot_general(a, b, (((1,), (1,)), ((), ())), preferred_element_type=F32)


def tn_dot(a, b):
    return lax.dot_general(a, b, (((0,), (0,)), ((), ())), preferred_element_type=F32)


def dot(a, b):
    return jnp.dot(a, b, preferred_element_type=F32)


def kernel(*refs):
    r = Refs(refs)
    ctx = lax.axis_index("ctx")
    ep = lax.axis_index("ep")
    z, y, x, c = ctx // NY, ctx % NY, ep // 2, ep % 2
    half, zl = z // 4, z % 4
    role = (y + z) % 2
    source = z % 2 == c
    keeper = c == role
    core = z % 2

    def ring_y(d):
        return lax.rem(y + d + NY, NY)

    def ring_z(d):
        return lax.rem(z + d + NZ, NZ)

    def ring_x(d):
        return lax.rem(x + d + NX, NX)

    def on_y(d):
        return at(z, ring_y(d), x, c)

    def on_z(d):
        return at(ring_z(d), y, x, c)

    def on_x(d):
        return at(z, y, ring_x(d), c)

    partner = at(z, y, x, 1 - c)
    beside = z + 1 - 2 * (z % 2)
    swap_to = (
        at(z, ring_y(1), x, 1 - c),
        at(z, ring_y(-1), x, 1 - c),
        at(beside, y, x, 1 - c),
    )
    barrier = pltpu.get_barrier_semaphore()
    greet(barrier, [on_y(d) for d in range(1, NY)])
    greet(barrier, [on_z(d) for d in range(1, NZ)])
    greet(barrier, [on_x(d) for d in range(1, NX)])
    greet(barrier, [at(z, y, ring_x(d), 1 - c) for d in range(NX)])
    greet(barrier, swap_to)

    def launch(copy):
        copy.start()

    def launch_if(condition, make):
        @pl.when(condition)
        def _():
            make().start()

    def units(n):
        return r.gate.at[pl.ds(0, 16 * n)]

    experts = ((r.gate_hbm, r.gate), (r.up_hbm, r.up), (r.down_hbm, r.down))
    own_rows = pl.ds(0, HIDDEN)

    def part_rows(base, k, side):
        return pl.ds(base + side * PIECE + k * PART, PART)

    def load(m):
        hbm, ref = experts[m]
        return pltpu.make_async_copy(hbm, ref.at[own_rows], r.own_r.at[m // 2])

    def head_columns(h):
        return pl.ds(pl.multiple_of(h * 128, 128), 128)

    blocks = ((r.key, r.key_in), (r.value, r.value_in), (r.query, r.query_in))
    for whole, own in blocks:
        pltpu.make_async_copy(whole.at[:, head_columns(y)], own.at[y], r.load_r.at[0]).start()
    pltpu.make_async_copy(r.weight, r.proj.at[0], r.load_r.at[0]).start()
    small = (
        (r.rates_hbm, r.rates),
        (r.stream_hbm, r.stream),
        (r.gain_hbm, r.gain),
        (r.routes_hbm, r.routes),
        (r.router_hbm, r.router),
    )
    for n, (hbm, ref) in enumerate(small):
        pltpu.make_async_copy(hbm, ref, r.load_r.at[n + 1]).start()

    @pl.when(keeper)
    def _():
        for m in range(3):
            load(m).start()

    away = jnp.logical_not(keeper)
    batches = (((0, 1), (0, 1)), ((0, 1), (2, 3, 4)), ((0, 1), (5,)), ((2,), range(6)))

    def parts(batch):
        sides, numbers = batches[batch]
        return [(number // 2, number % 2, side) for number in numbers for side in sides]

    def swap(batch, numbers=range(6)):
        for m, k, side in parts(batch):
            if m * 2 + k in numbers:
                launch_if(
                    away,
                    lambda m=m, k=k, side=side: remote(
                        experts[m][0].at[part_rows(0, k, side)],
                        experts[m][1].at[part_rows(HIDDEN, k, side)],
                        r.swap_s.at[side // 2],
                        r.swap_r.at[batch],
                        swap_to[side],
                    ),
                )

    def pass_on(batch):
        @pl.when(away)
        def _():
            await_bytes(units(3 * len(parts(batch))), r.swap_r.at[batch])
            for m, k, side in parts(batch):
                ref = experts[m][1].at[part_rows(HIDDEN, k, side)]
                remote(ref, ref, r.pass_s.at[side // 2], r.pass_r.at[side // 2], partner).start()

    def weights_ready():
        await_bytes(r.gate, r.own_r.at[0])
        await_bytes(r.gate.at[own_rows], r.own_r.at[1])

        @pl.when(keeper)
        def _():
            await_bytes(r.gate, r.pass_r.at[0])
            await_bytes(r.gate.at[own_rows], r.pass_r.at[1])

    pl.semaphore_wait(barrier, NY - 1 + NZ - 1 + NX - 1 + NX + 3)

    for n, (whole, own) in enumerate(blocks):
        for d in (2, 1, 3):
            launch(
                remote(
                    whole.at[:, head_columns(ring_y(d))],
                    own.at[y],
                    r.early_s.at[0],
                    r.block_r.at[0 if n == 2 else d],
                    on_y(d),
                )
            )

    def shard(distance):
        return r.proj.at[SHARD_ORDER.index(distance % NZ)]

    def z_step(k):
        a, b, to_a, to_b = shard(1 - k), shard(k - 1), shard(-k), shard(k)
        if k == 1:
            a = b = r.weight
        if k == 4:
            a, to_a = a.at[pl.ds(0, 48)], to_a.at[pl.ds(0, 48)]
            b, to_b = b.at[pl.ds(48, 48)], to_b.at[pl.ds(48, 48)]
        launch(remote(a, to_a, r.early_s.at[0], r.proj_r.at[k - 1], on_z(1)))
        launch(remote(b, to_b, r.early_s.at[0], r.proj_r.at[k - 1], on_z(-1)))

    def z_wait(k):
        await_bytes(r.proj.at[pl.ds(0, 2 if k < 4 else 1)], r.proj_r.at[k - 1])

    z_step(1)
    swap(0, (0,))
    for m in range(3):
        launch_if(
            keeper,
            lambda m=m: remote(
                experts[m][0], experts[m][1].at[own_rows], r.own_s.at[m // 2], r.own_r.at[m // 2], partner
            ),
        )

    for n, (hbm, ref) in enumerate(small):
        await_bytes(ref, r.load_r.at[n + 1])
    await_bytes(units(2), r.load_r.at[0])
    rates = r.rates[...]
    length = r.query.shape[0]
    gap = (
        lax.broadcasted_iota(jnp.int32, (length, length), 0)
        - lax.broadcasted_iota(jnp.int32, (length, length), 1)
    ).astype(F32)
    position = lax.broadcasted_iota(jnp.int32, (length, 1), 0).astype(F32)
    lane = lax.broadcasted_iota(jnp.int32, rates.shape, 1)
    own_rate = jnp.sum(jnp.where(lane == y, rates, 0.0), axis=1, keepdims=True)

    def power(n):
        return jnp.exp(-own_rate * (128.0 * n))

    fade = jnp.exp(-own_rate * (length - 1.0 - position))
    for d in (0, 1, 3, 2):
        if d:
            await_bytes(r.key_in.at[pl.ds(0, 2)], r.block_r.at[d])
        i = ring_y(-d)
        faded = (r.key_in[i].astype(F32) * fade).astype(BF16)
        r.local[i] = tn_dot(faded, r.value_in[i])
    swap(0, (1,))
    total = r.local[3]
    for i in range(3):
        total = total + power(3 - i) * r.local[i]
    r.total_out[...] = total.astype(BF16)
    for d in range(NZ - 1, 0, -1):
        launch_if(
            z + d < NZ,
            lambda d=d: remote(
                r.total_out, r.total_in.at[z], r.total_s.at[0], r.total_r.at[0], on_z(d)
            ),
        )
    z_wait(1)
    z_step(2)
    decay = jnp.where(gap >= 0, jnp.exp(-own_rate * jnp.maximum(gap, 0.0)), 0.0)
    await_bytes(r.key_in.at[pl.ds(0, 3)], r.block_r.at[0])
    for i in range(NY):
        scores = nt_dot(r.query_in[i], r.key_in[i])
        r.intra[i] = dot((scores * decay).astype(BF16), r.value_in[i])
    r.entry[...] = jnp.zeros_like(r.entry)
    for d in range(1, NZ):

        @pl.when(z == d)
        def _(d=d):
            await_bytes(r.total_in.at[pl.ds(0, d)], r.total_r.at[0])

    for d in range(1, NZ):

        @pl.when(z >= d)
        def _(d=d):
            r.entry[...] += power(4 * (d - 1)) * r.total_in[ring_z(-d)].astype(F32)

    incoming = r.entry[...]
    fade = jnp.exp(-own_rate * (position + 1.0))
    for i in range(NY):
        mixed = r.intra[i] + fade * dot(r.query_in[i], incoming.astype(BF16))
        incoming = power(1) * incoming + r.local[i]
        mean = jnp.mean(mixed * mixed, axis=-1, keepdims=True)
        out = (mixed * lax.rsqrt(mean + EPSILON)).astype(BF16)
        r.heads[y, i] = out.reshape(4, 2, 16, 128)
    for d in (2, 1, 3):
        launch(remote(r.heads.at[y], r.heads.at[y], r.early_s.at[0], r.heads_r.at[0], on_y(d)))
    z_wait(2)
    z_step(3)

    z_wait(3)
    z_step(4)
    swap(3)
    await_bytes(r.heads.at[pl.ds(0, 3)], r.heads_r.at[0])
    swap(1)

    def project(which, n):
        lhs = jnp.concatenate([r.heads[h, :, :, which].reshape(256, 128) for h in range(4)], axis=1)
        rhs = r.proj[4 * n : 4 * (n + 1)].reshape(384, 512)
        return nt_dot(lhs, rhs).reshape(4, 4, 16, 384)

    for n in range(2):
        if n == 1:
            z_wait(4)
        r.pair_out[n] = project(1 - c, n).astype(BF16)
        launch(remote(r.pair_out.at[n], r.pair_in.at[n], r.early_s.at[0], r.pair_r.at[n], partner))
        r.part[n] = project(c, n)
    for n in range(2):
        await_bytes(r.pair_in.at[n], r.pair_r.at[n])
        both = r.part[n] + r.pair_in[n].astype(F32)
        r.part[n] = both
        r.part_out[n] = both.astype(BF16)
        for d in (2, 1, 3):
            launch(
                remote(
                    r.part_out.at[n, :, ring_x(d)],
                    r.part_in.at[n, x],
                    r.early_s.at[0],
                    r.part_r.at[n],
                    on_x(d),
                )
            )
    pass_on(0)
    for n in range(2):
        slab = r.part[n, :, x]
        await_bytes(r.part_in.at[n, pl.ds(0, 3)], r.part_r.at[n])
        for d in (1, 3, 2):
            slab = slab + r.part_in[n, ring_x(-d)].astype(F32)
        r.slab[n] = slab
        r.slab_out[n] = slab.astype(BF16)
        for d in (2, 1, 3):
            launch(
                remote(
                    r.slab_out.at[n, ring_y(d)],
                    r.slab_in.at[n, y],
                    r.slab_s.at[0],
                    r.slab_r.at[0],
                    on_y(d),
                )
            )
    await_bytes(r.slab_in.at[:, pl.ds(0, 3)], r.slab_r.at[0])
    for n in range(2):
        for d in (1, 3, 2):
            r.slab[n, ring_y(-d)] = r.slab_in[n, ring_y(-d)].astype(F32)
    swap(2)
    def columns_of(yy):
        places = [SHARD_ORDER.index(distance) for distance in range(NZ)]
        ordered = [r.slab[p // 4, yy][:, SHARD * (p % 4) : SHARD * (p % 4 + 1)] for p in places]
        return pltpu.roll(jnp.concatenate(ordered, axis=1), z * SHARD, 1)

    quarters = [columns_of(yy) for yy in range(NY)]
    attended = jnp.concatenate(
        [
            quarters[yy][:, SHARD * zz : SHARD * (zz + 1)]
            for zz in range(NZ)
            for yy in range(NY)
        ],
        axis=1,
    )
    hidden = r.stream[...].astype(F32) + attended
    r.hidden[...] = hidden
    mean = jnp.mean(hidden * hidden, axis=-1, keepdims=True)
    r.tokens[ep] = (hidden * lax.rsqrt(mean + EPSILON) * r.gain[...]).astype(BF16)
    square = lax.broadcasted_iota(jnp.int32, (16, 16), 0) == lax.broadcasted_iota(
        jnp.int32, (16, 16), 1
    )

    def upright(row):
        wide = jnp.where(square, jnp.broadcast_to(row, (16, 16)).astype(F32), 0.0)
        return jnp.sum(wide, axis=1, keepdims=True)

    table_lane = lax.broadcasted_iota(jnp.int32, (16, 128), 1)
    r.tables[ep] = jnp.where(
        table_lane == 0, upright(r.routes[0:1, :]), upright(r.routes[1:2, :])
    ).astype(jnp.int32)

    for d in (2, 1, 3, 0):
        for n, ref in enumerate((r.tokens, r.tables)):

            def make(d=d, n=n, ref=ref):
                block = ref.at[ep]
                device = at(z, y, ring_x(d), core)
                return remote(block, block, r.tok_s.at[n if d else n + 2], r.tok_r.at[n], device)

            if d:
                launch(make())
            else:
                launch_if(jnp.logical_not(source), make)

    pass_on(1)

    near = zl // 2
    edge = (zl * zl - 3 * zl + 2) // 2
    cross_to = at(lax.rem(4 * half + 7 - 3 * near, NZ), y, x, c)

    def lanes_of(ref, q):
        return ref.at[:, pl.ds(WIDTH * q, WIDTH)]

    def cross_copy(t, q):
        return remote(
            lanes_of(r.cross.at[t], q),
            lanes_of(r.line.at[t, 3 - near], q),
            r.cross_s.at[0],
            r.line_r.at[t, 3 - near, q],
            cross_to,
        )

    low_lane = lax.broadcasted_iota(jnp.int32, (128, CHUNK), 1) < SLOTS

    def expert_of(rel, t):
        return x * 4 + t * 2 + (half if rel == 0 else 1 - half)

    @pl.when(source)
    def _():
        for n, ref in enumerate((r.tokens, r.tables)):
            await_bytes(ref.at[pl.ds(0, 7)], r.tok_r.at[n])
        rows = r.tokens[...].reshape(128, DM)
        table = r.tables[...].reshape(128, 128)
        first, second = table[:, 0:1], table[:, 1:2]
        lanes = lax.broadcasted_iota(jnp.int32, (128, 128), 1)
        earlier = (lanes < lax.broadcasted_iota(jnp.int32, (128, 128), 0)).astype(BF16)
        pairs = [(1, 0), (1, 1), (0, 0), (0, 1)]
        hits = []
        for rel, t in pairs:
            expert = expert_of(rel, t)
            hits.append(jnp.where(jnp.logical_or(first == expert, second == expert), 1.0, 0.0))
        wide = jnp.zeros((128, 128), F32)
        for n, hit in enumerate(hits):
            wide = jnp.where(lanes == n, hit, wide)
        ranks = dot(earlier, wide.astype(BF16)).astype(jnp.int32)
        slot = lax.broadcasted_iota(jnp.int32, (128, CHUNK), 1)
        lows, highs = [], []
        for n, (rel, t) in enumerate(pairs):
            rank = ranks[:, n : n + 1]
            low = jnp.where(slot == rank, hits[n], 0.0)
            low = jnp.where(low_lane, low, 0.0).astype(BF16)
            high = jnp.where(slot - SLOTS == rank, hits[n], 0.0).astype(BF16)
            r.sel[rel, t, 0] = low
            r.sel[rel, t, 1] = high
            lows.append(low)
            highs.append(high)
        for n in range(2):
            low = jnp.concatenate(lows[2 * n : 2 * n + 2], axis=1)
            high = jnp.concatenate(highs[2 * n : 2 * n + 2], axis=1)
            both = (tn_dot(low, rows[:, :HALF]) + tn_dot(high, rows[:, HALF:])).astype(BF16)
            for t in range(2):
                chunk = both[CHUNK * t : CHUNK * (t + 1)]
                if n == 0:
                    r.cross[t] = chunk
                    for q in range(PIECES):
                        cross_copy(t, q).start()
                else:
                    r.line[t, near] = chunk

    swapped = edge * (core - c) * (core - c)
    order = [
        near + 2 * swapped,
        edge * (2 + near - 2 * swapped) + (1 - edge) * (1 - near),
        edge * (1 - near) + (1 - edge) * (2 + near),
        3 - near,
    ]

    def origin(s):
        outer = s // 2
        return (1 - outer) * (c + 2 * s) + outer * (5 * s - 11)

    def spread(i):
        s = order[i]
        o = origin(s)
        for t in range(2):
            block = r.line.at[t, s]
            for q in range(PIECES):
                piece = lanes_of(block, q)
                if i > 0:
                    await_bytes(piece, r.line_r.at[t, s, q])
                else:

                    @pl.when(jnp.logical_not(source))
                    def _(t=t, q=q, piece=piece):
                        await_bytes(piece, r.line_r.at[t, s, q])

                for side, condition in (
                    (0, jnp.logical_and(o <= zl, zl < 3)),
                    (1, jnp.logical_and(o >= zl, zl > 0)),
                ):
                    launch_if(
                        condition,
                        lambda piece=piece, t=t, s=s, q=q, side=side: remote(
                            piece,
                            piece,
                            r.line_s.at[0],
                            r.line_r.at[t, s, q],
                            on_z(-1 if side else 1),
                        ),
                    )
            for j, d, wanted in ((0, 2, role == t), (1, 1, role != t), (2, -1, role != t)):
                launch_if(
                    wanted,
                    lambda block=block, s=s, j=j, d=d: remote(
                        block, r.got.at[j, s], r.row_s.at[0], r.got_r.at[s], on_y(d)
                    ),
                )

    spread(0)
    spread(1)
    pass_on(2)
    pass_on(3)
    spread(2)
    spread(3)

    @pl.when(source)
    def _():
        logits = nt_dot(r.tokens[...].reshape(128, DM), r.router[...])
        table = r.tables[...].reshape(128, 128)
        first, second = table[:, 0:1], table[:, 1:2]
        expert = lax.broadcasted_iota(jnp.int32, logits.shape, 1)

        def lifted(chosen):
            logit = jnp.sum(jnp.where(expert == chosen, logits, 0.0), axis=1, keepdims=True)
            return jax.nn.sigmoid(logit)

        lift_first, lift_second = lifted(first), lifted(second)
        both = lift_first + lift_second
        for rel in range(2):
            for t in range(2):
                chosen = expert_of(rel, t)
                share = jnp.where(first == chosen, lift_first / both, 0.0) + jnp.where(
                    second == chosen, lift_second / both, 0.0
                )
                r.share[rel, t] = jnp.broadcast_to(share, (128, 128))

    other, side_end, far_end = 1 - near, 2 + near, 3 - near
    third = side_end + swapped * (near - side_end)
    fourth = near + swapped * (side_end - near)

    def arrived(p):
        await_bytes(r.got.at[:, p], r.got_r.at[p])

    def flatten(p, place):
        chunks = [r.line[role, p]] + [r.got[j, p] for j in range(3)]
        for n in range(2):
            a, b = chunks[2 * n].astype(F32), chunks[2 * n + 1].astype(F32)
            rows = slice(CHUNK * (2 * place + n), CHUNK * (2 * place + n + 1))
            r.flat[rows, :HALF] = jnp.concatenate([a[:SLOTS], b[:SLOTS]], axis=0).astype(BF16)
            r.flat[rows, HALF:] = jnp.concatenate([a[SLOTS:], b[SLOTS:]], axis=0).astype(BF16)

    def compute(which):
        rows = r.flat[...]
        gated = nt_dot(rows, r.gate[...])
        inner = (gated * jax.nn.sigmoid(gated) * nt_dot(rows, r.up[...])).astype(BF16)
        left = dot(inner, r.down[:, :HALF])
        right = dot(inner, r.down[:, HALF:])
        for n, p in enumerate(which):
            for j in range(4):
                rows = slice(SLOTS * (4 * n + j), SLOTS * (4 * n + j + 1))
                r.partial[j, p] = jnp.concatenate([left[rows], right[rows]], axis=0).astype(BF16)

    def give_back(p):
        for j, d in ((0, 2), (1, -1), (2, 1)):
            launch(
                remote(
                    r.partial.at[j + 1, p], r.back.at[j, p], r.row_s.at[0], r.back_r.at[p], on_y(d)
                )
            )

    arrived(near)
    flatten(near, 0)
    weights_ready()
    arrived(other)
    flatten(other, 1)
    compute((near, other))
    give_back(other)
    arrived(side_end)
    flatten(side_end, 1)
    arrived(far_end)
    flatten(far_end, 0)
    compute((far_end, side_end))
    for p in (far_end, third, fourth):
        give_back(p)

    def collect(p):
        await_bytes(r.back.at[:, p], r.back_r.at[p])
        r.total[role, p] = r.partial[0, p].astype(F32) + r.back[0, p].astype(F32)
        r.total[1 - role, p] = r.back[1, p].astype(F32) + r.back[2, p].astype(F32)

    ends = (at(lax.rem(4 * half + 4 + c, NZ), y, x, c), at(lax.rem(4 * half + 6 + c, NZ), y, x, c))

    def stream(s, place, side):
        here = 1 - lax.min(1, (origin(s) - place) * (origin(s) - place))
        return s + here * side * (4 - s)

    def along(s):
        o = origin(s)
        for t in range(2):
            for q in range(PIECES):
                cols = slice(WIDTH * q, WIDTH * (q + 1))
                out = lanes_of(r.line_out.at[t, s], q)

                def add_line(side, t=t, q=q, cols=cols):
                    block = lanes_of(r.line_in.at[side, t, s], q)
                    await_bytes(block, r.sum_r.at[t, stream(s, zl, side), q])
                    r.total[t, s, :, cols] += r.line_in[side, t, s, :, cols].astype(F32)

                @pl.when(jnp.logical_and(o >= zl, zl > 0))
                def _(add_line=add_line):
                    add_line(0)

                @pl.when(jnp.logical_and(o <= zl, zl < 3))
                def _(add_line=add_line):
                    add_line(1)

                r.line_out[t, s, :, cols] = r.total[t, s, :, cols].astype(BF16)
                for side, wanted, last in ((0, o > zl, zl == 3), (1, o < zl, zl == 0)):
                    launch_if(
                        jnp.logical_and(wanted, jnp.logical_not(last)),
                        lambda out=out, t=t, s=s, q=q, side=side: remote(
                            out,
                            lanes_of(r.line_in.at[side, t, s], q),
                            r.sum_s.at[0],
                            r.sum_r.at[t, stream(s, zl + 1 - 2 * side, side), q],
                            on_z(-1 if side else 1),
                        ),
                    )
                    launch_if(
                        jnp.logical_and(wanted, last),
                        lambda out=out, t=t, s=s, q=q, side=side: remote(
                            out,
                            lanes_of(r.ret.at[t], q),
                            r.sum_s.at[0],
                            r.ret_r.at[0],
                            ends[side],
                        ),
                    )

    for p in (other, far_end, third, fourth):
        collect(p)
        along(p)

    def home_copy(side, d, cc):
        cols = pl.ds(HALF * side, HALF)
        return remote(
            r.home_out.at[ring_x(d), cc, :, cols],
            r.home_in.at[x, :, cols],
            r.home_s.at[0],
            r.home_r.at[1 if d else 0],
            at(z, y, ring_x(d), cc),
        )

    home_targets = [(d, other) for d in (2, 1, 3) for other in range(2)] + [(0, 1 - c)]

    @pl.when(source)
    def _():
        for side in range(2):
            cols = slice(HALF * side, HALF * (side + 1))
            value = None
            for rel in range(2):
                for t in range(2):
                    if rel == 1 and side == 0 and t == 0:
                        await_bytes(r.ret, r.ret_r.at[0])
                    rows = r.ret[t] if rel else r.line_out[t, near]
                    term = r.share[rel, t][:, 0:1] * dot(r.sel[rel, t, side], rows)
                    value = term if value is None else value + term
            value = value.reshape(4, 2, 16, HALF)
            r.mixed[:, :, :, cols] = value
            r.home_out[:, :, :, cols] = value.astype(BF16)
            for d, cc in home_targets:
                home_copy(side, d, cc).start()
        r.home[...] = r.mixed[x, c]

    @pl.when(jnp.logical_not(source))
    def _():
        await_bytes(r.home_in.at[0], r.home_r.at[0])
        r.home[...] = r.home_in[x].astype(F32)

    result = r.hidden[...] + r.home[...]
    await_bytes(r.home_in.at[pl.ds(0, 3)], r.home_r.at[1])
    for d in (1, 3, 2):
        result = result + r.home_in[ring_x(-d)].astype(F32)
    r.out[...] = result.astype(BF16)

    await_bytes(units(21), r.early_s.at[0])
    await_bytes(r.slab_out.at[:, pl.ds(0, 3)], r.slab_s.at[0])
    await_bytes(units(36), r.row_s.at[0])
    for n, ref in enumerate((r.tokens, r.tables)):
        await_bytes(ref.at[pl.ds(0, 3)], r.tok_s.at[n])
    for d in range(1, NZ):

        @pl.when(z + d == NZ - 1)
        def _(d=d):
            await_bytes(r.total_in.at[pl.ds(0, d)], r.total_s.at[0])

    @pl.when(keeper)
    def _():
        await_bytes(r.gate, r.own_s.at[0])
        await_bytes(r.gate.at[own_rows], r.own_s.at[1])

    @pl.when(away)
    def _():
        for semaphore in (r.swap_s, r.pass_s):
            await_bytes(r.gate, semaphore.at[0])
            await_bytes(r.gate.at[own_rows], semaphore.at[1])

    @pl.when(source)
    def _():
        await_bytes(units(3), r.cross_s.at[0])
        await_bytes(units(9), r.sum_s.at[0])
        await_bytes(units(7), r.home_s.at[0])

    @pl.when(jnp.logical_not(source))
    def _():
        for n, ref in enumerate((r.tokens, r.tables)):
            await_bytes(ref.at[0], r.tok_s.at[n + 2])
        await_bytes(units(12), r.sum_s.at[0])

    forwards = sum(
        jnp.where(jnp.logical_and(origin(s) <= zl, zl < 3), 1, 0)
        + jnp.where(jnp.logical_and(origin(s) >= zl, zl > 0), 1, 0)
        for s in range(4)
    )
    for n in range(1, 9):

        @pl.when(forwards == n)
        def _(n=n):
            await_bytes(units(3 * n), r.line_s.at[0])


VMEM = pl.BlockSpec(memory_space=pltpu.VMEM)
ANY = pl.BlockSpec(memory_space=pl.ANY)


def body(
    stream,
    query,
    key,
    value,
    decay_rate,
    out_weight,
    norm_gain,
    router_weight,
    routes,
    expert_gate,
    expert_up,
    expert_down,
):
    return pl.pallas_call(
        kernel,
        out_shape=jax.ShapeDtypeStruct(stream.shape, BF16),
        in_specs=[ANY] * 12,
        out_specs=VMEM,
        scratch_shapes=list(SCRATCH.values()),
        compiler_params=pltpu.CompilerParams(
            collective_id=0, has_side_effects=True, vmem_limit_bytes=56 * 2**20
        ),
        name="whole",
    )(
        stream,
        query,
        key,
        value,
        decay_rate.reshape(1, 4),
        out_weight.T,
        norm_gain.reshape(1, DM),
        routes.T,
        router_weight.T,
        expert_gate.T,
        expert_up.T,
        expert_down,
    )


def solution(mesh):
    placed = (
        P(("ctx", "ep"), None),
        P("ctx", "ep"),
        P("ctx", "ep"),
        P("ctx", "ep"),
        P("ep"),
        P("ep", "ctx"),
        P(),
        P(),
        P(("ctx", "ep"), None),
        P(None, ("ep", "ctx")),
        P(None, ("ep", "ctx")),
        P(("ep", "ctx"), None),
    )
    return jax.shard_map(
        body, mesh=mesh, in_specs=placed, out_specs=P(("ctx", "ep"), None), check_vma=False
    )
```

```python
import jax
import jax.numpy as jnp
from jax import lax
from jax.experimental import pallas as pl
from jax.experimental.pallas import tpu as pltpu
from jax.sharding import PartitionSpec as P

EPSILON = 1e-06
MESH = pl.DeviceIdType.MESH
F32 = jnp.float32
BF16 = jnp.bfloat16
NY = 4
NZ = 8
NX = 4
DM = 3072
HALF = 1536
SLOTS = 24
CHUNK = 48
SHARD = 96
HIDDEN = 288
PIECES = 4
WIDTH = HALF // PIECES
PIECE = 96
PART = 48
SHARD_ORDER = (0, 1, 7, 2, 6, 3, 5, 4)


def bf(*shape):
    return pltpu.VMEM(shape, BF16)


def fl(*shape):
    return pltpu.VMEM(shape, F32)


def dma(*shape):
    return pltpu.SemaphoreType.DMA(shape)


INPUTS = (
    "stream_hbm", "query", "key", "value", "rates_hbm", "weight", "gain_hbm", "routes_hbm",
    "router_hbm", "gate_hbm", "up_hbm", "down_hbm", "out",
)
SCRATCH = dict(
    stream=bf(16, DM),
    rates=fl(1, 4),
    gain=fl(1, DM),
    routes=pltpu.VMEM((2, 16), jnp.int32),
    router=bf(16, DM),
    intra=fl(4, 128, 128),
    key_in=bf(4, 128, 128),
    value_in=bf(4, 128, 128),
    query_in=bf(4, 128, 128),
    local=fl(4, 128, 128),
    total_out=bf(128, 128),
    total_in=bf(8, 128, 128),
    entry=fl(128, 128),
    proj=bf(8, SHARD, 512),
    heads=bf(4, 4, 4, 2, 16, 128),
    pair_out=bf(2, 4, 4, 16, 384),
    pair_in=bf(2, 4, 4, 16, 384),
    part=fl(2, 4, 4, 16, 384),
    part_out=bf(2, 4, 4, 16, 384),
    part_in=bf(2, 4, 4, 16, 384),
    slab=fl(2, 4, 16, 384),
    slab_out=bf(2, 4, 16, 384),
    slab_in=bf(2, 4, 16, 384),
    hidden=fl(16, DM),
    tokens=bf(8, 16, DM),
    tables=pltpu.VMEM((8, 16, 128), jnp.int32),
    gate=bf(2 * HIDDEN, DM),
    up=bf(2 * HIDDEN, DM),
    down=bf(2 * HIDDEN, DM),
    sel=bf(2, 2, 2, 128, CHUNK),
    share=fl(2, 2, 128, 128),
    cross=bf(2, CHUNK, HALF),
    line=bf(2, 4, CHUNK, HALF),
    got=bf(3, 4, CHUNK, HALF),
    flat=bf(192, DM),
    partial=bf(4, 4, CHUNK, HALF),
    back=bf(3, 4, CHUNK, HALF),
    extra=bf(CHUNK, HALF),
    total=fl(2, 4, CHUNK, HALF),
    line_out=bf(2, 4, CHUNK, HALF),
    line_in=bf(2, 2, 4, CHUNK, HALF),
    ret=bf(2, CHUNK, HALF),
    mixed=fl(4, 2, 16, DM),
    home_out=bf(4, 2, 16, DM),
    home_in=bf(4, 16, DM),
    home=fl(16, DM),
    load_r=dma(6), early_s=dma(1), slab_s=dma(1), tok_s=dma(4), total_s=dma(1), own_s=dma(2),
    swap_s=dma(2), pass_s=dma(2), cross_s=dma(1), line_s=dma(1), row_s=dma(1), sum_s=dma(1),
    home_s=dma(1),
    block_r=dma(4), total_r=dma(1), proj_r=dma(4), heads_r=dma(1), pair_r=dma(2), part_r=dma(2),
    slab_r=dma(1), tok_r=dma(2), own_r=dma(2), swap_r=dma(4), pass_r=dma(2),
    line_r=dma(2, 4, PIECES), got_r=dma(4), far_r=dma(4), back_r=dma(4), extra_r=dma(1), sum_r=dma(2, 5, PIECES), ret_r=dma(1),
    home_r=dma(2),
)


class Refs:
    def __init__(self, refs):
        for name, ref in zip(INPUTS + tuple(SCRATCH), refs, strict=True):
            setattr(self, name, ref)


def at(z, y, x, c):
    return (z * NY + y, x * 2 + c)


def remote(src, dst, send, recv, device):
    return pltpu.make_async_remote_copy(
        src_ref=src,
        dst_ref=dst,
        send_sem=send,
        recv_sem=recv,
        device_id=device,
        device_id_type=MESH,
    )


def await_bytes(ref, semaphore):
    pltpu.make_async_copy(ref, ref, semaphore).wait()


def greet(barrier, devices):
    for device in devices:
        pl.semaphore_signal(barrier, inc=1, device_id=device, device_id_type=MESH)


def nt_dot(a, b):
    return lax.dot_general(a, b, (((1,), (1,)), ((), ())), preferred_element_type=F32)


def tn_dot(a, b):
    return lax.dot_general(a, b, (((0,), (0,)), ((), ())), preferred_element_type=F32)


def dot(a, b):
    return jnp.dot(a, b, preferred_element_type=F32)


def kernel(*refs):
    r = Refs(refs)
    ctx = lax.axis_index("ctx")
    ep = lax.axis_index("ep")
    z, y, x, c = ctx // NY, ctx % NY, ep // 2, ep % 2
    half, zl = z // 4, z % 4
    role = (y + z) % 2
    source = z % 2 == c
    keeper = c == role
    core = z % 2

    def ring_y(d):
        return lax.rem(y + d + NY, NY)

    def ring_z(d):
        return lax.rem(z + d + NZ, NZ)

    def ring_x(d):
        return lax.rem(x + d + NX, NX)

    def on_y(d):
        return at(z, ring_y(d), x, c)

    def on_z(d):
        return at(ring_z(d), y, x, c)

    def on_x(d):
        return at(z, y, ring_x(d), c)

    partner = at(z, y, x, 1 - c)
    beside = z + 1 - 2 * (z % 2)
    swap_to = (
        at(z, ring_y(1), x, 1 - c),
        at(z, ring_y(-1), x, 1 - c),
        at(beside, y, x, 1 - c),
    )
    barrier = pltpu.get_barrier_semaphore()
    greet(barrier, [on_y(d) for d in range(1, NY)])
    greet(barrier, [on_z(d) for d in range(1, NZ)])
    greet(barrier, [on_x(d) for d in range(1, NX)])
    greet(barrier, [at(z, y, ring_x(d), 1 - c) for d in range(NX)])
    greet(barrier, swap_to)

    def launch(copy):
        copy.start()

    def launch_if(condition, make):
        @pl.when(condition)
        def _():
            make().start()

    def units(n):
        return r.gate.at[pl.ds(0, 16 * n)]

    experts = ((r.gate_hbm, r.gate), (r.up_hbm, r.up), (r.down_hbm, r.down))
    own_rows = pl.ds(0, HIDDEN)

    def part_rows(base, k, side):
        return pl.ds(base + side * PIECE + k * PART, PART)

    def load(m):
        hbm, ref = experts[m]
        return pltpu.make_async_copy(hbm, ref.at[own_rows], r.own_r.at[m // 2])

    def head_columns(h):
        return pl.ds(pl.multiple_of(h * 128, 128), 128)

    blocks = ((r.key, r.key_in), (r.value, r.value_in), (r.query, r.query_in))
    for whole, own in blocks:
        pltpu.make_async_copy(whole.at[:, head_columns(y)], own.at[y], r.load_r.at[0]).start()
    pltpu.make_async_copy(r.weight, r.proj.at[0], r.load_r.at[0]).start()
    small = (
        (r.rates_hbm, r.rates),
        (r.stream_hbm, r.stream),
        (r.gain_hbm, r.gain),
        (r.routes_hbm, r.routes),
        (r.router_hbm, r.router),
    )
    for n, (hbm, ref) in enumerate(small):
        pltpu.make_async_copy(hbm, ref, r.load_r.at[n + 1]).start()

    @pl.when(keeper)
    def _():
        for m in range(3):
            load(m).start()

    away = jnp.logical_not(keeper)
    batches = (((0, 1), (0, 1)), ((0, 1), (2, 3, 4)), ((0, 1), (5,)), ((2,), range(6)))

    def parts(batch):
        sides, numbers = batches[batch]
        return [(number // 2, number % 2, side) for number in numbers for side in sides]

    def swap(batch, numbers=range(6)):
        for m, k, side in parts(batch):
            if m * 2 + k in numbers:
                launch_if(
                    away,
                    lambda m=m, k=k, side=side: remote(
                        experts[m][0].at[part_rows(0, k, side)],
                        experts[m][1].at[part_rows(HIDDEN, k, side)],
                        r.swap_s.at[side // 2],
                        r.swap_r.at[batch],
                        swap_to[side],
                    ),
                )

    def pass_on(batch):
        @pl.when(away)
        def _():
            await_bytes(units(3 * len(parts(batch))), r.swap_r.at[batch])
            for m, k, side in parts(batch):
                ref = experts[m][1].at[part_rows(HIDDEN, k, side)]
                remote(ref, ref, r.pass_s.at[side // 2], r.pass_r.at[side // 2], partner).start()

    def weights_ready():
        await_bytes(r.gate, r.own_r.at[0])
        await_bytes(r.gate.at[own_rows], r.own_r.at[1])

        @pl.when(keeper)
        def _():
            await_bytes(r.gate, r.pass_r.at[0])
            await_bytes(r.gate.at[own_rows], r.pass_r.at[1])

    pl.semaphore_wait(barrier, NY - 1 + NZ - 1 + NX - 1 + NX + 3)

    for n, (whole, own) in enumerate(blocks):
        for d in (2, 1, 3):
            launch(
                remote(
                    whole.at[:, head_columns(ring_y(d))],
                    own.at[y],
                    r.early_s.at[0],
                    r.block_r.at[0 if n == 2 else d],
                    on_y(d),
                )
            )

    def shard(distance):
        return r.proj.at[SHARD_ORDER.index(distance % NZ)]

    def z_step(k):
        a, b, to_a, to_b = shard(1 - k), shard(k - 1), shard(-k), shard(k)
        if k == 1:
            a = b = r.weight
        if k == 4:
            a, to_a = a.at[pl.ds(0, 48)], to_a.at[pl.ds(0, 48)]
            b, to_b = b.at[pl.ds(48, 48)], to_b.at[pl.ds(48, 48)]
        launch(remote(a, to_a, r.early_s.at[0], r.proj_r.at[k - 1], on_z(1)))
        launch(remote(b, to_b, r.early_s.at[0], r.proj_r.at[k - 1], on_z(-1)))

    def z_wait(k):
        await_bytes(r.proj.at[pl.ds(0, 2 if k < 4 else 1)], r.proj_r.at[k - 1])

    z_step(1)
    swap(0, (0,))
    for m in range(3):
        launch_if(
            keeper,
            lambda m=m: remote(
                experts[m][0], experts[m][1].at[own_rows], r.own_s.at[m // 2], r.own_r.at[m // 2], partner
            ),
        )

    for n, (hbm, ref) in enumerate(small):
        await_bytes(ref, r.load_r.at[n + 1])
    await_bytes(units(2), r.load_r.at[0])
    rates = r.rates[...]
    length = r.query.shape[0]
    gap = (
        lax.broadcasted_iota(jnp.int32, (length, length), 0)
        - lax.broadcasted_iota(jnp.int32, (length, length), 1)
    ).astype(F32)
    position = lax.broadcasted_iota(jnp.int32, (length, 1), 0).astype(F32)
    lane = lax.broadcasted_iota(jnp.int32, rates.shape, 1)
    own_rate = jnp.sum(jnp.where(lane == y, rates, 0.0), axis=1, keepdims=True)

    def power(n):
        return jnp.exp(-own_rate * (128.0 * n))

    fade = jnp.exp(-own_rate * (length - 1.0 - position))
    for d in (0, 1, 3, 2):
        if d:
            await_bytes(r.key_in.at[pl.ds(0, 2)], r.block_r.at[d])
        i = ring_y(-d)
        faded = (r.key_in[i].astype(F32) * fade).astype(BF16)
        r.local[i] = tn_dot(faded, r.value_in[i])
    swap(0, (1,))
    total = r.local[3]
    for i in range(3):
        total = total + power(3 - i) * r.local[i]
    r.total_out[...] = total.astype(BF16)
    for d in range(NZ - 1, 0, -1):
        launch_if(
            z + d < NZ,
            lambda d=d: remote(
                r.total_out, r.total_in.at[z], r.total_s.at[0], r.total_r.at[0], on_z(d)
            ),
        )
    z_wait(1)
    z_step(2)
    decay = jnp.where(gap >= 0, jnp.exp(-own_rate * jnp.maximum(gap, 0.0)), 0.0)
    await_bytes(r.key_in.at[pl.ds(0, 3)], r.block_r.at[0])
    for i in range(NY):
        scores = nt_dot(r.query_in[i], r.key_in[i])
        r.intra[i] = dot((scores * decay).astype(BF16), r.value_in[i])
    r.entry[...] = jnp.zeros_like(r.entry)
    for d in range(1, NZ):

        @pl.when(z == d)
        def _(d=d):
            await_bytes(r.total_in.at[pl.ds(0, d)], r.total_r.at[0])

    for d in range(1, NZ):

        @pl.when(z >= d)
        def _(d=d):
            r.entry[...] += power(4 * (d - 1)) * r.total_in[ring_z(-d)].astype(F32)

    incoming = r.entry[...]
    fade = jnp.exp(-own_rate * (position + 1.0))
    for i in range(NY):
        mixed = r.intra[i] + fade * dot(r.query_in[i], incoming.astype(BF16))
        incoming = power(1) * incoming + r.local[i]
        mean = jnp.mean(mixed * mixed, axis=-1, keepdims=True)
        out = (mixed * lax.rsqrt(mean + EPSILON)).astype(BF16)
        r.heads[y, i] = out.reshape(4, 2, 16, 128)
    for d in (2, 1, 3):
        launch(remote(r.heads.at[y], r.heads.at[y], r.early_s.at[0], r.heads_r.at[0], on_y(d)))
    z_wait(2)
    z_step(3)

    z_wait(3)
    z_step(4)
    swap(3)
    await_bytes(r.heads.at[pl.ds(0, 3)], r.heads_r.at[0])
    swap(1)

    def project(which, n):
        lhs = jnp.concatenate([r.heads[h, :, :, which].reshape(256, 128) for h in range(4)], axis=1)
        rhs = r.proj[4 * n : 4 * (n + 1)].reshape(384, 512)
        return nt_dot(lhs, rhs).reshape(4, 4, 16, 384)

    for n in range(2):
        if n == 1:
            z_wait(4)
        r.pair_out[n] = project(1 - c, n).astype(BF16)
        launch(remote(r.pair_out.at[n], r.pair_in.at[n], r.early_s.at[0], r.pair_r.at[n], partner))
        r.part[n] = project(c, n)
    for n in range(2):
        await_bytes(r.pair_in.at[n], r.pair_r.at[n])
        both = r.part[n] + r.pair_in[n].astype(F32)
        r.part[n] = both
        r.part_out[n] = both.astype(BF16)
        for d in (2, 1, 3):
            launch(
                remote(
                    r.part_out.at[n, :, ring_x(d)],
                    r.part_in.at[n, x],
                    r.early_s.at[0],
                    r.part_r.at[n],
                    on_x(d),
                )
            )
    pass_on(0)
    for n in range(2):
        slab = r.part[n, :, x]
        await_bytes(r.part_in.at[n, pl.ds(0, 3)], r.part_r.at[n])
        for d in (1, 3, 2):
            slab = slab + r.part_in[n, ring_x(-d)].astype(F32)
        r.slab[n] = slab
        r.slab_out[n] = slab.astype(BF16)
        for d in (2, 1, 3):
            launch(
                remote(
                    r.slab_out.at[n, ring_y(d)],
                    r.slab_in.at[n, y],
                    r.slab_s.at[0],
                    r.slab_r.at[0],
                    on_y(d),
                )
            )
    await_bytes(r.slab_in.at[:, pl.ds(0, 3)], r.slab_r.at[0])
    for n in range(2):
        for d in (1, 3, 2):
            r.slab[n, ring_y(-d)] = r.slab_in[n, ring_y(-d)].astype(F32)
    swap(2)
    def columns_of(yy):
        places = [SHARD_ORDER.index(distance) for distance in range(NZ)]
        ordered = [r.slab[p // 4, yy][:, SHARD * (p % 4) : SHARD * (p % 4 + 1)] for p in places]
        return pltpu.roll(jnp.concatenate(ordered, axis=1), z * SHARD, 1)

    quarters = [columns_of(yy) for yy in range(NY)]
    attended = jnp.concatenate(
        [
            quarters[yy][:, SHARD * zz : SHARD * (zz + 1)]
            for zz in range(NZ)
            for yy in range(NY)
        ],
        axis=1,
    )
    hidden = r.stream[...].astype(F32) + attended
    r.hidden[...] = hidden
    mean = jnp.mean(hidden * hidden, axis=-1, keepdims=True)
    r.tokens[ep] = (hidden * lax.rsqrt(mean + EPSILON) * r.gain[...]).astype(BF16)
    square = lax.broadcasted_iota(jnp.int32, (16, 16), 0) == lax.broadcasted_iota(
        jnp.int32, (16, 16), 1
    )

    def upright(row):
        wide = jnp.where(square, jnp.broadcast_to(row, (16, 16)).astype(F32), 0.0)
        return jnp.sum(wide, axis=1, keepdims=True)

    table_lane = lax.broadcasted_iota(jnp.int32, (16, 128), 1)
    r.tables[ep] = jnp.where(
        table_lane == 0, upright(r.routes[0:1, :]), upright(r.routes[1:2, :])
    ).astype(jnp.int32)

    for d in (2, 1, 3, 0):
        for n, ref in enumerate((r.tokens, r.tables)):

            def make(d=d, n=n, ref=ref):
                block = ref.at[ep]
                device = at(z, y, ring_x(d), core)
                return remote(block, block, r.tok_s.at[n if d else n + 2], r.tok_r.at[n], device)

            if d:
                launch(make())
            else:
                launch_if(jnp.logical_not(source), make)

    pass_on(1)

    near = zl // 2
    edge = (zl * zl - 3 * zl + 2) // 2
    cross_to = at(lax.rem(4 * half + 7 - 3 * near, NZ), y, x, c)

    def lanes_of(ref, q):
        return ref.at[:, pl.ds(WIDTH * q, WIDTH)]

    def cross_copy(t, q):
        return remote(
            lanes_of(r.cross.at[t], q),
            lanes_of(r.line.at[t, 3 - near], q),
            r.cross_s.at[0],
            r.line_r.at[t, 3 - near, q],
            cross_to,
        )

    low_lane = lax.broadcasted_iota(jnp.int32, (128, CHUNK), 1) < SLOTS

    def expert_of(rel, t):
        return x * 4 + t * 2 + (half if rel == 0 else 1 - half)

    @pl.when(source)
    def _():
        for n, ref in enumerate((r.tokens, r.tables)):
            await_bytes(ref.at[pl.ds(0, 7)], r.tok_r.at[n])
        rows = r.tokens[...].reshape(128, DM)
        table = r.tables[...].reshape(128, 128)
        first, second = table[:, 0:1], table[:, 1:2]
        lanes = lax.broadcasted_iota(jnp.int32, (128, 128), 1)
        earlier = (lanes < lax.broadcasted_iota(jnp.int32, (128, 128), 0)).astype(BF16)
        pairs = [(1, 0), (1, 1), (0, 0), (0, 1)]
        hits = []
        for rel, t in pairs:
            expert = expert_of(rel, t)
            hits.append(jnp.where(jnp.logical_or(first == expert, second == expert), 1.0, 0.0))
        wide = jnp.zeros((128, 128), F32)
        for n, hit in enumerate(hits):
            wide = jnp.where(lanes == n, hit, wide)
        ranks = dot(earlier, wide.astype(BF16)).astype(jnp.int32)
        slot = lax.broadcasted_iota(jnp.int32, (128, CHUNK), 1)
        lows, highs = [], []
        for n, (rel, t) in enumerate(pairs):
            rank = ranks[:, n : n + 1]
            low = jnp.where(slot == rank, hits[n], 0.0)
            low = jnp.where(low_lane, low, 0.0).astype(BF16)
            high = jnp.where(slot - SLOTS == rank, hits[n], 0.0).astype(BF16)
            r.sel[rel, t, 0] = low
            r.sel[rel, t, 1] = high
            lows.append(low)
            highs.append(high)
        for n in range(2):
            low = jnp.concatenate(lows[2 * n : 2 * n + 2], axis=1)
            high = jnp.concatenate(highs[2 * n : 2 * n + 2], axis=1)
            both = (tn_dot(low, rows[:, :HALF]) + tn_dot(high, rows[:, HALF:])).astype(BF16)
            for t in range(2):
                chunk = both[CHUNK * t : CHUNK * (t + 1)]
                if n == 0:
                    r.cross[t] = chunk
                    for q in range(PIECES):
                        cross_copy(t, q).start()
                else:
                    r.line[t, near] = chunk

    swapped = edge * (core - c) * (core - c)
    order = [
        near + 2 * swapped,
        edge * (2 + near - 2 * swapped) + (1 - edge) * (1 - near),
        edge * (1 - near) + (1 - edge) * (2 + near),
        3 - near,
    ]

    other, side_end, far_end = 1 - near, 2 + near, 3 - near
    two_on = on_z(2 - 4 * near)

    def origin(s):
        outer = s // 2
        return (1 - outer) * (c + 2 * s) + outer * (5 * s - 11)

    def spread(i):
        s = order[i]
        o = origin(s)
        for t in range(2):
            block = r.line.at[t, s]
            for q in range(PIECES):
                piece = lanes_of(block, q)
                if i > 0:
                    await_bytes(piece, r.line_r.at[t, s, q])
                else:

                    @pl.when(jnp.logical_not(source))
                    def _(t=t, q=q, piece=piece):
                        await_bytes(piece, r.line_r.at[t, s, q])

                for side, condition in (
                    (0, jnp.logical_and(o <= zl, zl < 3)),
                    (1, jnp.logical_and(o >= zl, zl > 0)),
                ):
                    launch_if(
                        condition,
                        lambda piece=piece, t=t, s=s, q=q, side=side: remote(
                            piece,
                            piece,
                            r.line_s.at[0],
                            r.line_r.at[t, s, q],
                            on_z(-1 if side else 1),
                        ),
                    )
            straight = jnp.logical_and(role == t, s != far_end)
            for j, d, wanted in ((0, 2, straight), (1, 1, role != t), (2, -1, role != t)):
                launch_if(
                    wanted,
                    lambda block=block, s=s, j=j, d=d: remote(
                        block,
                        r.got.at[j, s],
                        r.row_s.at[0],
                        (r.got_r if j else r.far_r).at[s],
                        on_y(d),
                    ),
                )

    spread(0)
    spread(1)
    pass_on(2)
    pass_on(3)
    spread(2)
    spread(3)
    across = r.got.at[0, side_end]
    await_bytes(across, r.far_r.at[side_end])
    launch(remote(across, across, r.row_s.at[0], r.far_r.at[side_end], two_on))

    @pl.when(source)
    def _():
        logits = nt_dot(r.tokens[...].reshape(128, DM), r.router[...])
        table = r.tables[...].reshape(128, 128)
        first, second = table[:, 0:1], table[:, 1:2]
        expert = lax.broadcasted_iota(jnp.int32, logits.shape, 1)

        def lifted(chosen):
            logit = jnp.sum(jnp.where(expert == chosen, logits, 0.0), axis=1, keepdims=True)
            return jax.nn.sigmoid(logit)

        lift_first, lift_second = lifted(first), lifted(second)
        both = lift_first + lift_second
        for rel in range(2):
            for t in range(2):
                chosen = expert_of(rel, t)
                share = jnp.where(first == chosen, lift_first / both, 0.0) + jnp.where(
                    second == chosen, lift_second / both, 0.0
                )
                r.share[rel, t] = jnp.broadcast_to(share, (128, 128))

    third = side_end + swapped * (near - side_end)
    fourth = near + swapped * (side_end - near)

    def arrived(p):
        await_bytes(r.got.at[pl.ds(1, 2), p], r.got_r.at[p])
        if p is not side_end:
            await_bytes(r.got.at[0, p], r.far_r.at[p])

    def flatten(p, place):
        chunks = [r.line[role, p]] + [r.got[j, p] for j in range(3)]
        for n in range(2):
            a, b = chunks[2 * n].astype(F32), chunks[2 * n + 1].astype(F32)
            rows = slice(CHUNK * (2 * place + n), CHUNK * (2 * place + n + 1))
            r.flat[rows, :HALF] = jnp.concatenate([a[:SLOTS], b[:SLOTS]], axis=0).astype(BF16)
            r.flat[rows, HALF:] = jnp.concatenate([a[SLOTS:], b[SLOTS:]], axis=0).astype(BF16)

    def compute(which):
        rows = r.flat[...]
        gated = nt_dot(rows, r.gate[...])
        inner = (gated * jax.nn.sigmoid(gated) * nt_dot(rows, r.up[...])).astype(BF16)
        left = dot(inner, r.down[:, :HALF])
        right = dot(inner, r.down[:, HALF:])
        for n, p in enumerate(which):
            for j in range(4):
                rows = slice(SLOTS * (4 * n + j), SLOTS * (4 * n + j + 1))
                r.partial[j, p] = jnp.concatenate([left[rows], right[rows]], axis=0).astype(BF16)

    def give_back(p, ways=(0, 1, 2)):
        for j in ways:
            d = (2, -1, 1)[j]
            launch(
                remote(
                    r.partial.at[j + 1, p], r.back.at[j, p], r.row_s.at[0], r.back_r.at[p], on_y(d)
                )
            )

    arrived(near)
    flatten(near, 0)
    weights_ready()
    arrived(other)
    flatten(other, 1)
    compute((near, other))
    give_back(other)
    arrived(side_end)
    flatten(side_end, 1)
    arrived(far_end)
    flatten(far_end, 0)
    compute((far_end, side_end))
    launch(remote(r.partial.at[1, far_end], r.extra, r.row_s.at[0], r.extra_r.at[0], two_on))
    give_back(far_end, (1, 2))
    give_back(side_end, (1, 2))

    def collect(p):
        if p is far_end:
            await_bytes(r.back.at[pl.ds(1, 2), p], r.back_r.at[p])
            r.total[role, p] = r.partial[0, p].astype(F32)
        else:
            await_bytes(r.back.at[:, p], r.back_r.at[p])
            r.total[role, p] = r.partial[0, p].astype(F32) + r.back[0, p].astype(F32)
        r.total[1 - role, p] = r.back[1, p].astype(F32) + r.back[2, p].astype(F32)

    ends = (at(lax.rem(4 * half + 4 + c, NZ), y, x, c), at(lax.rem(4 * half + 6 + c, NZ), y, x, c))

    def stream(s, place, side):
        here = 1 - lax.min(1, (origin(s) - place) * (origin(s) - place))
        return s + here * side * (4 - s)

    def along(s):
        o = origin(s)
        for t in range(2):
            for q in range(PIECES):
                cols = slice(WIDTH * q, WIDTH * (q + 1))
                out = lanes_of(r.line_out.at[t, s], q)

                def add_line(side, t=t, q=q, cols=cols):
                    block = lanes_of(r.line_in.at[side, t, s], q)
                    await_bytes(block, r.sum_r.at[t, stream(s, zl, side), q])
                    r.total[t, s, :, cols] += r.line_in[side, t, s, :, cols].astype(F32)

                @pl.when(jnp.logical_and(o >= zl, zl > 0))
                def _(add_line=add_line):
                    add_line(0)

                @pl.when(jnp.logical_and(o <= zl, zl < 3))
                def _(add_line=add_line):
                    add_line(1)

                r.line_out[t, s, :, cols] = r.total[t, s, :, cols].astype(BF16)
                for side, wanted, last in ((0, o > zl, zl == 3), (1, o < zl, zl == 0)):
                    launch_if(
                        jnp.logical_and(wanted, jnp.logical_not(last)),
                        lambda out=out, t=t, s=s, q=q, side=side: remote(
                            out,
                            lanes_of(r.line_in.at[side, t, s], q),
                            r.sum_s.at[0],
                            r.sum_r.at[t, stream(s, zl + 1 - 2 * side, side), q],
                            on_z(-1 if side else 1),
                        ),
                    )
                    launch_if(
                        jnp.logical_and(wanted, last),
                        lambda out=out, t=t, s=s, q=q, side=side: remote(
                            out,
                            lanes_of(r.ret.at[t], q),
                            r.sum_s.at[0],
                            r.ret_r.at[0],
                            ends[side],
                        ),
                    )

    @pl.when(edge == 1)
    def _():
        collect(other)
        along(other)

    await_bytes(r.extra, r.extra_r.at[0])
    joined = r.partial[1, side_end].astype(F32) + r.extra[...].astype(F32)
    r.partial[1, side_end] = joined.astype(BF16)
    give_back(side_end, (0,))
    give_back(near)

    @pl.when(edge == 0)
    def _():
        collect(other)
        along(other)

    for p in (far_end, third, fourth):
        collect(p)
        along(p)

    def home_copy(side, d, cc):
        cols = pl.ds(HALF * side, HALF)
        return remote(
            r.home_out.at[ring_x(d), cc, :, cols],
            r.home_in.at[x, :, cols],
            r.home_s.at[0],
            r.home_r.at[1 if d else 0],
            at(z, y, ring_x(d), cc),
        )

    home_targets = [(d, other) for d in (2, 1, 3) for other in range(2)] + [(0, 1 - c)]

    @pl.when(source)
    def _():
        for side in range(2):
            cols = slice(HALF * side, HALF * (side + 1))
            value = None
            for rel in range(2):
                for t in range(2):
                    if rel == 1 and side == 0 and t == 0:
                        await_bytes(r.ret, r.ret_r.at[0])
                    rows = r.ret[t] if rel else r.line_out[t, near]
                    term = r.share[rel, t][:, 0:1] * dot(r.sel[rel, t, side], rows)
                    value = term if value is None else value + term
            value = value.reshape(4, 2, 16, HALF)
            r.mixed[:, :, :, cols] = value
            r.home_out[:, :, :, cols] = value.astype(BF16)
            for d, cc in home_targets:
                home_copy(side, d, cc).start()
        r.home[...] = r.mixed[x, c]

    @pl.when(jnp.logical_not(source))
    def _():
        await_bytes(r.home_in.at[0], r.home_r.at[0])
        r.home[...] = r.home_in[x].astype(F32)

    result = r.hidden[...] + r.home[...]
    await_bytes(r.home_in.at[pl.ds(0, 3)], r.home_r.at[1])
    for d in (1, 3, 2):
        result = result + r.home_in[ring_x(-d)].astype(F32)
    r.out[...] = result.astype(BF16)

    await_bytes(units(21), r.early_s.at[0])
    await_bytes(r.slab_out.at[:, pl.ds(0, 3)], r.slab_s.at[0])
    await_bytes(units(36), r.row_s.at[0])
    for n, ref in enumerate((r.tokens, r.tables)):
        await_bytes(ref.at[pl.ds(0, 3)], r.tok_s.at[n])
    for d in range(1, NZ):

        @pl.when(z + d == NZ - 1)
        def _(d=d):
            await_bytes(r.total_in.at[pl.ds(0, d)], r.total_s.at[0])

    @pl.when(keeper)
    def _():
        await_bytes(r.gate, r.own_s.at[0])
        await_bytes(r.gate.at[own_rows], r.own_s.at[1])

    @pl.when(away)
    def _():
        for semaphore in (r.swap_s, r.pass_s):
            await_bytes(r.gate, semaphore.at[0])
            await_bytes(r.gate.at[own_rows], semaphore.at[1])

    @pl.when(source)
    def _():
        await_bytes(units(3), r.cross_s.at[0])
        await_bytes(units(9), r.sum_s.at[0])
        await_bytes(units(7), r.home_s.at[0])

    @pl.when(jnp.logical_not(source))
    def _():
        for n, ref in enumerate((r.tokens, r.tables)):
            await_bytes(ref.at[0], r.tok_s.at[n + 2])
        await_bytes(units(12), r.sum_s.at[0])

    forwards = sum(
        jnp.where(jnp.logical_and(origin(s) <= zl, zl < 3), 1, 0)
        + jnp.where(jnp.logical_and(origin(s) >= zl, zl > 0), 1, 0)
        for s in range(4)
    )
    for n in range(1, 9):

        @pl.when(forwards == n)
        def _(n=n):
            await_bytes(units(3 * n), r.line_s.at[0])


VMEM = pl.BlockSpec(memory_space=pltpu.VMEM)
ANY = pl.BlockSpec(memory_space=pl.ANY)


def body(
    stream,
    query,
    key,
    value,
    decay_rate,
    out_weight,
    norm_gain,
    router_weight,
    routes,
    expert_gate,
    expert_up,
    expert_down,
):
    return pl.pallas_call(
        kernel,
        out_shape=jax.ShapeDtypeStruct(stream.shape, BF16),
        in_specs=[ANY] * 12,
        out_specs=VMEM,
        scratch_shapes=list(SCRATCH.values()),
        compiler_params=pltpu.CompilerParams(
            collective_id=0, has_side_effects=True, vmem_limit_bytes=56 * 2**20
        ),
        name="whole",
    )(
        stream,
        query,
        key,
        value,
        decay_rate.reshape(1, 4),
        out_weight.T,
        norm_gain.reshape(1, DM),
        routes.T,
        router_weight.T,
        expert_gate.T,
        expert_up.T,
        expert_down,
    )


def solution(mesh):
    placed = (
        P(("ctx", "ep"), None),
        P("ctx", "ep"),
        P("ctx", "ep"),
        P("ctx", "ep"),
        P("ep"),
        P("ep", "ctx"),
        P(),
        P(),
        P(("ctx", "ep"), None),
        P(None, ("ep", "ctx")),
        P(None, ("ep", "ctx")),
        P(("ep", "ctx"), None),
    )
    return jax.shard_map(
        body, mesh=mesh, in_specs=placed, out_specs=P(("ctx", "ep"), None), check_vma=False
    )
```

```python
import jax
import jax.numpy as jnp
from jax import lax
from jax.experimental import pallas as pl
from jax.experimental.pallas import tpu as pltpu
from jax.sharding import PartitionSpec as P

EPSILON = 1e-06
MESH = pl.DeviceIdType.MESH
F32 = jnp.float32
BF16 = jnp.bfloat16
NY = 4
NZ = 8
NX = 4
DM = 3072
HALF = 1536
SLOTS = 24
CHUNK = 48
SHARD = 96
HIDDEN = 288
PIECES = 3
WIDTH = HALF // PIECES
PIECE = 96
PART = 48
SHARD_ORDER = (0, 1, 7, 2, 6, 3, 5, 4)


def bf(*shape):
    return pltpu.VMEM(shape, BF16)


def fl(*shape):
    return pltpu.VMEM(shape, F32)


def dma(*shape):
    return pltpu.SemaphoreType.DMA(shape)


INPUTS = (
    "stream_hbm", "query", "key", "value", "rates_hbm", "weight", "gain_hbm", "routes_hbm",
    "router_hbm", "gate_hbm", "up_hbm", "down_hbm", "out",
)
SCRATCH = dict(
    stream=bf(16, DM),
    rates=fl(1, 4),
    gain=fl(1, DM),
    routes=pltpu.VMEM((2, 16), jnp.int32),
    router=bf(16, DM),
    intra=fl(4, 128, 128),
    key_in=bf(4, 128, 128),
    value_in=bf(4, 128, 128),
    query_in=bf(4, 128, 128),
    local=fl(4, 128, 128),
    total_out=bf(128, 128),
    total_in=bf(8, 128, 128),
    entry=fl(128, 128),
    proj=bf(8, SHARD, 512),
    heads=bf(4, 4, 4, 2, 16, 128),
    pair_out=bf(2, 4, 4, 16, 384),
    pair_in=bf(2, 4, 4, 16, 384),
    part=fl(2, 4, 4, 16, 384),
    part_out=bf(2, 4, 4, 16, 384),
    part_in=bf(2, 4, 4, 16, 384),
    slab=fl(2, 4, 16, 384),
    slab_out=bf(2, 4, 16, 384),
    slab_in=bf(2, 4, 16, 384),
    hidden=fl(16, DM),
    tokens=bf(8, 16, DM),
    tables=pltpu.VMEM((8, 16, 128), jnp.int32),
    gate=bf(2 * HIDDEN, DM),
    up=bf(2 * HIDDEN, DM),
    down=bf(2 * HIDDEN, DM),
    sel=bf(2, 2, 2, 128, CHUNK),
    share=fl(2, 2, 128, 128),
    cross=bf(2, CHUNK, HALF),
    line=bf(2, 4, CHUNK, HALF),
    got=bf(3, 4, CHUNK, HALF),
    flat=bf(192, DM),
    partial=bf(4, 4, CHUNK, HALF),
    back=bf(3, 4, CHUNK, HALF),
    extra=bf(CHUNK, HALF),
    total=fl(2, 4, CHUNK, HALF),
    line_out=bf(2, 4, CHUNK, HALF),
    line_in=bf(2, 2, 4, CHUNK, HALF),
    ret=bf(2, CHUNK, HALF),
    mixed=fl(4, 2, 16, DM),
    home_out=bf(4, 2, 16, DM),
    home_in=bf(4, 16, DM),
    home=fl(16, DM),
    load_r=dma(6), early_s=dma(1), slab_s=dma(1), tok_s=dma(4), total_s=dma(1), own_s=dma(2),
    swap_s=dma(2), pass_s=dma(2), cross_s=dma(1), line_s=dma(1), row_s=dma(1), sum_s=dma(1),
    home_s=dma(1),
    block_r=dma(4), total_r=dma(1), proj_r=dma(4), heads_r=dma(1), pair_r=dma(2), part_r=dma(2),
    slab_r=dma(1), tok_r=dma(2), own_r=dma(2), swap_r=dma(4), pass_r=dma(2),
    line_r=dma(2, 4, PIECES), got_r=dma(4), far_r=dma(4), back_r=dma(4), extra_r=dma(1), sum_r=dma(2, 5, PIECES), ret_r=dma(1),
    home_r=dma(2),
)


class Refs:
    def __init__(self, refs):
        for name, ref in zip(INPUTS + tuple(SCRATCH), refs, strict=True):
            setattr(self, name, ref)


def at(z, y, x, c):
    return (z * NY + y, x * 2 + c)


def remote(src, dst, send, recv, device):
    return pltpu.make_async_remote_copy(
        src_ref=src,
        dst_ref=dst,
        send_sem=send,
        recv_sem=recv,
        device_id=device,
        device_id_type=MESH,
    )


def await_bytes(ref, semaphore):
    pltpu.make_async_copy(ref, ref, semaphore).wait()


def greet(barrier, devices):
    for device in devices:
        pl.semaphore_signal(barrier, inc=1, device_id=device, device_id_type=MESH)


def nt_dot(a, b):
    return lax.dot_general(a, b, (((1,), (1,)), ((), ())), preferred_element_type=F32)


def tn_dot(a, b):
    return lax.dot_general(a, b, (((0,), (0,)), ((), ())), preferred_element_type=F32)


def dot(a, b):
    return jnp.dot(a, b, preferred_element_type=F32)


def kernel(*refs):
    r = Refs(refs)
    ctx = lax.axis_index("ctx")
    ep = lax.axis_index("ep")
    z, y, x, c = ctx // NY, ctx % NY, ep // 2, ep % 2
    half, zl = z // 4, z % 4
    role = (y + z) % 2
    source = z % 2 == c
    keeper = c == role
    core = z % 2

    def ring_y(d):
        return lax.rem(y + d + NY, NY)

    def ring_z(d):
        return lax.rem(z + d + NZ, NZ)

    def ring_x(d):
        return lax.rem(x + d + NX, NX)

    def on_y(d):
        return at(z, ring_y(d), x, c)

    def on_z(d):
        return at(ring_z(d), y, x, c)

    def on_x(d):
        return at(z, y, ring_x(d), c)

    partner = at(z, y, x, 1 - c)
    beside = z + 1 - 2 * (z % 2)
    swap_to = (
        at(z, ring_y(1), x, 1 - c),
        at(z, ring_y(-1), x, 1 - c),
        at(beside, y, x, 1 - c),
    )
    barrier = pltpu.get_barrier_semaphore()
    greet(barrier, [on_y(d) for d in range(1, NY)])
    greet(barrier, [on_z(d) for d in range(1, NZ)])
    greet(barrier, [on_x(d) for d in range(1, NX)])
    greet(barrier, [at(z, y, ring_x(d), 1 - c) for d in range(NX)])
    greet(barrier, swap_to)

    def launch(copy):
        copy.start()

    def launch_if(condition, make):
        @pl.when(condition)
        def _():
            make().start()

    def units(n):
        return r.gate.at[pl.ds(0, 16 * n)]

    experts = ((r.gate_hbm, r.gate), (r.up_hbm, r.up), (r.down_hbm, r.down))
    own_rows = pl.ds(0, HIDDEN)

    def part_rows(base, k, side):
        return pl.ds(base + side * PIECE + k * PART, PART)

    def load(m):
        hbm, ref = experts[m]
        return pltpu.make_async_copy(hbm, ref.at[own_rows], r.own_r.at[m // 2])

    def head_columns(h):
        return pl.ds(pl.multiple_of(h * 128, 128), 128)

    blocks = ((r.key, r.key_in), (r.value, r.value_in), (r.query, r.query_in))
    for whole, own in blocks:
        pltpu.make_async_copy(whole.at[:, head_columns(y)], own.at[y], r.load_r.at[0]).start()
    pltpu.make_async_copy(r.weight, r.proj.at[0], r.load_r.at[0]).start()
    small = (
        (r.rates_hbm, r.rates),
        (r.stream_hbm, r.stream),
        (r.gain_hbm, r.gain),
        (r.routes_hbm, r.routes),
        (r.router_hbm, r.router),
    )
    for n, (hbm, ref) in enumerate(small):
        pltpu.make_async_copy(hbm, ref, r.load_r.at[n + 1]).start()

    @pl.when(keeper)
    def _():
        for m in range(3):
            load(m).start()

    away = jnp.logical_not(keeper)
    batches = (((0, 1), (0, 1)), ((0, 1), (2, 3, 4)), ((0, 1), (5,)), ((2,), range(6)))

    def parts(batch):
        sides, numbers = batches[batch]
        return [(number // 2, number % 2, side) for number in numbers for side in sides]

    def swap(batch, numbers=range(6)):
        for m, k, side in parts(batch):
            if m * 2 + k in numbers:
                launch_if(
                    away,
                    lambda m=m, k=k, side=side: remote(
                        experts[m][0].at[part_rows(0, k, side)],
                        experts[m][1].at[part_rows(HIDDEN, k, side)],
                        r.swap_s.at[side // 2],
                        r.swap_r.at[batch],
                        swap_to[side],
                    ),
                )

    def pass_on(batch):
        @pl.when(away)
        def _():
            await_bytes(units(3 * len(parts(batch))), r.swap_r.at[batch])
            for m, k, side in parts(batch):
                ref = experts[m][1].at[part_rows(HIDDEN, k, side)]
                remote(ref, ref, r.pass_s.at[side // 2], r.pass_r.at[side // 2], partner).start()

    def weights_ready():
        await_bytes(r.gate, r.own_r.at[0])
        await_bytes(r.gate.at[own_rows], r.own_r.at[1])

        @pl.when(keeper)
        def _():
            await_bytes(r.gate, r.pass_r.at[0])
            await_bytes(r.gate.at[own_rows], r.pass_r.at[1])

    pl.semaphore_wait(barrier, NY - 1 + NZ - 1 + NX - 1 + NX + 3)

    for n, (whole, own) in enumerate(blocks):
        for d in (2, 1, 3):
            launch(
                remote(
                    whole.at[:, head_columns(ring_y(d))],
                    own.at[y],
                    r.early_s.at[0],
                    r.block_r.at[0 if n == 2 else d],
                    on_y(d),
                )
            )

    def shard(distance):
        return r.proj.at[SHARD_ORDER.index(distance % NZ)]

    def z_step(k):
        a, b, to_a, to_b = shard(1 - k), shard(k - 1), shard(-k), shard(k)
        if k == 1:
            a = b = r.weight
        if k == 4:
            a, to_a = a.at[pl.ds(0, 48)], to_a.at[pl.ds(0, 48)]
            b, to_b = b.at[pl.ds(48, 48)], to_b.at[pl.ds(48, 48)]
        launch(remote(a, to_a, r.early_s.at[0], r.proj_r.at[k - 1], on_z(1)))
        launch(remote(b, to_b, r.early_s.at[0], r.proj_r.at[k - 1], on_z(-1)))

    def z_wait(k):
        await_bytes(r.proj.at[pl.ds(0, 2 if k < 4 else 1)], r.proj_r.at[k - 1])

    z_step(1)
    swap(0, (0,))
    for m in range(3):
        launch_if(
            keeper,
            lambda m=m: remote(
                experts[m][0], experts[m][1].at[own_rows], r.own_s.at[m // 2], r.own_r.at[m // 2], partner
            ),
        )

    for n, (hbm, ref) in enumerate(small):
        await_bytes(ref, r.load_r.at[n + 1])
    await_bytes(units(2), r.load_r.at[0])
    rates = r.rates[...]
    length = r.query.shape[0]
    gap = (
        lax.broadcasted_iota(jnp.int32, (length, length), 0)
        - lax.broadcasted_iota(jnp.int32, (length, length), 1)
    ).astype(F32)
    position = lax.broadcasted_iota(jnp.int32, (length, 1), 0).astype(F32)
    lane = lax.broadcasted_iota(jnp.int32, rates.shape, 1)
    own_rate = jnp.sum(jnp.where(lane == y, rates, 0.0), axis=1, keepdims=True)

    square = lax.broadcasted_iota(jnp.int32, (16, 16), 0) == lax.broadcasted_iota(
        jnp.int32, (16, 16), 1
    )

    def upright(row):
        wide = jnp.where(square, jnp.broadcast_to(row, (16, 16)).astype(F32), 0.0)
        return jnp.sum(wide, axis=1, keepdims=True)

    table_lane = lax.broadcasted_iota(jnp.int32, (16, 128), 1)
    r.tables[ep] = jnp.where(
        table_lane == 0, upright(r.routes[0:1, :]), upright(r.routes[1:2, :])
    ).astype(jnp.int32)

    def gather(n, ref):
        block = ref.at[ep]
        for d in (2, 1, 3, 0):

            def make(d=d):
                device = at(z, y, ring_x(d), core)
                return remote(block, block, r.tok_s.at[n if d else n + 2], r.tok_r.at[n], device)

            if d:
                launch(make())
            else:
                launch_if(jnp.logical_not(source), make)

    gather(1, r.tables)

    def power(n):
        return jnp.exp(-own_rate * (128.0 * n))

    fade = jnp.exp(-own_rate * (length - 1.0 - position))
    for d in (0, 1, 3, 2):
        if d:
            await_bytes(r.key_in.at[pl.ds(0, 2)], r.block_r.at[d])
        i = ring_y(-d)
        faded = (r.key_in[i].astype(F32) * fade).astype(BF16)
        r.local[i] = tn_dot(faded, r.value_in[i])
    swap(0, (1,))
    total = r.local[3]
    for i in range(3):
        total = total + power(3 - i) * r.local[i]
    r.total_out[...] = total.astype(BF16)
    for d in range(NZ - 1, 0, -1):
        launch_if(
            z + d < NZ,
            lambda d=d: remote(
                r.total_out, r.total_in.at[z], r.total_s.at[0], r.total_r.at[0], on_z(d)
            ),
        )
    z_wait(1)
    z_step(2)
    decay = jnp.where(gap >= 0, jnp.exp(-own_rate * jnp.maximum(gap, 0.0)), 0.0)
    await_bytes(r.key_in.at[pl.ds(0, 3)], r.block_r.at[0])
    for i in range(NY):
        scores = nt_dot(r.query_in[i], r.key_in[i])
        r.intra[i] = dot((scores * decay).astype(BF16), r.value_in[i])
    r.entry[...] = jnp.zeros_like(r.entry)
    for d in range(1, NZ):

        @pl.when(z == d)
        def _(d=d):
            await_bytes(r.total_in.at[pl.ds(0, d)], r.total_r.at[0])

    for d in range(1, NZ):

        @pl.when(z >= d)
        def _(d=d):
            r.entry[...] += power(4 * (d - 1)) * r.total_in[ring_z(-d)].astype(F32)

    incoming = r.entry[...]
    fade = jnp.exp(-own_rate * (position + 1.0))
    for i in range(NY):
        mixed = r.intra[i] + fade * dot(r.query_in[i], incoming.astype(BF16))
        incoming = power(1) * incoming + r.local[i]
        mean = jnp.mean(mixed * mixed, axis=-1, keepdims=True)
        out = (mixed * lax.rsqrt(mean + EPSILON)).astype(BF16)
        r.heads[y, i] = out.reshape(4, 2, 16, 128)
    for d in (2, 1, 3):
        launch(remote(r.heads.at[y], r.heads.at[y], r.early_s.at[0], r.heads_r.at[0], on_y(d)))
    z_wait(2)
    z_step(3)

    z_wait(3)
    z_step(4)
    swap(3)
    low_lane = lax.broadcasted_iota(jnp.int32, (128, CHUNK), 1) < SLOTS

    def expert_of(rel, t):
        return x * 4 + t * 2 + (half if rel == 0 else 1 - half)

    @pl.when(source)
    def _():
        await_bytes(r.tables.at[pl.ds(0, 7)], r.tok_r.at[1])
        table = r.tables[...].reshape(128, 128)
        first, second = table[:, 0:1], table[:, 1:2]
        lanes = lax.broadcasted_iota(jnp.int32, (128, 128), 1)
        earlier = (lanes < lax.broadcasted_iota(jnp.int32, (128, 128), 0)).astype(BF16)
        pairs = [(1, 0), (1, 1), (0, 0), (0, 1)]
        hits = []
        for rel, t in pairs:
            expert = expert_of(rel, t)
            hits.append(jnp.where(jnp.logical_or(first == expert, second == expert), 1.0, 0.0))
        wide = jnp.zeros((128, 128), F32)
        for n, hit in enumerate(hits):
            wide = jnp.where(lanes == n, hit, wide)
        ranks = dot(earlier, wide.astype(BF16)).astype(jnp.int32)
        slot = lax.broadcasted_iota(jnp.int32, (128, CHUNK), 1)
        for n, (rel, t) in enumerate(pairs):
            rank = ranks[:, n : n + 1]
            low = jnp.where(slot == rank, hits[n], 0.0)
            low = jnp.where(low_lane, low, 0.0).astype(BF16)
            high = jnp.where(slot - SLOTS == rank, hits[n], 0.0).astype(BF16)
            r.sel[rel, t, 0] = low
            r.sel[rel, t, 1] = high
    await_bytes(r.heads.at[pl.ds(0, 3)], r.heads_r.at[0])
    swap(1)

    def project(which, n):
        lhs = jnp.concatenate([r.heads[h, :, :, which].reshape(256, 128) for h in range(4)], axis=1)
        rhs = r.proj[4 * n : 4 * (n + 1)].reshape(384, 512)
        return nt_dot(lhs, rhs).reshape(4, 4, 16, 384)

    for n in range(2):
        if n == 1:
            z_wait(4)
        r.pair_out[n] = project(1 - c, n).astype(BF16)
        launch(remote(r.pair_out.at[n], r.pair_in.at[n], r.early_s.at[0], r.pair_r.at[n], partner))
        r.part[n] = project(c, n)
        await_bytes(r.pair_in.at[n], r.pair_r.at[n])
        both = r.part[n] + r.pair_in[n].astype(F32)
        r.part[n] = both
        r.part_out[n] = both.astype(BF16)
        for d in (2, 1, 3):
            launch(
                remote(
                    r.part_out.at[n, :, ring_x(d)],
                    r.part_in.at[n, x],
                    r.early_s.at[0],
                    r.part_r.at[n],
                    on_x(d),
                )
            )
    pass_on(0)
    for n in range(2):
        slab = r.part[n, :, x]
        await_bytes(r.part_in.at[n, pl.ds(0, 3)], r.part_r.at[n])
        for d in (1, 3, 2):
            slab = slab + r.part_in[n, ring_x(-d)].astype(F32)
        r.slab[n] = slab
        r.slab_out[n] = slab.astype(BF16)
        for d in (2, 1, 3):
            launch(
                remote(
                    r.slab_out.at[n, ring_y(d)],
                    r.slab_in.at[n, y],
                    r.slab_s.at[0],
                    r.slab_r.at[0],
                    on_y(d),
                )
            )
    await_bytes(r.slab_in.at[:, pl.ds(0, 3)], r.slab_r.at[0])
    for n in range(2):
        for d in (1, 3, 2):
            r.slab[n, ring_y(-d)] = r.slab_in[n, ring_y(-d)].astype(F32)
    swap(2)
    def columns_of(yy):
        places = [SHARD_ORDER.index(distance) for distance in range(NZ)]
        ordered = [r.slab[p // 4, yy][:, SHARD * (p % 4) : SHARD * (p % 4 + 1)] for p in places]
        return pltpu.roll(jnp.concatenate(ordered, axis=1), z * SHARD, 1)

    quarters = [columns_of(yy) for yy in range(NY)]
    attended = jnp.concatenate(
        [
            quarters[yy][:, SHARD * zz : SHARD * (zz + 1)]
            for zz in range(NZ)
            for yy in range(NY)
        ],
        axis=1,
    )
    hidden = r.stream[...].astype(F32) + attended
    r.hidden[...] = hidden
    mean = jnp.mean(hidden * hidden, axis=-1, keepdims=True)
    r.tokens[ep] = (hidden * lax.rsqrt(mean + EPSILON) * r.gain[...]).astype(BF16)
    gather(0, r.tokens)

    pass_on(1)

    near = zl // 2
    edge = (zl * zl - 3 * zl + 2) // 2
    cross_to = at(lax.rem(4 * half + 7 - 3 * near, NZ), y, x, c)

    def lanes_of(ref, q):
        return ref.at[:, pl.ds(WIDTH * q, WIDTH)]

    def cross_copy(t, q):
        return remote(
            lanes_of(r.cross.at[t], q),
            lanes_of(r.line.at[t, 3 - near], q),
            r.cross_s.at[0],
            r.line_r.at[t, 3 - near, q],
            cross_to,
        )

    @pl.when(source)
    def _():
        await_bytes(r.tokens.at[pl.ds(0, 7)], r.tok_r.at[0])
        rows = r.tokens[...].reshape(128, DM)
        for n in range(2):
            low = jnp.concatenate([r.sel[1 - n, t, 0] for t in range(2)], axis=1)
            high = jnp.concatenate([r.sel[1 - n, t, 1] for t in range(2)], axis=1)
            both = (tn_dot(low, rows[:, :HALF]) + tn_dot(high, rows[:, HALF:])).astype(BF16)
            for t in range(2):
                chunk = both[CHUNK * t : CHUNK * (t + 1)]
                if n == 0:
                    r.cross[t] = chunk
                    for q in range(PIECES):
                        cross_copy(t, q).start()
                else:
                    r.line[t, near] = chunk

    swapped = edge * (core - c) * (core - c)
    order = [
        near + 2 * swapped,
        edge * (2 + near - 2 * swapped) + (1 - edge) * (1 - near),
        edge * (1 - near) + (1 - edge) * (2 + near),
        3 - near,
    ]

    other, side_end, far_end = 1 - near, 2 + near, 3 - near
    two_on = on_z(2 - 4 * near)

    def origin(s):
        outer = s // 2
        return (1 - outer) * (c + 2 * s) + outer * (5 * s - 11)

    def spread(i):
        s = order[i]
        o = origin(s)
        for t in range(2):
            block = r.line.at[t, s]
            for q in range(PIECES):
                piece = lanes_of(block, q)
                if i > 0:
                    await_bytes(piece, r.line_r.at[t, s, q])
                else:

                    @pl.when(jnp.logical_not(source))
                    def _(t=t, q=q, piece=piece):
                        await_bytes(piece, r.line_r.at[t, s, q])

                for side, condition in (
                    (0, jnp.logical_and(o <= zl, zl < 3)),
                    (1, jnp.logical_and(o >= zl, zl > 0)),
                ):
                    launch_if(
                        condition,
                        lambda piece=piece, t=t, s=s, q=q, side=side: remote(
                            piece,
                            piece,
                            r.line_s.at[0],
                            r.line_r.at[t, s, q],
                            on_z(-1 if side else 1),
                        ),
                    )
            straight = jnp.logical_and(role == t, s != far_end)
            for j, d, wanted in ((0, 2, straight), (1, 1, role != t), (2, -1, role != t)):
                launch_if(
                    wanted,
                    lambda block=block, s=s, j=j, d=d: remote(
                        block,
                        r.got.at[j, s],
                        r.row_s.at[0],
                        (r.got_r if j else r.far_r).at[s],
                        on_y(d),
                    ),
                )

    spread(0)
    spread(1)
    pass_on(2)
    pass_on(3)
    spread(2)
    spread(3)
    across = r.got.at[0, side_end]
    await_bytes(across, r.far_r.at[side_end])
    launch(remote(across, across, r.row_s.at[0], r.far_r.at[side_end], two_on))

    @pl.when(source)
    def _():
        logits = nt_dot(r.tokens[...].reshape(128, DM), r.router[...])
        table = r.tables[...].reshape(128, 128)
        first, second = table[:, 0:1], table[:, 1:2]
        expert = lax.broadcasted_iota(jnp.int32, logits.shape, 1)

        def lifted(chosen):
            logit = jnp.sum(jnp.where(expert == chosen, logits, 0.0), axis=1, keepdims=True)
            return jax.nn.sigmoid(logit)

        lift_first, lift_second = lifted(first), lifted(second)
        both = lift_first + lift_second
        for rel in range(2):
            for t in range(2):
                chosen = expert_of(rel, t)
                share = jnp.where(first == chosen, lift_first / both, 0.0) + jnp.where(
                    second == chosen, lift_second / both, 0.0
                )
                r.share[rel, t] = jnp.broadcast_to(share, (128, 128))

    third = side_end + swapped * (near - side_end)
    fourth = near + swapped * (side_end - near)

    def arrived(p):
        await_bytes(r.got.at[pl.ds(1, 2), p], r.got_r.at[p])
        if p is not side_end:
            await_bytes(r.got.at[0, p], r.far_r.at[p])

    def flatten(p, place):
        chunks = [r.line[role, p]] + [r.got[j, p] for j in range(3)]
        for n in range(2):
            a, b = chunks[2 * n].astype(F32), chunks[2 * n + 1].astype(F32)
            rows = slice(CHUNK * (2 * place + n), CHUNK * (2 * place + n + 1))
            r.flat[rows, :HALF] = jnp.concatenate([a[:SLOTS], b[:SLOTS]], axis=0).astype(BF16)
            r.flat[rows, HALF:] = jnp.concatenate([a[SLOTS:], b[SLOTS:]], axis=0).astype(BF16)

    def compute(which):
        rows = r.flat[...]
        gated = nt_dot(rows, r.gate[...])
        inner = (gated * jax.nn.sigmoid(gated) * nt_dot(rows, r.up[...])).astype(BF16)
        left = dot(inner, r.down[:, :HALF])
        right = dot(inner, r.down[:, HALF:])
        for n, p in enumerate(which):
            for j in range(4):
                rows = slice(SLOTS * (4 * n + j), SLOTS * (4 * n + j + 1))
                r.partial[j, p] = jnp.concatenate([left[rows], right[rows]], axis=0).astype(BF16)

    def give_back(p, ways=(0, 1, 2)):
        for j in ways:
            d = (2, -1, 1)[j]
            launch(
                remote(
                    r.partial.at[j + 1, p], r.back.at[j, p], r.row_s.at[0], r.back_r.at[p], on_y(d)
                )
            )

    arrived(near)
    flatten(near, 0)
    weights_ready()
    arrived(other)
    flatten(other, 1)
    compute((near, other))
    give_back(other)
    arrived(side_end)
    flatten(side_end, 1)
    arrived(far_end)
    flatten(far_end, 0)
    compute((far_end, side_end))
    launch(remote(r.partial.at[1, far_end], r.extra, r.row_s.at[0], r.extra_r.at[0], two_on))
    give_back(far_end, (1, 2))
    give_back(side_end, (1, 2))

    def collect(p):
        if p is far_end:
            await_bytes(r.back.at[pl.ds(1, 2), p], r.back_r.at[p])
            r.total[role, p] = r.partial[0, p].astype(F32)
        else:
            await_bytes(r.back.at[:, p], r.back_r.at[p])
            r.total[role, p] = r.partial[0, p].astype(F32) + r.back[0, p].astype(F32)
        r.total[1 - role, p] = r.back[1, p].astype(F32) + r.back[2, p].astype(F32)

    ends = (at(lax.rem(4 * half + 4 + c, NZ), y, x, c), at(lax.rem(4 * half + 6 + c, NZ), y, x, c))

    def stream(s, place, side):
        here = 1 - lax.min(1, (origin(s) - place) * (origin(s) - place))
        return s + here * side * (4 - s)

    def along(s):
        o = origin(s)
        for t in range(2):
            for q in range(PIECES):
                cols = slice(WIDTH * q, WIDTH * (q + 1))
                out = lanes_of(r.line_out.at[t, s], q)

                def add_line(side, t=t, q=q, cols=cols):
                    block = lanes_of(r.line_in.at[side, t, s], q)
                    await_bytes(block, r.sum_r.at[t, stream(s, zl, side), q])
                    r.total[t, s, :, cols] += r.line_in[side, t, s, :, cols].astype(F32)

                @pl.when(jnp.logical_and(o >= zl, zl > 0))
                def _(add_line=add_line):
                    add_line(0)

                @pl.when(jnp.logical_and(o <= zl, zl < 3))
                def _(add_line=add_line):
                    add_line(1)

                r.line_out[t, s, :, cols] = r.total[t, s, :, cols].astype(BF16)
                for side, wanted, last in ((0, o > zl, zl == 3), (1, o < zl, zl == 0)):
                    launch_if(
                        jnp.logical_and(wanted, jnp.logical_not(last)),
                        lambda out=out, t=t, s=s, q=q, side=side: remote(
                            out,
                            lanes_of(r.line_in.at[side, t, s], q),
                            r.sum_s.at[0],
                            r.sum_r.at[t, stream(s, zl + 1 - 2 * side, side), q],
                            on_z(-1 if side else 1),
                        ),
                    )
                    launch_if(
                        jnp.logical_and(wanted, last),
                        lambda out=out, t=t, s=s, q=q, side=side: remote(
                            out,
                            lanes_of(r.ret.at[t], q),
                            r.sum_s.at[0],
                            r.ret_r.at[0],
                            ends[side],
                        ),
                    )

    @pl.when(edge == 1)
    def _():
        collect(other)
        along(other)

    await_bytes(r.extra, r.extra_r.at[0])
    joined = r.partial[1, side_end].astype(F32) + r.extra[...].astype(F32)
    r.partial[1, side_end] = joined.astype(BF16)
    give_back(side_end, (0,))
    give_back(near)

    @pl.when(edge == 0)
    def _():
        collect(other)
        along(other)

    for p in (far_end, third, fourth):
        collect(p)
        along(p)

    def home_copy(side, d, cc):
        cols = pl.ds(HALF * side, HALF)
        return remote(
            r.home_out.at[ring_x(d), cc, :, cols],
            r.home_in.at[x, :, cols],
            r.home_s.at[0],
            r.home_r.at[1 if d else 0],
            at(z, y, ring_x(d), cc),
        )

    home_targets = [(d, other) for d in (2, 1, 3) for other in range(2)] + [(0, 1 - c)]

    @pl.when(source)
    def _():
        for side in range(2):
            cols = slice(HALF * side, HALF * (side + 1))
            value = None
            for rel in range(2):
                for t in range(2):
                    if rel == 1 and side == 0 and t == 0:
                        await_bytes(r.ret, r.ret_r.at[0])
                    rows = r.ret[t] if rel else r.line_out[t, near]
                    term = r.share[rel, t][:, 0:1] * dot(r.sel[rel, t, side], rows)
                    value = term if value is None else value + term
            value = value.reshape(4, 2, 16, HALF)
            r.mixed[:, :, :, cols] = value
            r.home_out[:, :, :, cols] = value.astype(BF16)
            for d, cc in home_targets:
                home_copy(side, d, cc).start()
        r.home[...] = r.mixed[x, c]

    @pl.when(jnp.logical_not(source))
    def _():
        await_bytes(r.home_in.at[0], r.home_r.at[0])
        r.home[...] = r.home_in[x].astype(F32)

    result = r.hidden[...] + r.home[...]
    await_bytes(r.home_in.at[pl.ds(0, 3)], r.home_r.at[1])
    for d in (1, 3, 2):
        result = result + r.home_in[ring_x(-d)].astype(F32)
    r.out[...] = result.astype(BF16)

    await_bytes(units(21), r.early_s.at[0])
    await_bytes(r.slab_out.at[:, pl.ds(0, 3)], r.slab_s.at[0])
    await_bytes(units(36), r.row_s.at[0])
    for n, ref in enumerate((r.tokens, r.tables)):
        await_bytes(ref.at[pl.ds(0, 3)], r.tok_s.at[n])
    for d in range(1, NZ):

        @pl.when(z + d == NZ - 1)
        def _(d=d):
            await_bytes(r.total_in.at[pl.ds(0, d)], r.total_s.at[0])

    @pl.when(keeper)
    def _():
        await_bytes(r.gate, r.own_s.at[0])
        await_bytes(r.gate.at[own_rows], r.own_s.at[1])

    @pl.when(away)
    def _():
        for semaphore in (r.swap_s, r.pass_s):
            await_bytes(r.gate, semaphore.at[0])
            await_bytes(r.gate.at[own_rows], semaphore.at[1])

    @pl.when(source)
    def _():
        await_bytes(units(3), r.cross_s.at[0])
        await_bytes(units(9), r.sum_s.at[0])
        await_bytes(units(7), r.home_s.at[0])

    @pl.when(jnp.logical_not(source))
    def _():
        for n, ref in enumerate((r.tokens, r.tables)):
            await_bytes(ref.at[0], r.tok_s.at[n + 2])
        await_bytes(units(12), r.sum_s.at[0])

    forwards = sum(
        jnp.where(jnp.logical_and(origin(s) <= zl, zl < 3), 1, 0)
        + jnp.where(jnp.logical_and(origin(s) >= zl, zl > 0), 1, 0)
        for s in range(4)
    )
    for n in range(1, 9):

        @pl.when(forwards == n)
        def _(n=n):
            await_bytes(units(3 * n), r.line_s.at[0])


VMEM = pl.BlockSpec(memory_space=pltpu.VMEM)
ANY = pl.BlockSpec(memory_space=pl.ANY)


def body(
    stream,
    query,
    key,
    value,
    decay_rate,
    out_weight,
    norm_gain,
    router_weight,
    routes,
    expert_gate,
    expert_up,
    expert_down,
):
    return pl.pallas_call(
        kernel,
        out_shape=jax.ShapeDtypeStruct(stream.shape, BF16),
        in_specs=[ANY] * 12,
        out_specs=VMEM,
        scratch_shapes=list(SCRATCH.values()),
        compiler_params=pltpu.CompilerParams(
            collective_id=0, has_side_effects=True, vmem_limit_bytes=56 * 2**20
        ),
        name="whole",
    )(
        stream,
        query,
        key,
        value,
        decay_rate.reshape(1, 4),
        out_weight.T,
        norm_gain.reshape(1, DM),
        routes.T,
        router_weight.T,
        expert_gate.T,
        expert_up.T,
        expert_down,
    )


def solution(mesh):
    placed = (
        P(("ctx", "ep"), None),
        P("ctx", "ep"),
        P("ctx", "ep"),
        P("ctx", "ep"),
        P("ep"),
        P("ep", "ctx"),
        P(),
        P(),
        P(("ctx", "ep"), None),
        P(None, ("ep", "ctx")),
        P(None, ("ep", "ctx")),
        P(("ep", "ctx"), None),
    )
    return jax.shard_map(
        body, mesh=mesh, in_specs=placed, out_specs=P(("ctx", "ep"), None), check_vma=False
    )
```

```python
import jax
import jax.numpy as jnp
from jax import lax
from jax.experimental import pallas as pl
from jax.experimental.pallas import tpu as pltpu
from jax.sharding import PartitionSpec as P

EPSILON = 1e-06
MESH = pl.DeviceIdType.MESH
F32 = jnp.float32
BF16 = jnp.bfloat16
NY = 4
NZ = 8
NX = 4
DM = 3072
HALF = 1536
SLOTS = 24
CHUNK = 48
SHARD = 96
HIDDEN = 288
PIECES = 3
WIDTH = HALF // PIECES
PIECE = 96
PART = 48
SHARD_ORDER = (0, 1, 7, 2, 6, 3, 5, 4)


def bf(*shape):
    return pltpu.VMEM(shape, BF16)


def fl(*shape):
    return pltpu.VMEM(shape, F32)


def dma(*shape):
    return pltpu.SemaphoreType.DMA(shape)


INPUTS = (
    "stream_hbm", "query", "key", "value", "rates_hbm", "weight", "gain_hbm", "routes_hbm",
    "router_hbm", "gate_hbm", "up_hbm", "down_hbm", "out",
)
SCRATCH = dict(
    stream=bf(16, DM),
    rates=fl(1, 4),
    gain=fl(1, DM),
    routes=pltpu.VMEM((2, 16), jnp.int32),
    router=bf(16, DM),
    intra=fl(4, 128, 128),
    key_in=bf(4, 128, 128),
    value_in=bf(4, 128, 128),
    query_in=bf(4, 128, 128),
    local=fl(4, 128, 128),
    total_out=bf(128, 128),
    total_in=bf(8, 128, 128),
    entry=fl(128, 128),
    proj=bf(8, SHARD, 512),
    heads=bf(4, 4, 4, 2, 16, 128),
    pair_out=bf(2, 4, 4, 16, 384),
    pair_in=bf(2, 4, 4, 16, 384),
    part=fl(2, 4, 4, 16, 384),
    part_out=bf(2, 4, 4, 16, 384),
    part_in=bf(2, 4, 4, 16, 384),
    slab=fl(2, 4, 16, 384),
    slab_out=bf(2, 4, 16, 384),
    slab_in=bf(2, 4, 16, 384),
    hidden=fl(16, DM),
    tokens=bf(8, 16, DM),
    tables=pltpu.VMEM((8, 16, 128), jnp.int32),
    gate=bf(2 * HIDDEN, DM),
    up=bf(2 * HIDDEN, DM),
    down=bf(2 * HIDDEN, DM),
    sel=bf(2, 2, 2, 128, CHUNK),
    weighted=bf(2, 128, 8 * CHUNK),
    cross=bf(2, CHUNK, HALF),
    line=bf(2, 4, CHUNK, HALF),
    got=bf(3, 4, CHUNK, HALF),
    flat=bf(192, DM),
    partial=bf(4, 4, CHUNK, HALF),
    back=bf(3, 4, CHUNK, HALF),
    extra=bf(CHUNK, HALF),
    total=fl(2, 4, CHUNK, HALF),
    line_out=bf(2, 4, CHUNK, HALF),
    line_in=bf(2, 2, 4, CHUNK, HALF),
    ret=bf(2, CHUNK, HALF),
    mixed=fl(4, 2, 16, DM),
    home_out=bf(4, 2, 16, DM),
    home_in=bf(4, 16, DM),
    home=fl(16, DM),
    load_r=dma(6), early_s=dma(1), slab_s=dma(1), tok_s=dma(4), total_s=dma(1), own_s=dma(2),
    swap_s=dma(2), pass_s=dma(2), cross_s=dma(1), line_s=dma(1), row_s=dma(1), sum_s=dma(1),
    home_s=dma(1),
    block_r=dma(4), total_r=dma(1), proj_r=dma(4), heads_r=dma(1), pair_r=dma(2), part_r=dma(2),
    slab_r=dma(1), tok_r=dma(2), own_r=dma(2), swap_r=dma(4), pass_r=dma(2),
    line_r=dma(2, 4, PIECES), got_r=dma(4), far_r=dma(4), back_r=dma(4), extra_r=dma(1), sum_r=dma(2, 5, PIECES), ret_r=dma(1),
    home_r=dma(2),
)


class Refs:
    def __init__(self, refs):
        for name, ref in zip(INPUTS + tuple(SCRATCH), refs, strict=True):
            setattr(self, name, ref)


def at(z, y, x, c):
    return (z * NY + y, x * 2 + c)


def remote(src, dst, send, recv, device):
    return pltpu.make_async_remote_copy(
        src_ref=src,
        dst_ref=dst,
        send_sem=send,
        recv_sem=recv,
        device_id=device,
        device_id_type=MESH,
    )


def await_bytes(ref, semaphore):
    pltpu.make_async_copy(ref, ref, semaphore).wait()


def greet(barrier, devices):
    for device in devices:
        pl.semaphore_signal(barrier, inc=1, device_id=device, device_id_type=MESH)


def nt_dot(a, b):
    return lax.dot_general(a, b, (((1,), (1,)), ((), ())), preferred_element_type=F32)


def tn_dot(a, b):
    return lax.dot_general(a, b, (((0,), (0,)), ((), ())), preferred_element_type=F32)


def dot(a, b):
    return jnp.dot(a, b, preferred_element_type=F32)


def kernel(*refs):
    r = Refs(refs)
    ctx = lax.axis_index("ctx")
    ep = lax.axis_index("ep")
    z, y, x, c = ctx // NY, ctx % NY, ep // 2, ep % 2
    half, zl = z // 4, z % 4
    role = (y + z) % 2
    source = z % 2 == c
    keeper = c == role
    core = z % 2

    def ring_y(d):
        return lax.rem(y + d + NY, NY)

    def ring_z(d):
        return lax.rem(z + d + NZ, NZ)

    def ring_x(d):
        return lax.rem(x + d + NX, NX)

    def on_y(d):
        return at(z, ring_y(d), x, c)

    def on_z(d):
        return at(ring_z(d), y, x, c)

    def on_x(d):
        return at(z, y, ring_x(d), c)

    partner = at(z, y, x, 1 - c)
    beside = z + 1 - 2 * (z % 2)
    swap_to = (
        at(z, ring_y(1), x, 1 - c),
        at(z, ring_y(-1), x, 1 - c),
        at(beside, y, x, 1 - c),
    )
    barrier = pltpu.get_barrier_semaphore()
    greet(barrier, [on_y(d) for d in range(1, NY)])
    greet(barrier, [on_z(d) for d in range(1, NZ)])
    greet(barrier, [on_x(d) for d in range(1, NX)])
    greet(barrier, [at(z, y, ring_x(d), 1 - c) for d in range(NX)])
    greet(barrier, swap_to)

    def launch(copy):
        copy.start()

    def launch_if(condition, make):
        @pl.when(condition)
        def _():
            make().start()

    def units(n):
        return r.gate.at[pl.ds(0, 16 * n)]

    experts = ((r.gate_hbm, r.gate), (r.up_hbm, r.up), (r.down_hbm, r.down))
    own_rows = pl.ds(0, HIDDEN)

    def part_rows(base, k, side):
        return pl.ds(base + side * PIECE + k * PART, PART)

    def load(m):
        hbm, ref = experts[m]
        return pltpu.make_async_copy(hbm, ref.at[own_rows], r.own_r.at[m // 2])

    def head_columns(h):
        return pl.ds(pl.multiple_of(h * 128, 128), 128)

    blocks = ((r.key, r.key_in), (r.value, r.value_in), (r.query, r.query_in))
    for whole, own in blocks:
        pltpu.make_async_copy(whole.at[:, head_columns(y)], own.at[y], r.load_r.at[0]).start()
    pltpu.make_async_copy(r.weight, r.proj.at[0], r.load_r.at[0]).start()
    small = (
        (r.rates_hbm, r.rates),
        (r.stream_hbm, r.stream),
        (r.gain_hbm, r.gain),
        (r.routes_hbm, r.routes),
        (r.router_hbm, r.router),
    )
    for n, (hbm, ref) in enumerate(small):
        pltpu.make_async_copy(hbm, ref, r.load_r.at[n + 1]).start()

    @pl.when(keeper)
    def _():
        for m in range(3):
            load(m).start()

    away = jnp.logical_not(keeper)
    batches = (((0, 1), (0, 1)), ((0, 1), (2, 3, 4)), ((0, 1), (5,)), ((2,), range(6)))

    def parts(batch):
        sides, numbers = batches[batch]
        return [(number // 2, number % 2, side) for number in numbers for side in sides]

    def swap(batch, numbers=range(6)):
        for m, k, side in parts(batch):
            if m * 2 + k in numbers:
                launch_if(
                    away,
                    lambda m=m, k=k, side=side: remote(
                        experts[m][0].at[part_rows(0, k, side)],
                        experts[m][1].at[part_rows(HIDDEN, k, side)],
                        r.swap_s.at[side // 2],
                        r.swap_r.at[batch],
                        swap_to[side],
                    ),
                )

    def pass_on(batch):
        @pl.when(away)
        def _():
            await_bytes(units(3 * len(parts(batch))), r.swap_r.at[batch])
            for m, k, side in parts(batch):
                ref = experts[m][1].at[part_rows(HIDDEN, k, side)]
                remote(ref, ref, r.pass_s.at[side // 2], r.pass_r.at[side // 2], partner).start()

    def weights_ready():
        await_bytes(r.gate, r.own_r.at[0])
        await_bytes(r.gate.at[own_rows], r.own_r.at[1])

        @pl.when(keeper)
        def _():
            await_bytes(r.gate, r.pass_r.at[0])
            await_bytes(r.gate.at[own_rows], r.pass_r.at[1])

    pl.semaphore_wait(barrier, NY - 1 + NZ - 1 + NX - 1 + NX + 3)

    for n, (whole, own) in enumerate(blocks):
        for d in (2, 1, 3):
            launch(
                remote(
                    whole.at[:, head_columns(ring_y(d))],
                    own.at[y],
                    r.early_s.at[0],
                    r.block_r.at[0 if n == 2 else d],
                    on_y(d),
                )
            )

    def shard(distance):
        return r.proj.at[SHARD_ORDER.index(distance % NZ)]

    def z_step(k):
        a, b, to_a, to_b = shard(1 - k), shard(k - 1), shard(-k), shard(k)
        if k == 1:
            a = b = r.weight
        if k == 4:
            a, to_a = a.at[pl.ds(0, 48)], to_a.at[pl.ds(0, 48)]
            b, to_b = b.at[pl.ds(48, 48)], to_b.at[pl.ds(48, 48)]
        launch(remote(a, to_a, r.early_s.at[0], r.proj_r.at[k - 1], on_z(1)))
        launch(remote(b, to_b, r.early_s.at[0], r.proj_r.at[k - 1], on_z(-1)))

    def z_wait(k):
        await_bytes(r.proj.at[pl.ds(0, 2 if k < 4 else 1)], r.proj_r.at[k - 1])

    z_step(1)
    swap(0, (0,))
    for m in range(3):
        launch_if(
            keeper,
            lambda m=m: remote(
                experts[m][0], experts[m][1].at[own_rows], r.own_s.at[m // 2], r.own_r.at[m // 2], partner
            ),
        )

    for n, (hbm, ref) in enumerate(small):
        await_bytes(ref, r.load_r.at[n + 1])
    await_bytes(units(2), r.load_r.at[0])
    rates = r.rates[...]
    length = r.query.shape[0]
    gap = (
        lax.broadcasted_iota(jnp.int32, (length, length), 0)
        - lax.broadcasted_iota(jnp.int32, (length, length), 1)
    ).astype(F32)
    position = lax.broadcasted_iota(jnp.int32, (length, 1), 0).astype(F32)
    lane = lax.broadcasted_iota(jnp.int32, rates.shape, 1)
    own_rate = jnp.sum(jnp.where(lane == y, rates, 0.0), axis=1, keepdims=True)

    square = lax.broadcasted_iota(jnp.int32, (16, 16), 0) == lax.broadcasted_iota(
        jnp.int32, (16, 16), 1
    )

    def upright(row):
        wide = jnp.where(square, jnp.broadcast_to(row, (16, 16)).astype(F32), 0.0)
        return jnp.sum(wide, axis=1, keepdims=True)

    table_lane = lax.broadcasted_iota(jnp.int32, (16, 128), 1)
    r.tables[ep] = jnp.where(
        table_lane == 0, upright(r.routes[0:1, :]), upright(r.routes[1:2, :])
    ).astype(jnp.int32)

    def gather(n, ref):
        block = ref.at[ep]
        for d in (2, 1, 3, 0):

            def make(d=d):
                device = at(z, y, ring_x(d), core)
                return remote(block, block, r.tok_s.at[n if d else n + 2], r.tok_r.at[n], device)

            if d:
                launch(make())
            else:
                launch_if(jnp.logical_not(source), make)

    gather(1, r.tables)

    def power(n):
        return jnp.exp(-own_rate * (128.0 * n))

    fade = jnp.exp(-own_rate * (length - 1.0 - position))
    for d in (0, 1, 3, 2):
        if d:
            await_bytes(r.key_in.at[pl.ds(0, 2)], r.block_r.at[d])
        i = ring_y(-d)
        faded = (r.key_in[i].astype(F32) * fade).astype(BF16)
        r.local[i] = tn_dot(faded, r.value_in[i])
    swap(0, (1,))
    total = r.local[3]
    for i in range(3):
        total = total + power(3 - i) * r.local[i]
    r.total_out[...] = total.astype(BF16)
    for d in range(NZ - 1, 0, -1):
        launch_if(
            z + d < NZ,
            lambda d=d: remote(
                r.total_out, r.total_in.at[z], r.total_s.at[0], r.total_r.at[0], on_z(d)
            ),
        )
    z_wait(1)
    z_step(2)
    decay = jnp.where(gap >= 0, jnp.exp(-own_rate * jnp.maximum(gap, 0.0)), 0.0)
    await_bytes(r.key_in.at[pl.ds(0, 3)], r.block_r.at[0])
    for i in range(NY):
        scores = nt_dot(r.query_in[i], r.key_in[i])
        r.intra[i] = dot((scores * decay).astype(BF16), r.value_in[i])
    r.entry[...] = jnp.zeros_like(r.entry)
    for d in range(1, NZ):

        @pl.when(z == d)
        def _(d=d):
            await_bytes(r.total_in.at[pl.ds(0, d)], r.total_r.at[0])

    for d in range(1, NZ):

        @pl.when(z >= d)
        def _(d=d):
            r.entry[...] += power(4 * (d - 1)) * r.total_in[ring_z(-d)].astype(F32)

    incoming = r.entry[...]
    fade = jnp.exp(-own_rate * (position + 1.0))
    for i in range(NY):
        mixed = r.intra[i] + fade * dot(r.query_in[i], incoming.astype(BF16))
        incoming = power(1) * incoming + r.local[i]
        mean = jnp.mean(mixed * mixed, axis=-1, keepdims=True)
        out = (mixed * lax.rsqrt(mean + EPSILON)).astype(BF16)
        r.heads[y, i] = out.reshape(4, 2, 16, 128)
    for d in (2, 1, 3):
        launch(remote(r.heads.at[y], r.heads.at[y], r.early_s.at[0], r.heads_r.at[0], on_y(d)))
    z_wait(2)
    z_step(3)

    z_wait(3)
    z_step(4)
    swap(3)
    low_lane = lax.broadcasted_iota(jnp.int32, (128, CHUNK), 1) < SLOTS

    def expert_of(rel, t):
        return x * 4 + t * 2 + (half if rel == 0 else 1 - half)

    @pl.when(source)
    def _():
        await_bytes(r.tables.at[pl.ds(0, 7)], r.tok_r.at[1])
        table = r.tables[...].reshape(128, 128)
        first, second = table[:, 0:1], table[:, 1:2]
        lanes = lax.broadcasted_iota(jnp.int32, (128, 128), 1)
        earlier = (lanes < lax.broadcasted_iota(jnp.int32, (128, 128), 0)).astype(BF16)
        pairs = [(1, 0), (1, 1), (0, 0), (0, 1)]
        hits = []
        for rel, t in pairs:
            expert = expert_of(rel, t)
            hits.append(jnp.where(jnp.logical_or(first == expert, second == expert), 1.0, 0.0))
        wide = jnp.zeros((128, 128), F32)
        for n, hit in enumerate(hits):
            wide = jnp.where(lanes == n, hit, wide)
        ranks = dot(earlier, wide.astype(BF16)).astype(jnp.int32)
        slot = lax.broadcasted_iota(jnp.int32, (128, CHUNK), 1)
        for n, (rel, t) in enumerate(pairs):
            rank = ranks[:, n : n + 1]
            low = jnp.where(slot == rank, hits[n], 0.0)
            low = jnp.where(low_lane, low, 0.0).astype(BF16)
            high = jnp.where(slot - SLOTS == rank, hits[n], 0.0).astype(BF16)
            r.sel[rel, t, 0] = low
            r.sel[rel, t, 1] = high
    await_bytes(r.heads.at[pl.ds(0, 3)], r.heads_r.at[0])
    swap(1)

    def project(which, n):
        lhs = jnp.concatenate([r.heads[h, :, :, which].reshape(256, 128) for h in range(4)], axis=1)
        rhs = r.proj[4 * n : 4 * (n + 1)].reshape(384, 512)
        return nt_dot(lhs, rhs).reshape(4, 4, 16, 384)

    for n in range(2):
        if n == 1:
            z_wait(4)
        r.pair_out[n] = project(1 - c, n).astype(BF16)
        launch(remote(r.pair_out.at[n], r.pair_in.at[n], r.early_s.at[0], r.pair_r.at[n], partner))
        r.part[n] = project(c, n)
        await_bytes(r.pair_in.at[n], r.pair_r.at[n])
        both = r.part[n] + r.pair_in[n].astype(F32)
        r.part[n] = both
        r.part_out[n] = both.astype(BF16)
        for d in (2, 1, 3):
            launch(
                remote(
                    r.part_out.at[n, :, ring_x(d)],
                    r.part_in.at[n, x],
                    r.early_s.at[0],
                    r.part_r.at[n],
                    on_x(d),
                )
            )
    pass_on(0)
    for n in range(2):
        slab = r.part[n, :, x]
        await_bytes(r.part_in.at[n, pl.ds(0, 3)], r.part_r.at[n])
        for d in (1, 3, 2):
            slab = slab + r.part_in[n, ring_x(-d)].astype(F32)
        r.slab[n] = slab
        r.slab_out[n] = slab.astype(BF16)
        for d in (2, 1, 3):
            launch(
                remote(
                    r.slab_out.at[n, ring_y(d)],
                    r.slab_in.at[n, y],
                    r.slab_s.at[0],
                    r.slab_r.at[0],
                    on_y(d),
                )
            )
    await_bytes(r.slab_in.at[:, pl.ds(0, 3)], r.slab_r.at[0])
    for n in range(2):
        for d in (1, 3, 2):
            r.slab[n, ring_y(-d)] = r.slab_in[n, ring_y(-d)].astype(F32)
    swap(2)
    def columns_of(yy):
        places = [SHARD_ORDER.index(distance) for distance in range(NZ)]
        ordered = [r.slab[p // 4, yy][:, SHARD * (p % 4) : SHARD * (p % 4 + 1)] for p in places]
        return pltpu.roll(jnp.concatenate(ordered, axis=1), z * SHARD, 1)

    quarters = [columns_of(yy) for yy in range(NY)]
    attended = jnp.concatenate(
        [
            quarters[yy][:, SHARD * zz : SHARD * (zz + 1)]
            for zz in range(NZ)
            for yy in range(NY)
        ],
        axis=1,
    )
    hidden = r.stream[...].astype(F32) + attended
    r.hidden[...] = hidden
    mean = jnp.mean(hidden * hidden, axis=-1, keepdims=True)
    r.tokens[ep] = (hidden * lax.rsqrt(mean + EPSILON) * r.gain[...]).astype(BF16)
    gather(0, r.tokens)

    pass_on(1)

    near = zl // 2
    edge = (zl * zl - 3 * zl + 2) // 2
    cross_to = at(lax.rem(4 * half + 7 - 3 * near, NZ), y, x, c)

    def lanes_of(ref, q):
        return ref.at[:, pl.ds(WIDTH * q, WIDTH)]

    def cross_copy(t, q):
        return remote(
            lanes_of(r.cross.at[t], q),
            lanes_of(r.line.at[t, 3 - near], q),
            r.cross_s.at[0],
            r.line_r.at[t, 3 - near, q],
            cross_to,
        )

    @pl.when(source)
    def _():
        await_bytes(r.tokens.at[pl.ds(0, 7)], r.tok_r.at[0])
        rows = r.tokens[...].reshape(128, DM)
        for n in range(2):
            low = jnp.concatenate([r.sel[1 - n, t, 0] for t in range(2)], axis=1)
            high = jnp.concatenate([r.sel[1 - n, t, 1] for t in range(2)], axis=1)
            both = (tn_dot(low, rows[:, :HALF]) + tn_dot(high, rows[:, HALF:])).astype(BF16)
            for t in range(2):
                chunk = both[CHUNK * t : CHUNK * (t + 1)]
                if n == 0:
                    r.cross[t] = chunk
                    for q in range(PIECES):
                        cross_copy(t, q).start()
                else:
                    r.line[t, near] = chunk

    swapped = edge * (core - c) * (core - c)
    order = [
        near + 2 * swapped,
        edge * (2 + near - 2 * swapped) + (1 - edge) * (1 - near),
        edge * (1 - near) + (1 - edge) * (2 + near),
        3 - near,
    ]

    other, side_end, far_end = 1 - near, 2 + near, 3 - near
    two_on = on_z(2 - 4 * near)

    def origin(s):
        outer = s // 2
        return (1 - outer) * (c + 2 * s) + outer * (5 * s - 11)

    def spread(i):
        s = order[i]
        o = origin(s)
        for t in range(2):
            block = r.line.at[t, s]
            for q in range(PIECES):
                piece = lanes_of(block, q)
                if i > 0:
                    await_bytes(piece, r.line_r.at[t, s, q])
                else:

                    @pl.when(jnp.logical_not(source))
                    def _(t=t, q=q, piece=piece):
                        await_bytes(piece, r.line_r.at[t, s, q])

                for side, condition in (
                    (0, jnp.logical_and(o <= zl, zl < 3)),
                    (1, jnp.logical_and(o >= zl, zl > 0)),
                ):
                    launch_if(
                        condition,
                        lambda piece=piece, t=t, s=s, q=q, side=side: remote(
                            piece,
                            piece,
                            r.line_s.at[0],
                            r.line_r.at[t, s, q],
                            on_z(-1 if side else 1),
                        ),
                    )
            straight = jnp.logical_and(role == t, s != far_end)
            for j, d, wanted in ((0, 2, straight), (1, 1, role != t), (2, -1, role != t)):
                launch_if(
                    wanted,
                    lambda block=block, s=s, j=j, d=d: remote(
                        block,
                        r.got.at[j, s],
                        r.row_s.at[0],
                        (r.got_r if j else r.far_r).at[s],
                        on_y(d),
                    ),
                )

    spread(0)
    spread(1)
    pass_on(2)
    pass_on(3)
    spread(2)
    spread(3)
    across = r.got.at[0, side_end]
    await_bytes(across, r.far_r.at[side_end])
    launch(remote(across, across, r.row_s.at[0], r.far_r.at[side_end], two_on))

    @pl.when(source)
    def _():
        logits = nt_dot(r.tokens[...].reshape(128, DM), r.router[...])
        table = r.tables[...].reshape(128, 128)
        first, second = table[:, 0:1], table[:, 1:2]
        expert = lax.broadcasted_iota(jnp.int32, logits.shape, 1)

        def lifted(chosen):
            logit = jnp.sum(jnp.where(expert == chosen, logits, 0.0), axis=1, keepdims=True)
            return jax.nn.sigmoid(logit)

        lift_first, lift_second = lifted(first), lifted(second)
        both = lift_first + lift_second
        shares = []
        for rel in range(2):
            for t in range(2):
                chosen = expert_of(rel, t)
                share = jnp.where(first == chosen, lift_first / both, 0.0) + jnp.where(
                    second == chosen, lift_second / both, 0.0
                )
                shares.append(share)
        for side in range(2):
            wide = jnp.concatenate(
                [r.sel[n // 2, n % 2, side].astype(F32) * shares[n] for n in range(4)], axis=1
            )
            high = wide.astype(BF16)
            low = (wide - high.astype(F32)).astype(BF16)
            r.weighted[side] = jnp.concatenate([high, low], axis=1)

    third = side_end + swapped * (near - side_end)
    fourth = near + swapped * (side_end - near)

    def arrived(p):
        await_bytes(r.got.at[pl.ds(1, 2), p], r.got_r.at[p])
        if p is not side_end:
            await_bytes(r.got.at[0, p], r.far_r.at[p])

    def flatten(p, place):
        chunks = [r.line[role, p]] + [r.got[j, p] for j in range(3)]
        for n in range(2):
            a, b = chunks[2 * n].astype(F32), chunks[2 * n + 1].astype(F32)
            rows = slice(CHUNK * (2 * place + n), CHUNK * (2 * place + n + 1))
            r.flat[rows, :HALF] = jnp.concatenate([a[:SLOTS], b[:SLOTS]], axis=0).astype(BF16)
            r.flat[rows, HALF:] = jnp.concatenate([a[SLOTS:], b[SLOTS:]], axis=0).astype(BF16)

    def compute(which):
        rows = r.flat[...]
        gated = nt_dot(rows, r.gate[...])
        inner = (gated * jax.nn.sigmoid(gated) * nt_dot(rows, r.up[...])).astype(BF16)
        left = dot(inner, r.down[:, :HALF])
        right = dot(inner, r.down[:, HALF:])
        for n, p in enumerate(which):
            for j in range(4):
                rows = slice(SLOTS * (4 * n + j), SLOTS * (4 * n + j + 1))
                r.partial[j, p] = jnp.concatenate([left[rows], right[rows]], axis=0).astype(BF16)

    def give_back(p, ways=(0, 1, 2)):
        for j in ways:
            d = (2, -1, 1)[j]
            launch(
                remote(
                    r.partial.at[j + 1, p], r.back.at[j, p], r.row_s.at[0], r.back_r.at[p], on_y(d)
                )
            )

    arrived(near)
    flatten(near, 0)
    weights_ready()
    arrived(other)
    flatten(other, 1)
    compute((near, other))
    give_back(other)
    arrived(side_end)
    flatten(side_end, 1)
    arrived(far_end)
    flatten(far_end, 0)
    compute((far_end, side_end))
    launch(remote(r.partial.at[1, far_end], r.extra, r.row_s.at[0], r.extra_r.at[0], two_on))
    give_back(far_end, (1, 2))
    give_back(side_end, (1, 2))

    def collect(p):
        if p is far_end:
            await_bytes(r.back.at[pl.ds(1, 2), p], r.back_r.at[p])
            r.total[role, p] = r.partial[0, p].astype(F32)
        else:
            await_bytes(r.back.at[:, p], r.back_r.at[p])
            r.total[role, p] = r.partial[0, p].astype(F32) + r.back[0, p].astype(F32)
        r.total[1 - role, p] = r.back[1, p].astype(F32) + r.back[2, p].astype(F32)

    ends = (at(lax.rem(4 * half + 4 + c, NZ), y, x, c), at(lax.rem(4 * half + 6 + c, NZ), y, x, c))

    def stream(s, place, side):
        here = 1 - lax.min(1, (origin(s) - place) * (origin(s) - place))
        return s + here * side * (4 - s)

    def along(s):
        o = origin(s)
        for t in range(2):
            for q in range(PIECES):
                cols = slice(WIDTH * q, WIDTH * (q + 1))
                out = lanes_of(r.line_out.at[t, s], q)

                def add_line(side, t=t, q=q, cols=cols):
                    block = lanes_of(r.line_in.at[side, t, s], q)
                    await_bytes(block, r.sum_r.at[t, stream(s, zl, side), q])
                    r.total[t, s, :, cols] += r.line_in[side, t, s, :, cols].astype(F32)

                @pl.when(jnp.logical_and(o >= zl, zl > 0))
                def _(add_line=add_line):
                    add_line(0)

                @pl.when(jnp.logical_and(o <= zl, zl < 3))
                def _(add_line=add_line):
                    add_line(1)

                r.line_out[t, s, :, cols] = r.total[t, s, :, cols].astype(BF16)
                for side, wanted, last in ((0, o > zl, zl == 3), (1, o < zl, zl == 0)):
                    launch_if(
                        jnp.logical_and(wanted, jnp.logical_not(last)),
                        lambda out=out, t=t, s=s, q=q, side=side: remote(
                            out,
                            lanes_of(r.line_in.at[side, t, s], q),
                            r.sum_s.at[0],
                            r.sum_r.at[t, stream(s, zl + 1 - 2 * side, side), q],
                            on_z(-1 if side else 1),
                        ),
                    )
                    launch_if(
                        jnp.logical_and(wanted, last),
                        lambda out=out, t=t, s=s, q=q, side=side: remote(
                            out,
                            lanes_of(r.ret.at[t], q),
                            r.sum_s.at[0],
                            r.ret_r.at[0],
                            ends[side],
                        ),
                    )

    @pl.when(edge == 1)
    def _():
        collect(other)
        along(other)

    await_bytes(r.extra, r.extra_r.at[0])
    joined = r.partial[1, side_end].astype(F32) + r.extra[...].astype(F32)
    r.partial[1, side_end] = joined.astype(BF16)
    give_back(side_end, (0,))
    give_back(near)

    @pl.when(edge == 0)
    def _():
        collect(other)
        along(other)

    for p in (far_end, third, fourth):
        collect(p)
        along(p)

    def home_copy(side, d, cc):
        cols = pl.ds(HALF * side, HALF)
        return remote(
            r.home_out.at[ring_x(d), cc, :, cols],
            r.home_in.at[x, :, cols],
            r.home_s.at[0],
            r.home_r.at[1 if d else 0],
            at(z, y, ring_x(d), cc),
        )

    home_targets = [(d, other) for d in (2, 1, 3) for other in range(2)] + [(0, 1 - c)]

    @pl.when(source)
    def _():
        await_bytes(r.ret, r.ret_r.at[0])
        rows = jnp.concatenate([r.line_out[0, near], r.line_out[1, near], r.ret[0], r.ret[1]] * 2, axis=0)
        for side in range(2):
            cols = slice(HALF * side, HALF * (side + 1))
            value = dot(r.weighted[side], rows)
            value = value.reshape(4, 2, 16, HALF)
            r.mixed[:, :, :, cols] = value
            r.home_out[:, :, :, cols] = value.astype(BF16)
            for d, cc in home_targets:
                home_copy(side, d, cc).start()
        r.home[...] = r.mixed[x, c]

    @pl.when(jnp.logical_not(source))
    def _():
        await_bytes(r.home_in.at[0], r.home_r.at[0])
        r.home[...] = r.home_in[x].astype(F32)

    result = r.hidden[...] + r.home[...]
    await_bytes(r.home_in.at[pl.ds(0, 3)], r.home_r.at[1])
    for d in (1, 3, 2):
        result = result + r.home_in[ring_x(-d)].astype(F32)
    r.out[...] = result.astype(BF16)

    await_bytes(units(21), r.early_s.at[0])
    await_bytes(r.slab_out.at[:, pl.ds(0, 3)], r.slab_s.at[0])
    await_bytes(units(36), r.row_s.at[0])
    for n, ref in enumerate((r.tokens, r.tables)):
        await_bytes(ref.at[pl.ds(0, 3)], r.tok_s.at[n])
    for d in range(1, NZ):

        @pl.when(z + d == NZ - 1)
        def _(d=d):
            await_bytes(r.total_in.at[pl.ds(0, d)], r.total_s.at[0])

    @pl.when(keeper)
    def _():
        await_bytes(r.gate, r.own_s.at[0])
        await_bytes(r.gate.at[own_rows], r.own_s.at[1])

    @pl.when(away)
    def _():
        for semaphore in (r.swap_s, r.pass_s):
            await_bytes(r.gate, semaphore.at[0])
            await_bytes(r.gate.at[own_rows], semaphore.at[1])

    @pl.when(source)
    def _():
        await_bytes(units(3), r.cross_s.at[0])
        await_bytes(units(9), r.sum_s.at[0])
        await_bytes(units(7), r.home_s.at[0])

    @pl.when(jnp.logical_not(source))
    def _():
        for n, ref in enumerate((r.tokens, r.tables)):
            await_bytes(ref.at[0], r.tok_s.at[n + 2])
        await_bytes(units(12), r.sum_s.at[0])

    forwards = sum(
        jnp.where(jnp.logical_and(origin(s) <= zl, zl < 3), 1, 0)
        + jnp.where(jnp.logical_and(origin(s) >= zl, zl > 0), 1, 0)
        for s in range(4)
    )
    for n in range(1, 9):

        @pl.when(forwards == n)
        def _(n=n):
            await_bytes(units(3 * n), r.line_s.at[0])


VMEM = pl.BlockSpec(memory_space=pltpu.VMEM)
ANY = pl.BlockSpec(memory_space=pl.ANY)


def body(
    stream,
    query,
    key,
    value,
    decay_rate,
    out_weight,
    norm_gain,
    router_weight,
    routes,
    expert_gate,
    expert_up,
    expert_down,
):
    return pl.pallas_call(
        kernel,
        out_shape=jax.ShapeDtypeStruct(stream.shape, BF16),
        in_specs=[ANY] * 12,
        out_specs=VMEM,
        scratch_shapes=list(SCRATCH.values()),
        compiler_params=pltpu.CompilerParams(
            collective_id=0, has_side_effects=True, vmem_limit_bytes=56 * 2**20
        ),
        name="whole",
    )(
        stream,
        query,
        key,
        value,
        decay_rate.reshape(1, 4),
        out_weight.T,
        norm_gain.reshape(1, DM),
        routes.T,
        router_weight.T,
        expert_gate.T,
        expert_up.T,
        expert_down,
    )


def solution(mesh):
    placed = (
        P(("ctx", "ep"), None),
        P("ctx", "ep"),
        P("ctx", "ep"),
        P("ctx", "ep"),
        P("ep"),
        P("ep", "ctx"),
        P(),
        P(),
        P(("ctx", "ep"), None),
        P(None, ("ep", "ctx")),
        P(None, ("ep", "ctx")),
        P(("ep", "ctx"), None),
    )
    return jax.shard_map(
        body, mesh=mesh, in_specs=placed, out_specs=P(("ctx", "ep"), None), check_vma=False
    )
```
